32 devices in a mesh: blk: 16 (over z, x, core), dim: 2 (over y).
Axes of the slice: x: 2, y: 2, z: 4, core: 2. Of those that a mesh axis runs over, the one named last changes fastest.
Arguments:
- question_matrix: float32 [2048, 768], P('blk', 'dim'), may hold values from -20 to 20, as said below
- document_matrix: float32 [2048, 768], P('blk', 'dim'), may hold values from -0.5 to 0.5
- pool: float32 [768, 32768], P('dim', 'blk'), may hold values from -1.4 to 1.4
- hard_owner: int32 [2048, 8], P('blk'), may hold values from 0 to 15, all different within a row; in each aligned block of 128 rows (0 to 127, 128 to 255, ...) at most 128 rows name the same one
- hard_local: int32 [2048, 8], P('blk'), may hold values from 0 to 2047
Outputs:
- loss: float32 [2048], P('blk')
- question_derivative: float32 [2048, 768], P('blk', 'dim')
- document_derivative: float32 [2048, 768], P('blk', 'dim')
- grad_pool: float32 [768, 32768], P('dim', 'blk')
The draws below stay inside these ranges and needn't reach their ends.
Inputs may be any that keep to these rules, and one draw needn't show every extreme that they name: `question_matrix`: query embeddings; some rows may be much larger than the rest. `hard_owner`: the 8 owners named in one row are different. Among the rows of one index of blk, no owner is named more than 128 times, a bound that some block reaches.
All inputs are finite; a program needn't handle non-finite values.
Results may differ from the reference program's by a relative error of at most 0.0003.
Values sent between devices are 32-bit elements; how exact they have to be, the bound alone decides.
No kernel may reach another device: no remote copies, remote signals or barrier semaphores. Data moves between devices by JAX's collectives and lax.ppermute only.
A program may use at most 64 MiB of HBM per device.

```python
import math
import jax
import jax.numpy as jnp
import numpy as np
from jax import lax

VECTOR_LENGTH = 768
H = 8
Q_DEV = 128
POOL_DEV = 2048
NQ = 2048
POOL = 32768
MOST = 128
N_BLK = 16


def draw_question_matrix(key, part):
    values = jax.random.normal(key, (NQ, VECTOR_LENGTH), jnp.float32) * 0.074
    values = jnp.clip(values, -0.5, 0.5)
    return values


def set_ends(values, rng, low, top_value):
    longest = values.shape.index(max(values.shape))
    spots = []
    for shift in (0, 1):
        where = [jax.random.randint(jax.random.fold_in(rng, axis), (), 0, length) for axis, length in enumerate(values.shape)]
        where[longest] = (where[longest] + shift) % values.shape[longest]
        spots.append(tuple(where))
    return values.at[spots[0]].set(low).at[spots[1]].set(top_value)


def steps_of(stream_key, shape, cuts, least, largest):
    level = 1.0
    for dim, parts in cuts:
        steps = jax.random.uniform(jax.random.fold_in(jax.random.fold_in(stream_key, 6), dim), (parts,), jnp.float32, least / len(cuts), largest / len(cuts))
        level = level * jnp.repeat(jnp.exp(steps), shape[dim] // parts).reshape((-1,) + (1,) * (len(shape) - 1 - dim))
    return level


def deal_out(key, own, number, rows, count, top, limit, skew):
    order = jax.random.permutation(key, count)
    packed, ordinary = portions_of(count, rows * top, limit, skew, True), portions_of(count, rows * top, limit, skew, False)
    places = jnp.arange(count)

    def named(lengths, offset_by):
        used = int((lengths > 0).sum())
        fixed = max(1, used // 4)
        shifted = fixed + (places - fixed + offset_by * (used - fixed)) % max(1, count - fixed)
        return jnp.zeros((count,), jnp.int32).at[order[jnp.where(places < fixed, places, shifted)]].set(jnp.asarray(lengths, jnp.int32))

    lengths = jnp.where(number % 4 == 0, named(packed, number // 4), named(ordinary, number - number // 4 - 1))
    mixed = jax.random.permutation(jax.random.fold_in(own, 3), count)
    source_of, taker = mixed[0:count // 2 * 2:2], mixed[1:count // 2 * 2:2]
    room = jnp.minimum(lengths[source_of] - 1, limit - lengths[taker]) // 2
    room = jnp.where((source_of == order[0]) | (taker == order[0]) | (lengths[taker] == 0), 0, jnp.maximum(room, 0))
    shifted = jax.random.randint(jax.random.fold_in(own, 4), (count // 2,), 0, 1 << 20) % (room + 1)
    lengths = lengths.at[source_of].add(-shifted).at[taker].add(shifted)
    members = jnp.searchsorted(jnp.cumsum(lengths), jnp.arange(rows * top), side="right").astype(jnp.int32)
    table = members.reshape(top, rows).T
    table = table[jax.random.permutation(jax.random.fold_in(own, 1), rows)]
    offset_by = jax.random.randint(jax.random.fold_in(own, 2), (rows, 1), 0, top)
    return jnp.take_along_axis(table, (jnp.arange(top)[None, :] + offset_by) % top, axis=1)


def portions_of(number_of, total, reach, lean, full):
    weights = [(1 << 20) // math.isqrt(rank ** lean) + 1 for rank in range(1, number_of + 1)]
    largest = reach if full else min(reach, max(-(-total // number_of), total * weights[0] // sum(weights)))
    least = 1 if total - largest >= number_of - 1 else 0
    holding, spare = [largest] + [least] * (number_of - 1), total - largest - least * (number_of - 1)
    while spare > 0:
        free = [i for i in range(1, number_of) if holding[i] < largest] or [i for i in range(1, number_of) if holding[i] < reach]
        mass, remaining = sum([weights[i] for i in free]), spare
        for i in free:
            addition = min(reach - holding[i], max(1, remaining * weights[i] // mass), spare)
            holding[i] = holding[i] + addition
            spare = spare - addition
    return np.array(holding)


def centred(stream_key, extent, spread, bound, split=(), dtype=jnp.bfloat16):
    drawn = jax.random.normal(stream_key, extent, jnp.float32) * spread
    if len(split) > 0:
        drawn = steps_of(stream_key, extent, split, -0.22, 0.18) * drawn
    return jnp.clip(drawn, min=-bound, max=bound).astype(dtype)


def setup_inputs(seed: int = 0) -> dict:
    key_of = jax.random.split(jax.random.key(seed), 6)
    question_matrix = draw_question_matrix(jax.random.fold_in(key_of[5], 71), 0)
    document_matrix = centred(key_of[1], (NQ, VECTOR_LENGTH), 0.074, 0.5, ((0, 16), (1, 2)), jnp.float32)
    pool = centred(key_of[2], (VECTOR_LENGTH, POOL), 0.22, 1.4, ((0, 2), (1, 16)), jnp.float32)
    hard_owner_keys = jax.random.split(jax.random.fold_in(key_of[3], 1), NQ // Q_DEV)
    hard_owner_turns = jax.random.permutation(jax.random.fold_in(key_of[3], 3), NQ // Q_DEV)
    hard_owner = jax.vmap(lambda own, number: deal_out(jax.random.fold_in(key_of[3], 2), own, number, Q_DEV, N_BLK, H, MOST, 2))(hard_owner_keys, hard_owner_turns).reshape((NQ, H))
    hard_local = set_ends(jax.random.randint(key_of[4], (NQ, H), 0, POOL_DEV), jax.random.fold_in(key_of[4], 1), 0, POOL_DEV - 1).astype(jnp.int32)
    return {"question_matrix": question_matrix, "document_matrix": document_matrix, "pool": pool, "hard_owner": hard_owner, "hard_local": hard_local}


logit_divisor = 0.05


def reference(question_matrix, document_matrix, pool, hard_owner, hard_local):
    highest_accuracy = lax.Precision.HIGHEST
    pool_rows = pool.T
    rows = (hard_owner * POOL_DEV + hard_local).astype(jnp.int32)
    query_blocks = question_matrix.reshape(N_BLK, Q_DEV, VECTOR_LENGTH)
    passage_blocks = document_matrix.reshape(N_BLK, Q_DEV, VECTOR_LENGTH)
    row_blocks = rows.reshape(N_BLK, Q_DEV, H)

    def advance(carry, block):
        document_derivative_round, grad_rows = carry
        question_derivative_share, document_derivative_share, named = block
        affinity_logits = jnp.dot(question_derivative_share, document_matrix.T, precision=highest_accuracy, preferred_element_type=jnp.float32) / logit_divisor
        distractor_lines = pool_rows[named]
        distractor_logits = jnp.einsum("pq,pcq->pc", question_derivative_share, distractor_lines, precision=highest_accuracy) / logit_divisor
        matching_logit = jnp.sum(question_derivative_share * document_derivative_share, axis=1) / logit_divisor
        peak = jnp.maximum(jnp.max(affinity_logits, axis=1), jnp.max(distractor_logits, axis=1))
        summed = jnp.sum(jnp.exp(affinity_logits - peak[:, None]), axis=1) + jnp.sum(jnp.exp(distractor_logits - peak[:, None]), axis=1)
        normalizer_logarithm = peak + jnp.log(summed)
        chance = jnp.exp(affinity_logits - normalizer_logarithm[:, None])
        distractor_likelihood = jnp.exp(distractor_logits - normalizer_logarithm[:, None])
        grad_query = (jnp.dot(chance, document_matrix, precision=highest_accuracy, preferred_element_type=jnp.float32)
                      + jnp.einsum("jg,jgu->ju", distractor_likelihood, distractor_lines, precision=highest_accuracy) - document_derivative_share) / logit_divisor
        document_derivative_round = document_derivative_round + jnp.dot(chance.T, question_derivative_share, precision=highest_accuracy, preferred_element_type=jnp.float32)
        dispatched_deltas = (distractor_likelihood[:, :, None] * question_derivative_share[:, None, :] / logit_divisor).reshape(-1, VECTOR_LENGTH)
        grad_rows = grad_rows.at[named.reshape(-1)].add(dispatched_deltas)
        return (document_derivative_round, grad_rows), (normalizer_logarithm - matching_logit, grad_query)

    start = (jnp.zeros((NQ, VECTOR_LENGTH), jnp.float32), jnp.zeros((POOL, VECTOR_LENGTH), jnp.float32))
    (document_derivative_round, grad_rows), (objective_entries, question_derivative) = lax.scan(advance, start, (query_blocks, passage_blocks, row_blocks))
    document_derivative = (document_derivative_round - question_matrix) / logit_divisor
    return objective_entries.reshape(NQ), question_derivative.reshape(NQ, VECTOR_LENGTH), document_derivative, grad_rows.T
```

```python
import functools

import jax
import jax.numpy as jnp
import numpy as np
from jax import lax
from jax.experimental import pallas as pl
from jax.experimental.pallas import tpu as pltpu
from jax.sharding import PartitionSpec as P

logit_divisor = 0.05
LOWEST = -3.0e38
SLACK = 8

f32 = jnp.float32
bf16 = jnp.bfloat16


def split2(x):
    high = x.astype(bf16)
    return high, (x - high.astype(f32)).astype(bf16)


def dot(a, b, contract=((1,), (0,)), precision=None):
    return lax.dot_general(
        a, b, (contract, ((), ())), precision=precision, preferred_element_type=f32
    )


def call(body, out_shape, name, flops=0, data=1 << 20, limit=48 << 20, **kw):
    return pl.pallas_call(
        body,
        out_shape=out_shape,
        name=name,
        cost_estimate=pl.CostEstimate(flops=flops, bytes_accessed=data, transcendentals=0),
        compiler_params=pltpu.CompilerParams(vmem_limit_bytes=limit),
        **kw,
    )


def shape(*dims, dtype=f32):
    return jax.ShapeDtypeStruct(dims, dtype)


def pack_body(q_ref, owner_ref, local_ref, columns, x_ref):
    features = q_ref.shape[1]
    x_ref[:features, :] = q_ref[...].T
    x_ref[features:, :] = (owner_ref[...] * columns + local_ref[...]).astype(f32)


def prepare_body(d_ref, pool_ref, dt_ref, pool_parts_ref):
    features = d_ref.shape[1]
    high, low = split2(d_ref[...].T)
    dt_ref[:features, :] = high
    dt_ref[features:, :] = low
    values = pool_ref[...]
    high = values.astype(bf16)
    rest = values - high.astype(f32)
    middle = rest.astype(bf16)
    pool_parts_ref[:features, :] = high
    pool_parts_ref[features : 2 * features, :] = middle
    pool_parts_ref[2 * features :, :] = (rest - middle.astype(f32)).astype(bf16)


def score_body(pieces, me_ref, d_ref, pool_ref, *refs):
    part_ref, rows_ref = refs[-2:]
    rows, features = d_ref.shape
    columns = pool_ref.shape[1]
    blocks, at = [], 0
    for count in pieces:
        held = [r[...] for r in refs[at : at + count]]
        blocks.append(held[0] if count == 1 else jnp.concatenate(held, axis=0))
        at += count
    x = blocks[0] if len(blocks) == 1 else jnp.concatenate(blocks, axis=1)
    named = x[features:].astype(jnp.int32) - me_ref[0] * columns
    here = (named >= 0) & (named < columns)
    local = jnp.sum(jnp.where(here, named, 0), axis=0, keepdims=True)
    local = jnp.where(jnp.any(here, axis=0, keepdims=True), local, -1)
    x = x[:features]
    marks = lax.broadcasted_iota(jnp.int32, (columns, x.shape[1]), 0) == local
    found = dot(pool_ref[...], jnp.where(marks, 1.0, 0.0).astype(bf16))
    found = found[:features] + found[features : 2 * features] + found[2 * features :]
    scores = dot(d_ref[...], x, precision=lax.Precision.HIGHEST)
    hard = jnp.sum(x * found, axis=0, keepdims=True)
    chosen = local.astype(f32)
    for k in range(len(pieces)):
        at = slice(k * rows, (k + 1) * rows)
        part_ref[k, :rows] = scores[:, at]
        part_ref[k, rows:] = jnp.concatenate(
            [hard[:, at], chosen[:, at], jnp.zeros((SLACK - 2, rows), f32)], axis=0
        )
        rows_ref[k] = found[:, at]


def softmax_body(counts, others, dt_ref, rows_ref, part_ref, *refs):
    got, (e_ref, *sum_refs) = refs[:others], refs[others:]
    features = dt_ref.shape[0] // 2
    rows = dt_ref.shape[1]
    half = features // 2
    k = 0
    for count, sum_ref in zip(counts, sum_refs):
        for slot in range(count):
            whole = part_ref[k]
            chosen = whole[rows + 1 : rows + 2]
            for r in got:
                whole = whole + r[k]
            scores = whole[:rows] / logit_divisor
            hard = jnp.where(chosen >= 0, whole[rows : rows + 1] / logit_divisor, LOWEST)
            peak = jnp.maximum(jnp.max(scores, axis=0, keepdims=True), hard)
            e = jnp.exp(scores - peak)
            hard_e = jnp.where(chosen >= 0, jnp.exp(hard - peak), 0.0)
            total = jnp.sum(e, axis=0, keepdims=True) + hard_e
            own = lax.broadcasted_iota(jnp.int32, (rows, rows), 0) == lax.broadcasted_iota(
                jnp.int32, (rows, rows), 1
            )
            positive = jnp.sum(jnp.where(own, scores, 0.0), axis=0, keepdims=True)
            e_ref[k, :rows] = e
            e_ref[k, rows:] = jnp.concatenate(
                [hard_e, chosen, peak, total, positive, jnp.zeros((SLACK - 5, rows), f32)],
                axis=0,
            )
            high, low = split2(e)
            both = dot(dt_ref[...], high)
            sums = both[:features] + both[features:] + dot(dt_ref[:features], low)
            sums = sums + rows_ref[k] * hard_e
            for h in range(2):
                sum_ref[slot, h, :half] = sums[h * half : (h + 1) * half]
                sum_ref[slot, h, half:] = jnp.concatenate(
                    [peak, total, jnp.zeros((SLACK - 2, rows), f32)], axis=0
                )
            k += 1


def merge(terms):
    half = terms[0].shape[0] - SLACK
    peaks = [t[half : half + 1] for t in terms]
    peak = functools.reduce(jnp.maximum, peaks)
    scales = [jnp.exp(p - peak) for p in peaks]
    sums = functools.reduce(jnp.add, [t[:half] * s for t, s in zip(terms, scales)])
    total = functools.reduce(
        jnp.add, [t[half + 1 : half + 2] * s for t, s in zip(terms, scales)]
    )
    return sums, peak, total


def merged(terms):
    sums, peak, total = merge(terms)
    tail = jnp.concatenate([peak, total, jnp.zeros((SLACK - 2, peak.shape[1]), f32)], axis=0)
    return jnp.concatenate([sums, tail], axis=0)


def first_body(mine_ref, other_ref, up_ref, down_ref):
    up_ref[...] = merged([mine_ref[0, 0], other_ref[0, 0]])
    down_ref[...] = merged([mine_ref[0, 1], other_ref[0, 1]])


def step_body(halves, mine_ref, other_ref, up_in, down_in, up_ref, down_ref):
    for arrived, out, slot, first in ((up_in, up_ref, 1, 0), (down_in, down_ref, 0, 1)):
        for h in range(2):
            terms = [mine_ref[slot, h], other_ref[slot, h]]
            if not halves:
                terms.append(arrived[h])
            elif h == first:
                terms.append(arrived[...])
            out[h] = merged(terms)


def last_body(mine_ref, other_ref, up_ref, down_ref, d_ref, e_ref, dq_ref, loss_ref):
    rows, features = d_ref.shape
    half = features // 2
    for h in range(2):
        sums, peak, total = merge([mine_ref[0, h], other_ref[0, h], up_ref[h], down_ref[h]])
        at = slice(h * half, (h + 1) * half)
        if half % 128 == 0:
            dq_ref[:, at] = ((sums / total).T - d_ref[:, at]) / logit_divisor
        elif h == 0:
            held = sums / total
        else:
            held = jnp.concatenate([held, sums / total], axis=0)
            dq_ref[...] = (held.T - d_ref[...]) / logit_divisor
    log_total = peak + jnp.log(total)
    loss_ref[...] = jnp.broadcast_to(log_total - e_ref[0, 4:5], loss_ref.shape)


def stats_body(counts, table_ref, *refs):
    out_ref = refs[-1]
    slot = 0
    for ref, count in zip(refs, counts):
        for k in range(count):
            at = pl.ds(table_ref[slot], 1)
            out_ref[0, at, :] = ref[k, 2:3]
            out_ref[1, at, :] = ref[k, 3:4]
            slot += 1


def gradient_body(pieces, counts, group, table_ref, q_ref, tot_ref, *refs):
    n = len(pieces)
    x_refs, refs = refs[: sum(pieces)], refs[sum(pieces) :]
    e_refs, refs = refs[: len(counts)], refs[len(counts) :]
    dd_ref, pool_ref, scaled_ref, local_ref = refs
    rows, features = q_ref.shape

    @pl.when(pl.program_id(0) == 0)
    def _():
        where = [(b, k) for b, count in enumerate(counts) for k in range(count)]
        at, total = 0, jnp.zeros((rows, features), f32)
        for g in range(n // group):
            xs, es, hards, locals_ = [], [], [], []
            for s in range(g * group, (g + 1) * group):
                held = [r[...] for r in x_refs[at : at + pieces[s]]]
                at += pieces[s]
                x = held[0] if len(held) == 1 else jnp.concatenate(held, axis=0)
                xs.append(x[:features])
                b, k = where[s]
                e = e_refs[b][k]
                row = pl.ds(table_ref[s], 1)
                scale = jnp.exp(e[rows + 2 : rows + 3] - tot_ref[0, row, :])
                scale = scale / tot_ref[1, row, :]
                es.append(e[:rows] * scale)
                hards.append(e[rows : rows + 1] * scale)
                locals_.append(e[rows + 1 : rows + 2])
            x = jnp.concatenate(xs, axis=1)
            chance = jnp.concatenate(es, axis=1)
            total = total + dot(chance, x, ((1,), (1,)), precision=lax.Precision.HIGHEST)
            high, low = split2(x * (jnp.concatenate(hards, axis=1) / logit_divisor))
            scaled_ref[g, :features] = high
            scaled_ref[g, features:] = low
            local_ref[g] = jnp.broadcast_to(
                jnp.concatenate(locals_, axis=1).astype(jnp.int32), local_ref.shape[1:]
            )
        dd_ref[...] = (total - q_ref[...]) / logit_divisor

    width = pool_ref.shape[1]
    first = pl.program_id(0) * width
    acc = jnp.zeros((2 * features, width), f32)
    for g in range(n // group):
        local = local_ref[g, :1]
        column = first + lax.broadcasted_iota(jnp.int32, (width, local.shape[1]), 0)
        marks = jnp.where(column == local, 1.0, 0.0).astype(bf16)
        acc = acc + dot(scaled_ref[g], marks, ((1,), (1,)))
    pool_ref[...] = acc[:features] + acc[features:]


def ring_order(chips):
    if chips < 4:
        return list(range(chips))
    return list(range(0, chips, 2)) + list(range(chips - 1, 0, -2))


def per_device(question_matrix, document_matrix, pool, hard_owner, hard_local):
    n, depth = lax.axis_size("blk"), lax.axis_size("dim")
    rows, features = question_matrix.shape
    columns = pool.shape[1]
    half = features // 2
    chips = n // 2
    walk = ring_order(chips)
    reach = chips // 2
    me = lax.axis_index("blk")

    up = [(2 * a + c, 2 * b + c) for a, b in zip(walk, walk[1:] + walk[:1]) for c in range(2)]
    down = [(b, a) for a, b in up]
    across = [(i, i ^ 1) for i in range(n)]

    def send(x, perm):
        return lax.ppermute(x, "blk", perm)

    own = [[0]] + [[-t, t] for t in range(1, reach)] + [[reach], []]
    other = [[]] + own[:-1]
    slots = [(0, d) for d in own[0]]
    for b in range(1, reach + 2):
        slots += [(0, d) for d in own[b]] + [(1, d) for d in other[b]]
    place = {chip: i for i, chip in enumerate(walk)}
    table = np.zeros((n, n), np.int32)
    for i in range(n):
        for s, (swap, d) in enumerate(slots):
            chip = walk[(place[i // 2] + d) % chips]
            table[i, s] = 2 * chip + ((i % 2) ^ swap)
    table = lax.dynamic_index_in_dim(jnp.asarray(table), me, 0, keepdims=False)

    smem = pl.BlockSpec(memory_space=pltpu.SMEM)
    vmem = pl.BlockSpec(memory_space=pltpu.VMEM)

    packed = call(
        lambda q, o, l, x: pack_body(q, o, l, columns, x),
        shape(features + SLACK, rows),
        "pack",
    )(question_matrix, hard_owner.T, hard_local.T)

    arrived = [[[packed]]]
    from_up, from_down = packed, packed
    cut = half + SLACK
    for t in range(1, reach):
        from_up, from_down = send(from_up, up), send(from_down, down)
        arrived.append([[from_up], [from_down]])
    arrived.append([[send(from_up[:cut], up), send(from_down[cut:], down)]])
    arrived.append([])
    shared = [[]] + [
        [[send(piece, across) for piece in block] for block in batch] for batch in arrived[:-1]
    ]
    batches = [a + s for a, s in zip(arrived, shared)]
    pieces = [[len(block) for block in batch] for batch in batches]
    counts = [len(batch) for batch in batches]

    dt, pool_parts = call(
        prepare_body,
        (shape(2 * features, rows, dtype=bf16), shape(3 * features, columns, dtype=bf16)),
        "prepare",
        data=features * columns * 10,
    )(document_matrix, pool)

    weights, own_sums, other_sums = [], [], []
    for b, batch in enumerate(batches):
        k = counts[b]
        part, found = call(
            functools.partial(score_body, pieces[b]),
            (shape(k, rows + SLACK, rows), shape(k, features, rows)),
            "score",
            flops=2 * features * rows * k * (3 * columns + 6 * rows),
            data=features * columns * 6,
            in_specs=[smem] + [vmem] * (2 + sum(pieces[b])),
        )(
            me.reshape(1), document_matrix, pool_parts, *[piece for block in batch for piece in block]
        )
        got = [
            lax.ppermute(part, "dim", [(i, (i + s) % depth) for i in range(depth)])
            for s in range(1, depth)
        ]
        sizes = [c for c in (len(own[b]), len(other[b])) if c]
        e, *sums = call(
            functools.partial(softmax_body, sizes, len(got)),
            [shape(k, rows + SLACK, rows)] + [shape(c, 2, half + SLACK, rows) for c in sizes],
            "softmax",
            flops=6 * features * rows * rows * k,
        )(dt, found, part, *got)
        weights.append(e)
        own_sums.append(sums.pop(0) if own[b] else None)
        other_sums.append(send(sums.pop(0), across) if other[b] else None)
    other_sums = other_sums[1:]

    message = shape(half + SLACK, rows)
    wide = shape(2, half + SLACK, rows)
    going_up, going_down = call(first_body, (message, message), "first_merge")(
        own_sums[reach], other_sums[reach]
    )
    for t in range(reach - 1, 0, -1):
        going_up, going_down = call(
            functools.partial(step_body, t == reach - 1), (wide, wide), "merge"
        )(own_sums[t], other_sums[t], send(going_up, up), send(going_down, down))
    whole = pl.BlockSpec((1, SLACK, rows), lambda i: (0, rows // SLACK, 0))
    full = lambda *dims: pl.BlockSpec(dims, lambda i: (0,) * len(dims))
    sums_spec = full(1, 2, half + SLACK, rows)
    question_derivative, loss = call(
        last_body,
        (shape(rows, features), shape(SLACK, rows)),
        "finish",
        grid=(1,),
        in_specs=[sums_spec, sums_spec, full(2, half + SLACK, rows), full(2, half + SLACK, rows)]
        + [full(rows, features), whole],
        out_specs=(full(rows, features), full(SLACK, rows)),
    )(
        own_sums[0],
        other_sums[0],
        send(going_up, up),
        send(going_down, down),
        document_matrix,
        weights[0],
    )

    totals = call(
        functools.partial(stats_body, counts),
        shape(2, n, rows),
        "stats",
        grid=(1,),
        in_specs=[smem]
        + [pl.BlockSpec((c, SLACK, rows), lambda i: (0, rows // SLACK, 0)) for c in counts],
        out_specs=full(2, n, rows),
    )(table, *weights)
    step = 1
    while step < n:
        there = send(totals, [(i, i ^ step) for i in range(n)])
        peak = jnp.maximum(totals[0], there[0])
        total = totals[1] * jnp.exp(totals[0] - peak) + there[1] * jnp.exp(there[0] - peak)
        totals = jnp.stack([peak, total])
        step *= 2

    flat = [block for batch in batches for block in batch]
    group = 4
    width = 512
    document_derivative, grad_pool = call(
        functools.partial(gradient_body, [len(block) for block in flat], counts, group),
        (shape(rows, features), shape(features, columns)),
        "gradient",
        flops=2 * features * rows * n * (2 * columns + 6 * rows),
        data=features * columns * 8,
        grid=(columns // width,),
        in_specs=[smem] + [vmem] * (2 + sum(len(block) for block in flat) + len(counts)),
        out_specs=(full(rows, features), pl.BlockSpec((features, width), lambda i: (0, i))),
        scratch_shapes=[
            pltpu.VMEM((n // group, 2 * features, group * rows), bf16),
            pltpu.VMEM((n // group, SLACK, group * rows), jnp.int32),
        ],
    )(table, question_matrix, totals, *[piece for block in flat for piece in block], *weights)
    return loss[0], question_derivative, document_derivative, grad_pool


def solution(mesh):
    placed = (P("blk", "dim"), P("blk", "dim"), P("dim", "blk"), P("blk", None), P("blk", None))
    return jax.shard_map(
        per_device,
        mesh=mesh,
        in_specs=placed,
        out_specs=(P("blk"), P("blk", "dim"), P("blk", "dim"), P("dim", "blk")),
        check_vma=False,
    )
```

```python
import functools

import jax
import jax.numpy as jnp
from jax import lax
from jax.experimental import pallas as pl
from jax.experimental.pallas import tpu as pltpu
from jax.sharding import PartitionSpec as P

logit_divisor = 0.05
LOWEST = -3.0e38
SLACK = 8

f32 = jnp.float32
bf16 = jnp.bfloat16


def split2(x):
    high = x.astype(bf16)
    return high, (x - high.astype(f32)).astype(bf16)


def dot(a, b, contract=((1,), (0,)), precision=None):
    return lax.dot_general(
        a, b, (contract, ((), ())), precision=precision, preferred_element_type=f32
    )


def call(body, out_shape, name, flops=0, data=1 << 20, limit=48 << 20, **kw):
    return pl.pallas_call(
        body,
        out_shape=out_shape,
        name=name,
        cost_estimate=pl.CostEstimate(flops=flops, bytes_accessed=data, transcendentals=0),
        compiler_params=pltpu.CompilerParams(vmem_limit_bytes=limit),
        **kw,
    )


def shape(*dims, dtype=f32):
    return jax.ShapeDtypeStruct(dims, dtype)


def pack_body(q_ref, owner_ref, local_ref, columns, x_ref):
    features = q_ref.shape[1]
    x_ref[:features, :] = q_ref[...].T
    x_ref[features:, :] = (owner_ref[...] * columns + local_ref[...]).astype(f32)


def flip_body(d_ref, dt_ref):
    dt_ref[...] = d_ref[...].T


def score_body(places, after, me_ref, d_ref, pool_ref, *refs):
    part_ref, rows_ref = refs[-2:]
    rows, features = d_ref.shape
    columns = pool_ref.shape[1]
    tile = 128
    blocks = [refs[a][...] if k is None else refs[a][k] for a, k in places]
    for k, block in enumerate(blocks):
        x = block[:features]
        named = block[features:].astype(jnp.int32) - me_ref[0] * columns
        here = (named >= 0) & (named < columns)
        local = jnp.sum(jnp.where(here, named, 0), axis=0, keepdims=True)
        owned = jnp.any(here, axis=0, keepdims=True)
        lane = jnp.broadcast_to(local % tile, (features, rows))
        found = jnp.zeros((features, rows), f32)
        for t in range(columns // tile):
            picked = jnp.take_along_axis(
                pool_ref[:, t * tile : (t + 1) * tile], lane, axis=1, mode="promise_in_bounds"
            )
            found = jnp.where(local // tile == t, picked, found)
        rows_ref[k] = found
        hard = jnp.sum(x * found, axis=0, keepdims=True)
        chosen = jnp.where(owned, local, -1).astype(f32)
        part_ref[k, rows:] = jnp.concatenate(
            [hard, chosen, jnp.zeros((SLACK - 2, rows), f32)], axis=0
        )
    x = [block[:features] for block in blocks]
    x = x[0] if len(x) == 1 else jnp.concatenate(x, axis=1)
    scores = dot(d_ref[...], x, precision=lax.Precision.HIGHEST)
    for k in range(len(blocks)):
        part_ref[k, :rows] = scores[:, k * rows : (k + 1) * rows]


def softmax_body(evens, others, dt_ref, rows_ref, part_ref, *refs):
    got, (e_ref, *sum_refs) = refs[:others], refs[others:]
    features, rows = dt_ref.shape
    count = part_ref.shape[0]
    own = lax.broadcasted_iota(jnp.int32, (rows, rows), 0) == lax.broadcasted_iota(
        jnp.int32, (rows, rows), 1
    )
    tails, es = [], []
    for k in range(count):
        whole = part_ref[k]
        chosen = whole[rows + 1 : rows + 2]
        for r in got:
            whole = whole + r[k]
        scores = whole[:rows] / logit_divisor
        hard = jnp.where(chosen >= 0, whole[rows : rows + 1] / logit_divisor, LOWEST)
        peak = jnp.maximum(jnp.max(scores, axis=0, keepdims=True), hard)
        e = jnp.exp(scores - peak)
        hard_e = jnp.where(chosen >= 0, jnp.exp(hard - peak), 0.0)
        total = jnp.sum(e, axis=0, keepdims=True) + hard_e
        positive = jnp.sum(jnp.where(own, scores, 0.0), axis=0, keepdims=True)
        e_ref[k, :rows] = e
        e_ref[k, rows:] = jnp.concatenate(
            [hard_e, chosen, peak, total, positive, jnp.zeros((SLACK - 5, rows), f32)], axis=0
        )
        es.append(e)
        tails.append((hard_e, peak, total))
    e = es[0] if count == 1 else jnp.concatenate(es, axis=1)
    sums = dot(dt_ref[...], e, precision=lax.Precision.HIGHEST)
    for k, (hard_e, peak, total) in enumerate(tails):
        at = sum_refs[0].at[k] if k < evens else sum_refs[-1].at[k - evens]
        at[:features] = sums[:, k * rows : (k + 1) * rows] + rows_ref[k] * hard_e
        at[features:] = jnp.concatenate([peak, total, jnp.zeros((SLACK - 2, rows), f32)], axis=0)


def merge(terms):
    size = terms[0].shape[0] - SLACK
    peaks = [t[size : size + 1] for t in terms]
    peak = functools.reduce(jnp.maximum, peaks)
    scales = [jnp.exp(p - peak) for p in peaks]
    sums = functools.reduce(jnp.add, [t[:size] * s for t, s in zip(terms, scales)])
    total = functools.reduce(
        jnp.add, [t[size + 1 : size + 2] * s for t, s in zip(terms, scales)]
    )
    return sums, peak, total


def merge_body(places, *refs):
    out_ref = refs[-1]
    sums, peak, total = merge([refs[i][...] if k is None else refs[i][k] for i, k in places])
    size = sums.shape[0]
    out_ref[:size] = sums
    out_ref[size:] = jnp.concatenate(
        [peak, total, jnp.zeros((SLACK - 2, peak.shape[1]), f32)], axis=0
    )


def last_body(places, d_ref, e_ref, *refs):
    dq_ref, loss_ref = refs[-2:]
    sums, peak, total = merge([refs[i][...] if k is None else refs[i][k] for i, k in places])
    dq_ref[...] = ((sums / total).T - d_ref[...]) / logit_divisor
    log_total = peak + jnp.log(total)
    loss_ref[...] = jnp.broadcast_to(log_total - e_ref[0, 4:5], loss_ref.shape)


def stats_body(places, *refs):
    out_ref = refs[-1]
    for r, (i, k) in enumerate(places):
        out_ref[0, r : r + 1] = refs[i][k, 2:3]
        out_ref[1, r : r + 1] = refs[i][k, 3:4]


def stats_merge_body(masks, own_ref, *refs):
    out_ref = refs[-1]
    n = own_ref.shape[1]
    peaks, totals = [own_ref[0]], [own_ref[1]]
    for ref, mask in zip(refs, masks):
        for values, into in ((ref[0], peaks), (ref[1], totals)):
            into.append(
                jnp.concatenate([values[r ^ mask : (r ^ mask) + 1] for r in range(n)], axis=0)
            )
    peak = functools.reduce(jnp.maximum, peaks)
    out_ref[0] = peak
    out_ref[1] = functools.reduce(
        jnp.add, [t * jnp.exp(p - peak) for p, t in zip(peaks, totals)]
    )


def gradient_body(x_places, e_places, group, q_ref, tot_ref, *refs):
    n = len(x_places)
    dd_ref, pool_ref, scaled_ref, local_ref = refs[-4:]
    rows, features = q_ref.shape
    lanes = local_ref.shape[-1]

    @pl.when(pl.program_id(0) == 0)
    def _():
        total = jnp.zeros((rows, features), f32)
        for g in range(n // group):
            xs, es, hards = [], [], []
            for r in range(g * group, (g + 1) * group):
                i, k = x_places[r]
                xs.append(refs[i][:features] if k is None else refs[i][k, :features])
                i, k = e_places[r]
                scale = jnp.exp(refs[i][k, rows + 2 : rows + 3] - tot_ref[0, r : r + 1])
                scale = scale / tot_ref[1, r : r + 1]
                es.append(refs[i][k, :rows] * scale)
                hards.append(refs[i][k, rows : rows + 1] * scale)
                chosen = jnp.broadcast_to(refs[i][k, rows + 1 : rows + 2], (lanes, rows))
                first = (r - g * group) * rows
                local_ref[g, first : first + rows] = chosen.T.astype(jnp.int32)
            x = jnp.concatenate(xs, axis=1)
            chance = jnp.concatenate(es, axis=1)
            total = total + dot(chance, x, ((1,), (1,)), precision=lax.Precision.HIGHEST)
            high, low = split2(x * (jnp.concatenate(hards, axis=1) / logit_divisor))
            scaled_ref[g, :features] = high
            scaled_ref[g, features:] = low
        dd_ref[...] = (total - q_ref[...]) / logit_divisor

    width = pool_ref.shape[1]
    first = pl.program_id(0) * width
    acc = jnp.zeros((2 * features, width), f32)
    for g in range(n // group):
        local = local_ref[g]
        column = first + lax.broadcasted_iota(jnp.int32, local.shape, 1)
        marks = jnp.concatenate(
            [
                jnp.where(local == column + t * lanes, 1.0, 0.0).astype(bf16)
                for t in range(width // lanes)
            ],
            axis=1,
        )
        acc = acc + dot(scaled_ref[g], marks)
    pool_ref[...] = acc[:features] + acc[features:]


def per_device(question_matrix, document_matrix, pool, hard_owner, hard_local):
    n, depth = lax.axis_size("blk"), lax.axis_size("dim")
    rows, features = question_matrix.shape
    columns = pool.shape[1]
    me = lax.axis_index("blk")
    smem = pl.BlockSpec(memory_space=pltpu.SMEM)
    vmem = pl.BlockSpec(memory_space=pltpu.VMEM)
    unread = pl.BlockSpec(memory_space=pl.ANY)

    def full(*dims):
        return pl.BlockSpec(dims, lambda i: (0,) * len(dims))

    def send(x, mask):
        return lax.ppermute(x, "blk", [(i, i ^ mask) for i in range(n)])

    packed = call(
        lambda q, o, l, x: pack_body(q, o, l, columns, x), shape(features + SLACK, rows), "pack"
    )(question_matrix, hard_owner.T, hard_local.T)
    far = n // 4
    x = {0: packed}
    for k in [1, 2] + list(range(3, far)):
        x[4 * k] = send(x[4 * k - 4], 4) if k % 2 and k > 1 else send(packed, 4 * k)
    for k in [0] + list(range(2, far)) + [1]:
        x[4 * k + 2] = send(x[4 * k], 2)
    waves = [[0], [2, 4]] + [[4 * k, 4 * k + 2] for k in range(2, far)] + [[6]]
    x_arrays, x_place = [], {}
    for wave in waves:
        evens = [x[r] for r in wave]
        shared = send(jnp.stack(evens) if len(wave) > 1 else evens[0], 1)
        for k, r in enumerate(wave):
            x_place[r] = (len(x_arrays) + k, None)
            x_place[r + 1] = (len(x_arrays) + len(wave), k if len(wave) > 1 else None)
        x_arrays += evens + [shared]

    dt = call(flip_body, shape(features, rows), "flip")(document_matrix)

    batches = [
        (waves[b] if b < len(waves) else [], [r + 1 for r in waves[b - 1]] if b else [])
        for b in range(len(waves) + 1)
    ]
    weights, sums, e_place, sum_place = [], [], {}, {}
    waiting = []

    def finish_batch():
        b, part, found, got = waiting.pop(0)
        evens, odds = batches[b]
        k = len(evens) + len(odds)
        e, *out = call(
            functools.partial(softmax_body, len(evens), len(got)),
            [shape(k, rows + SLACK, rows)]
            + [shape(len(half), features + SLACK, rows) for half in batches[b] if half],
            "softmax",
            flops=12 * features * rows * rows * k,
        )(dt, found, part, *got)
        for i, r in enumerate(evens + odds):
            e_place[r] = (len(weights), i)
        weights.append(e)
        if evens:
            for i, r in enumerate(evens):
                sum_place[r] = (len(sums), i)
            sums.append(out[0])
        if odds:
            for i, r in enumerate(odds):
                sum_place[r] = (len(sums), i)
            sums.append(send(out[-1], 1))

    for b, (evens, odds) in enumerate(batches):
        blocks = evens + odds
        k = len(blocks)
        used = sorted({x_place[r][0] for r in blocks})
        after = weights[-1:]
        part, found = call(
            functools.partial(
                score_body, [(used.index(x_place[r][0]), x_place[r][1]) for r in blocks], len(after)
            ),
            (shape(k, rows + SLACK, rows), shape(k, features, rows)),
            "score",
            flops=12 * features * rows * rows * k,
            data=features * columns * 4 * k,
            in_specs=[smem] + [vmem] * (2 + len(used)) + [unread] * len(after),
        )(me.reshape(1), document_matrix, pool, *[x_arrays[i] for i in used], *after)
        got = [
            lax.ppermute(part, "dim", [(i, (i + s) % depth) for i in range(depth)])
            for s in range(1, depth)
        ]
        waiting.append((b, part, found, got))
        if len(waiting) > 1:
            finish_batch()
    while waiting:
        finish_batch()

    def terms(blocks, extra):
        used = sorted({sum_place[r][0] for r in blocks})
        places = [(used.index(sum_place[r][0]), sum_place[r][1]) for r in blocks]
        places += [(len(used) + i, None) for i in range(len(extra))]
        return places, [sums[i] for i in used] + extra

    def add(blocks, extra=()):
        places, arrays = terms(blocks, list(extra))
        return call(
            functools.partial(merge_body, places), shape(features + SLACK, rows), "merge"
        )(*arrays)

    home = []
    for k in [0] + list(range(2, far)) + [1]:
        beside = send(add([4 * k + 2, 4 * k + 3]), 2)
        if k:
            home.append(send(add([4 * k, 4 * k + 1], [beside]), 4 * k))
        else:
            home.append(beside)

    totals = call(
        functools.partial(stats_body, [e_place[r] for r in range(n)]),
        shape(2, n, rows),
        "stats",
        grid=(1,),
        in_specs=[
            pl.BlockSpec((e.shape[0], SLACK, rows), lambda i: (0, rows // SLACK, 0))
            for e in weights
        ],
        out_specs=full(2, n, rows),
    )(*weights)
    for masks in ([1], [2], [4 * k for k in range(1, far)]):
        totals = call(
            functools.partial(stats_merge_body, masks), shape(2, n, rows), "stats_merge"
        )(totals, *[send(totals, mask) for mask in masks])

    group = 4
    width = 512
    e_at = len(x_arrays)
    document_derivative, grad_pool = call(
        functools.partial(
            gradient_body,
            [x_place[r] for r in range(n)],
            [(e_at + e_place[r][0], e_place[r][1]) for r in range(n)],
            group,
        ),
        (shape(rows, features), shape(features, columns)),
        "gradient",
        flops=2 * features * rows * n * (2 * columns + 6 * rows),
        data=features * columns * 8,
        grid=(columns // width,),
        in_specs=[vmem] * (2 + len(x_arrays) + len(weights)),
        out_specs=(full(rows, features), pl.BlockSpec((features, width), lambda i: (0, i))),
        scratch_shapes=[
            pltpu.VMEM((n // group, 2 * features, group * rows), bf16),
            pltpu.VMEM((n // group, group * rows, 128), jnp.int32),
        ],
    )(question_matrix, totals, *x_arrays, *weights)

    places, arrays = terms([0, 1], home)
    question_derivative, loss = call(
        functools.partial(last_body, places),
        (shape(rows, features), shape(SLACK, rows)),
        "finish",
        grid=(1,),
        in_specs=[full(rows, features)]
        + [pl.BlockSpec((1, SLACK, rows), lambda i: (0, rows // SLACK, 0))]
        + [full(*a.shape) for a in arrays],
        out_specs=(full(rows, features), full(SLACK, rows)),
    )(document_matrix, weights[0], *arrays)
    return loss[0], question_derivative, document_derivative, grad_pool


def solution(mesh):
    placed = (P("blk", "dim"), P("blk", "dim"), P("dim", "blk"), P("blk", None), P("blk", None))
    return jax.shard_map(
        per_device,
        mesh=mesh,
        in_specs=placed,
        out_specs=(P("blk"), P("blk", "dim"), P("blk", "dim"), P("dim", "blk")),
        check_vma=False,
    )
```

```python
import functools

import jax
import jax.numpy as jnp
from jax import lax
from jax.experimental import pallas as pl
from jax.experimental.pallas import tpu as pltpu
from jax.sharding import PartitionSpec as P

logit_divisor = 0.05
LOWEST = -3.0e38
SLACK = 8

f32 = jnp.float32
bf16 = jnp.bfloat16


def split2(x):
    high = x.astype(bf16)
    return high, (x - high.astype(f32)).astype(bf16)


def dot(a, b, contract=((1,), (0,)), precision=None):
    return lax.dot_general(
        a, b, (contract, ((), ())), precision=precision, preferred_element_type=f32
    )


class Line:
    def __init__(self):
        self.last = None

    def __call__(self, body, out_shape, name, arrays, in_specs=None, limit=16, **kw):
        count = len(arrays)
        if in_specs is None:
            in_specs = [pl.BlockSpec(memory_space=pltpu.VMEM)] * count
        if self.last is not None:
            in_specs = list(in_specs) + [pl.BlockSpec(memory_space=pl.ANY)]
            arrays = list(arrays) + [self.last]

        def kernel(*refs):
            body(*refs[:count], *refs[len(arrays) :])

        out = pl.pallas_call(
            kernel,
            out_shape=out_shape,
            name=name,
            in_specs=in_specs,
            cost_estimate=pl.CostEstimate(flops=0, bytes_accessed=0, transcendentals=0),
            compiler_params=pltpu.CompilerParams(vmem_limit_bytes=limit << 20),
            **kw,
        )(*arrays)
        self.last = out[-1] if isinstance(out, (list, tuple)) else out
        return out


def shape(*dims, dtype=f32):
    return jax.ShapeDtypeStruct(dims, dtype)


def pack_body(columns, q_hbm, owner_hbm, local_hbm, x_ref, q_ref, owner_ref, local_ref, sems):
    pairs = ((q_hbm, q_ref), (owner_hbm, owner_ref), (local_hbm, local_ref))
    copies = [pltpu.make_async_copy(a, b, sems.at[i]) for i, (a, b) in enumerate(pairs)]
    for copy in copies:
        copy.start()
    for copy in copies:
        copy.wait()
    features = q_ref.shape[1]
    x_ref[:features, :] = q_ref[...].T
    x_ref[features:, :] = (owner_ref[...] * columns + local_ref[...]).astype(f32)


def relay_body(*refs):
    refs[1][...] = refs[0][...]


def flip_body(d_ref, dt_ref):
    dt_ref[...] = d_ref[...].T


def score_body(places, me_ref, d_ref, pool_ref, *refs):
    part_ref, rows_ref = refs[-2:]
    rows, features = d_ref.shape
    columns = pool_ref.shape[1]
    tile = 128
    blocks = [refs[a][...] if k is None else refs[a][k] for a, k in places]
    for k, block in enumerate(blocks):
        x = block[:features]
        named = block[features:].astype(jnp.int32) - me_ref[0] * columns
        here = (named >= 0) & (named < columns)
        local = jnp.sum(jnp.where(here, named, 0), axis=0, keepdims=True)
        owned = jnp.any(here, axis=0, keepdims=True)
        lane = jnp.broadcast_to(local % tile, (features, rows))
        found = jnp.zeros((features, rows), f32)
        for t in range(columns // tile):
            picked = jnp.take_along_axis(
                pool_ref[:, t * tile : (t + 1) * tile], lane, axis=1, mode="promise_in_bounds"
            )
            found = jnp.where(local // tile == t, picked, found)
        rows_ref[k] = found
        hard = jnp.sum(x * found, axis=0, keepdims=True)
        chosen = jnp.where(owned, local, -1).astype(f32)
        part_ref[k, rows:] = jnp.concatenate(
            [hard, chosen, jnp.zeros((SLACK - 2, rows), f32)], axis=0
        )
    x = [block[:features] for block in blocks]
    x = x[0] if len(x) == 1 else jnp.concatenate(x, axis=1)
    scores = dot(d_ref[...], x, precision=lax.Precision.HIGHEST)
    for k in range(len(blocks)):
        part_ref[k, :rows] = scores[:, k * rows : (k + 1) * rows]


def softmax_body(others, dt_ref, rows_ref, part_ref, *refs):
    got, (e_ref, *sum_refs) = refs[:others], refs[others:]
    features, rows = dt_ref.shape
    count = part_ref.shape[0]
    own = lax.broadcasted_iota(jnp.int32, (rows, rows), 0) == lax.broadcasted_iota(
        jnp.int32, (rows, rows), 1
    )
    tails, es = [], []
    for k in range(count):
        whole = part_ref[k]
        chosen = whole[rows + 1 : rows + 2]
        for r in got:
            whole = whole + r[k]
        scores = whole[:rows] / logit_divisor
        hard = jnp.where(chosen >= 0, whole[rows : rows + 1] / logit_divisor, LOWEST)
        peak = jnp.maximum(jnp.max(scores, axis=0, keepdims=True), hard)
        e = jnp.exp(scores - peak)
        hard_e = jnp.where(chosen >= 0, jnp.exp(hard - peak), 0.0)
        total = jnp.sum(e, axis=0, keepdims=True) + hard_e
        positive = jnp.sum(jnp.where(own, scores, 0.0), axis=0, keepdims=True)
        e_ref[k, :rows] = e
        e_ref[k, rows:] = jnp.concatenate(
            [hard_e, chosen, peak, total, positive, jnp.zeros((SLACK - 5, rows), f32)], axis=0
        )
        es.append(e)
        tails.append((hard_e, peak, total))
    e = es[0] if count == 1 else jnp.concatenate(es, axis=1)
    sums = dot(dt_ref[...], e, precision=lax.Precision.HIGHEST)
    for k, (hard_e, peak, total) in enumerate(tails):
        at = sum_refs[k]
        at[:features] = sums[:, k * rows : (k + 1) * rows] + rows_ref[k] * hard_e
        at[features:] = jnp.concatenate([peak, total, jnp.zeros((SLACK - 2, rows), f32)], axis=0)


def merge(terms):
    size = terms[0].shape[0] - SLACK
    peaks = [t[size : size + 1] for t in terms]
    peak = functools.reduce(jnp.maximum, peaks)
    scales = [jnp.exp(p - peak) for p in peaks]
    sums = functools.reduce(jnp.add, [t[:size] * s for t, s in zip(terms, scales)])
    total = functools.reduce(
        jnp.add, [t[size + 1 : size + 2] * s for t, s in zip(terms, scales)]
    )
    return sums, peak, total


def merge_body(*refs):
    out_ref = refs[-1]
    sums, peak, total = merge([ref[...] for ref in refs[:-1]])
    size = sums.shape[0]
    out_ref[:size] = sums
    out_ref[size:] = jnp.concatenate(
        [peak, total, jnp.zeros((SLACK - 2, peak.shape[1]), f32)], axis=0
    )


def last_body(d_ref, e_ref, *refs):
    dq_ref, loss_ref = refs[-2:]
    sums, peak, total = merge([ref[...] for ref in refs[:-2]])
    dq_ref[...] = ((sums / total).T - d_ref[...]) / logit_divisor
    log_total = peak + jnp.log(total)
    loss_ref[...] = (log_total - e_ref[0, 4:5]).reshape(loss_ref.shape)


def stats_body(places, *refs):
    out_ref = refs[-1]
    for r, (i, k) in enumerate(places):
        out_ref[0, r : r + 1] = refs[i][k, 2:3]
        out_ref[1, r : r + 1] = refs[i][k, 3:4]


def stats_merge_body(masks, own_ref, *refs):
    out_ref = refs[-1]
    n = own_ref.shape[1]
    peaks, totals = [own_ref[0]], [own_ref[1]]
    for ref, mask in zip(refs, masks):
        for values, into in ((ref[0], peaks), (ref[1], totals)):
            into.append(
                jnp.concatenate([values[r ^ mask : (r ^ mask) + 1] for r in range(n)], axis=0)
            )
    peak = functools.reduce(jnp.maximum, peaks)
    out_ref[0] = peak
    out_ref[1] = functools.reduce(
        jnp.add, [t * jnp.exp(p - peak) for p, t in zip(peaks, totals)]
    )


def gradient_body(x_places, e_places, group, *refs):
    n = len(x_places)
    q_ref, tot_ref = refs[:2]
    dd_ref, pool_ref, scaled_ref, local_ref = refs[-4:]
    rows, features = q_ref.shape
    lanes = local_ref.shape[-1]

    @pl.when(pl.program_id(0) == 0)
    def _():
        total = jnp.zeros((rows, features), f32)
        for g in range(n // group):
            xs, es, hards = [], [], []
            for r in range(g * group, (g + 1) * group):
                i, k = x_places[r]
                xs.append(refs[i][:features] if k is None else refs[i][k, :features])
                i, k = e_places[r]
                scale = jnp.exp(refs[i][k, rows + 2 : rows + 3] - tot_ref[0, r : r + 1])
                scale = scale / tot_ref[1, r : r + 1]
                es.append(refs[i][k, :rows] * scale)
                hards.append(refs[i][k, rows : rows + 1] * scale)
                chosen = jnp.broadcast_to(refs[i][k, rows + 1 : rows + 2], (lanes, rows))
                first = (r - g * group) * rows
                local_ref[g, first : first + rows] = chosen.T.astype(jnp.int32)
            x = jnp.concatenate(xs, axis=1)
            chance = jnp.concatenate(es, axis=1)
            total = total + dot(chance, x, ((1,), (1,)), precision=lax.Precision.HIGHEST)
            high, low = split2(x * (jnp.concatenate(hards, axis=1) / logit_divisor))
            scaled_ref[g, :features] = high
            scaled_ref[g, features:] = low
        dd_ref[...] = (total - q_ref[...]) / logit_divisor

    width = pool_ref.shape[1]
    first = pl.program_id(0) * width
    acc = jnp.zeros((2 * features, width), f32)
    for g in range(n // group):
        local = local_ref[g]
        column = first + lax.broadcasted_iota(jnp.int32, local.shape, 1)
        marks = jnp.concatenate(
            [
                jnp.where(local == column + t * lanes, 1.0, 0.0).astype(bf16)
                for t in range(width // lanes)
            ],
            axis=1,
        )
        acc = acc + dot(scaled_ref[g], marks)
    pool_ref[...] = acc[:features] + acc[features:]


def per_device(question_matrix, document_matrix, pool, hard_owner, hard_local):
    n, depth = lax.axis_size("blk"), lax.axis_size("dim")
    rows, features = question_matrix.shape
    columns = pool.shape[1]
    me = lax.axis_index("blk")
    smem = pl.BlockSpec(memory_space=pltpu.SMEM)
    vmem = pl.BlockSpec(memory_space=pltpu.VMEM)
    block = shape(features + SLACK, rows)
    line = Line()

    def full(*dims):
        return pl.BlockSpec(dims, lambda i: (0,) * len(dims))

    def send(x, mask):
        return lax.ppermute(x, "blk", [(i, i ^ mask) for i in range(n)])

    far = n // 4
    waves = [[0], [2, 4, 8]] + [[4 * k + 2, 4 * k + 4] for k in range(2, far - 1)]
    waves += [[4 * far - 2], [6]]

    x, x_arrays, x_place = {}, [], {}

    def keep(array, r):
        x[r] = array
        x_place[r] = (len(x_arrays), None)
        x_arrays.append(array)

    def relay(r):
        return line(relay_body, block, "relay", [x[r]])

    def forward(k):
        held = relay(4 * k)
        if k % 2 == 0 and 2 <= k < far - 1:
            keep(send(held, 4), 4 * k + 4)
        keep(send(held, 2), 4 * k + 2)

    def share(wave):
        for r in wave:
            keep(send(x[r], 1), r + 1)

    weights, sums, e_place = [], {}, {}
    waiting, stage = [], {}

    def score(blocks):
        k = len(blocks)
        used = sorted({x_place[r][0] for r in blocks})
        part, found = line(
            functools.partial(
                score_body, [(used.index(x_place[r][0]), x_place[r][1]) for r in blocks]
            ),
            (shape(k, rows + SLACK, rows), shape(k, features, rows)),
            "score",
            [me.reshape(1), document_matrix, pool] + [x_arrays[i] for i in used],
            [smem] + [vmem] * (2 + len(used)),
        )
        got = [
            lax.ppermute(part, "dim", [(i, (i + s) % depth) for i in range(depth)])
            for s in range(1, depth)
        ]
        waiting.append((blocks, part, found, got))
        while len(waiting) > 2:
            softmax()

    def softmax():
        blocks, part, found, got = waiting.pop(0)
        k = len(blocks)
        e, *out = line(
            functools.partial(softmax_body, len(got)),
            [shape(k, rows + SLACK, rows)] + [block] * k,
            "softmax",
            [dt, found, part, *got],
        )
        for i, r in enumerate(blocks):
            e_place[r] = (len(weights), i)
        weights.append(e)
        for r, array in zip(blocks, out):
            sums[r] = send(array, 1) if r % 2 else array
        ready = [k for k in groups if 4 * k + 2 in sums and 4 * k + 3 in sums]
        for k in groups:
            if stage.get(k) == 1:
                inward(k)
        for k in ready:
            if k not in stage:
                stage[k] = 0
            elif stage[k] == 0:
                beside(k)

    groups = [0] + list(range(2, far)) + [1]
    over_x, home = {}, []

    def add(*terms):
        return line(merge_body, block, "merge", list(terms))

    def beside(k):
        stage[k] = 1
        over_x[k] = send(add(sums[4 * k + 2], sums[4 * k + 3]), 2)

    def inward(k):
        stage[k] = 2
        whole = add(sums[4 * k], sums[4 * k + 1], over_x[k])
        home.append(send(whole, 4 * k) if k else whole)

    packed = line(
        functools.partial(pack_body, columns),
        block,
        "pack",
        [question_matrix, hard_owner.T, hard_local.T],
        [pl.BlockSpec(memory_space=pltpu.HBM)] * 3,
        limit=62,
        scratch_shapes=[
            pltpu.VMEM(question_matrix.shape, f32),
            pltpu.VMEM(hard_owner.shape[::-1], jnp.int32),
            pltpu.VMEM(hard_local.shape[::-1], jnp.int32),
            pltpu.SemaphoreType.DMA((3,)),
        ],
    )
    keep(packed, 0)
    for k in [2, 1] + [k for k in range(4, far) if k % 2 == 0]:
        keep(send(packed, 4 * k), 4 * k)
    keep(send(packed, 2), 2)
    keep(send(packed, 1), 1)
    dt = line(flip_body, shape(features, rows), "flip", [document_matrix])
    score([0, 1])
    forward(2)
    share(waves[1])
    softmax()
    score([2, 4, 8])
    for w in range(1, len(waves) - 1):
        upcoming = waves[w + 1]
        odds = [r + 1 for r in waves[w]]
        if len(upcoming) == 2:
            forward(upcoming[1] // 4)
        elif w == len(waves) - 3:
            forward(1)
        if len(odds) > 1:
            score(odds)
        share(upcoming)
        if len(upcoming) > 1:
            score(upcoming)
        else:
            score(upcoming + [r + 1 for r in upcoming])
    while waiting:
        softmax()

    totals = line(
        functools.partial(stats_body, [e_place[r] for r in range(n)]),
        shape(2, n, rows),
        "stats",
        weights,
        [
            pl.BlockSpec((e.shape[0], SLACK, rows), lambda i: (0, rows // SLACK, 0))
            for e in weights
        ],
        grid=(1,),
        out_specs=full(2, n, rows),
    )
    mask = 1
    while mask < n:
        there = send(totals, mask)
        if mask < 4:
            for k in groups:
                if stage[k] == 0:
                    beside(k)
        totals = line(
            functools.partial(stats_merge_body, [mask]),
            shape(2, n, rows),
            "stats_merge",
            [totals, there],
        )
        mask *= 2
    for k in groups:
        if stage[k] == 1:
            inward(k)

    group = 4
    width = 512
    e_at = 2 + len(x_arrays)
    document_derivative, grad_pool = line(
        functools.partial(
            gradient_body,
            [(x_place[r][0] + 2, x_place[r][1]) for r in range(n)],
            [(e_at + e_place[r][0], e_place[r][1]) for r in range(n)],
            group,
        ),
        (shape(rows, features), shape(features, columns)),
        "gradient",
        [question_matrix, totals, *x_arrays, *weights],
        limit=48,
        grid=(columns // width,),
        out_specs=(full(rows, features), pl.BlockSpec((features, width), lambda i: (0, i))),
        scratch_shapes=[
            pltpu.VMEM((n // group, 2 * features, group * rows), bf16),
            pltpu.VMEM((n // group, group * rows, 128), jnp.int32),
        ],
    )

    line.last = totals
    arrays = home
    question_derivative, loss = line(
        last_body,
        (shape(rows, features), shape(rows)),
        "finish",
        [document_matrix, weights[0], *arrays],
        [full(rows, features)]
        + [pl.BlockSpec((1, SLACK, rows), lambda i: (0, rows // SLACK, 0))]
        + [full(*a.shape) for a in arrays],
        grid=(1,),
        out_specs=(full(rows, features), full(rows)),
    )
    return loss, question_derivative, document_derivative, grad_pool


def solution(mesh):
    placed = (P("blk", "dim"), P("blk", "dim"), P("dim", "blk"), P("blk", None), P("blk", None))
    return jax.shard_map(
        per_device,
        mesh=mesh,
        in_specs=placed,
        out_specs=(P("blk"), P("blk", "dim"), P("blk", "dim"), P("dim", "blk")),
        check_vma=False,
    )
```

```python
import functools

import jax
import jax.numpy as jnp
from jax import lax
from jax.experimental import pallas as pl
from jax.experimental.pallas import tpu as pltpu
from jax.sharding import PartitionSpec as P

logit_divisor = 0.05
LOWEST = -3.0e38
COST = 3.7e6
SLACK = 8

f32 = jnp.float32
bf16 = jnp.bfloat16


def split2(x):
    high = x.astype(bf16)
    return high, (x - high.astype(f32)).astype(bf16)


def dot(a, b, contract=((1,), (0,)), precision=None):
    return lax.dot_general(
        a, b, (contract, ((), ())), precision=precision, preferred_element_type=f32
    )


class Line:
    def __init__(self):
        self.last = None

    def __call__(self, body, out_shape, name, arrays, us, in_specs=None, limit=16, **kw):
        count = len(arrays)
        if in_specs is None:
            in_specs = [pl.BlockSpec(memory_space=pltpu.VMEM)] * count
        if self.last is not None:
            in_specs = list(in_specs) + [pl.BlockSpec(memory_space=pl.ANY)]
            arrays = list(arrays) + [self.last]

        def kernel(*refs):
            body(*refs[:count], *refs[len(arrays) :])

        out = pl.pallas_call(
            kernel,
            out_shape=out_shape,
            name=name,
            in_specs=in_specs,
            cost_estimate=pl.CostEstimate(
                flops=0, bytes_accessed=int(us * COST), transcendentals=0
            ),
            compiler_params=pltpu.CompilerParams(vmem_limit_bytes=limit << 20),
            **kw,
        )(*arrays)
        self.last = out[-1] if isinstance(out, (list, tuple)) else out
        return out


def shape(*dims, dtype=f32):
    return jax.ShapeDtypeStruct(dims, dtype)


def pack_body(columns, q_hbm, owner_hbm, local_hbm, x_ref, q_ref, owner_ref, local_ref, sems):
    pairs = ((q_hbm, q_ref), (owner_hbm, owner_ref), (local_hbm, local_ref))
    copies = [pltpu.make_async_copy(a, b, sems.at[i]) for i, (a, b) in enumerate(pairs)]
    for copy in copies:
        copy.start()
    for copy in copies:
        copy.wait()
    features = q_ref.shape[1]
    x_ref[:features, :] = q_ref[...].T
    x_ref[features:, :] = (owner_ref[...] * columns + local_ref[...]).astype(f32)


def relay_body(*refs):
    refs[1][...] = refs[0][...]


def flip_body(d_ref, dt_ref):
    dt_ref[...] = d_ref[...].T


def score_body(places, me_ref, d_ref, pool_ref, *refs):
    part_ref, rows_ref = refs[-2:]
    rows, features = d_ref.shape
    columns = pool_ref.shape[1]
    tile = 128
    blocks = [refs[a][...] if k is None else refs[a][k] for a, k in places]
    for k, block in enumerate(blocks):
        x = block[:features]
        named = block[features:].astype(jnp.int32) - me_ref[0] * columns
        here = (named >= 0) & (named < columns)
        local = jnp.sum(jnp.where(here, named, 0), axis=0, keepdims=True)
        owned = jnp.any(here, axis=0, keepdims=True)
        lane = jnp.broadcast_to(local % tile, (features, rows))
        found = jnp.zeros((features, rows), f32)
        for t in range(columns // tile):
            picked = jnp.take_along_axis(
                pool_ref[:, t * tile : (t + 1) * tile], lane, axis=1, mode="promise_in_bounds"
            )
            found = jnp.where(local // tile == t, picked, found)
        rows_ref[k] = found
        hard = jnp.sum(x * found, axis=0, keepdims=True)
        chosen = jnp.where(owned, local, -1).astype(f32)
        part_ref[k, rows:] = jnp.concatenate(
            [hard, chosen, jnp.zeros((SLACK - 2, rows), f32)], axis=0
        )
    x = [block[:features] for block in blocks]
    x = x[0] if len(x) == 1 else jnp.concatenate(x, axis=1)
    scores = dot(d_ref[...], x, precision=lax.Precision.HIGHEST)
    for k in range(len(blocks)):
        part_ref[k, :rows] = scores[:, k * rows : (k + 1) * rows]


def softmax_body(others, dt_ref, rows_ref, part_ref, *refs):
    got, (e_ref, *sum_refs) = refs[:others], refs[others:]
    features, rows = dt_ref.shape
    count = part_ref.shape[0]
    own = lax.broadcasted_iota(jnp.int32, (rows, rows), 0) == lax.broadcasted_iota(
        jnp.int32, (rows, rows), 1
    )
    tails, es = [], []
    for k in range(count):
        whole = part_ref[k]
        chosen = whole[rows + 1 : rows + 2]
        for r in got:
            whole = whole + r[k]
        scores = whole[:rows] / logit_divisor
        hard = jnp.where(chosen >= 0, whole[rows : rows + 1] / logit_divisor, LOWEST)
        peak = jnp.maximum(jnp.max(scores, axis=0, keepdims=True), hard)
        e = jnp.exp(scores - peak)
        hard_e = jnp.where(chosen >= 0, jnp.exp(hard - peak), 0.0)
        total = jnp.sum(e, axis=0, keepdims=True) + hard_e
        positive = jnp.sum(jnp.where(own, scores, 0.0), axis=0, keepdims=True)
        e_ref[k, :rows] = e
        e_ref[k, rows:] = jnp.concatenate(
            [hard_e, chosen, peak, total, positive, jnp.zeros((SLACK - 5, rows), f32)], axis=0
        )
        es.append(e)
        tails.append((hard_e, peak, total))
    e = es[0] if count == 1 else jnp.concatenate(es, axis=1)
    sums = dot(dt_ref[...], e, precision=lax.Precision.HIGHEST)
    for k, (hard_e, peak, total) in enumerate(tails):
        at = sum_refs[k]
        at[:features] = sums[:, k * rows : (k + 1) * rows] + rows_ref[k] * hard_e
        at[features:] = jnp.concatenate([peak, total, jnp.zeros((SLACK - 2, rows), f32)], axis=0)


def merge(terms):
    size = terms[0].shape[0] - SLACK
    peaks = [t[size : size + 1] for t in terms]
    peak = functools.reduce(jnp.maximum, peaks)
    scales = [jnp.exp(p - peak) for p in peaks]
    sums = functools.reduce(jnp.add, [t[:size] * s for t, s in zip(terms, scales)])
    total = functools.reduce(
        jnp.add, [t[size + 1 : size + 2] * s for t, s in zip(terms, scales)]
    )
    return sums, peak, total


def merge_body(*refs):
    out_ref = refs[-1]
    sums, peak, total = merge([ref[...] for ref in refs[:-1]])
    size = sums.shape[0]
    out_ref[:size] = sums
    out_ref[size:] = jnp.concatenate(
        [peak, total, jnp.zeros((SLACK - 2, peak.shape[1]), f32)], axis=0
    )


def last_body(d_ref, e_ref, *refs):
    dq_ref, loss_ref = refs[-2:]
    sums, peak, total = merge([ref[...] for ref in refs[:-2]])
    dq_ref[...] = ((sums / total).T - d_ref[...]) / logit_divisor
    log_total = peak + jnp.log(total)
    loss_ref[...] = (log_total - e_ref[0, 4:5]).reshape(loss_ref.shape)


def stats_body(places, *refs):
    out_ref = refs[-1]
    for r, (i, k) in enumerate(places):
        out_ref[0, r : r + 1] = refs[i][k, 2:3]
        out_ref[1, r : r + 1] = refs[i][k, 3:4]


def stats_merge_body(masks, own_ref, *refs):
    out_ref = refs[-1]
    n = own_ref.shape[1]
    peaks, totals = [own_ref[0]], [own_ref[1]]
    for ref, mask in zip(refs, masks):
        for values, into in ((ref[0], peaks), (ref[1], totals)):
            into.append(
                jnp.concatenate([values[r ^ mask : (r ^ mask) + 1] for r in range(n)], axis=0)
            )
    peak = functools.reduce(jnp.maximum, peaks)
    out_ref[0] = peak
    out_ref[1] = functools.reduce(
        jnp.add, [t * jnp.exp(p - peak) for p, t in zip(peaks, totals)]
    )


def gradient_body(x_places, e_places, group, *refs):
    n = len(x_places)
    q_ref, tot_ref = refs[:2]
    dd_ref, pool_ref, scaled_ref, local_ref = refs[-4:]
    rows, features = q_ref.shape
    lanes = local_ref.shape[-1]

    @pl.when(pl.program_id(0) == 0)
    def _():
        total = jnp.zeros((rows, features), f32)
        for g in range(n // group):
            xs, es, hards = [], [], []
            for r in range(g * group, (g + 1) * group):
                i, k = x_places[r]
                xs.append(refs[i][:features] if k is None else refs[i][k, :features])
                i, k = e_places[r]
                scale = jnp.exp(refs[i][k, rows + 2 : rows + 3] - tot_ref[0, r : r + 1])
                scale = scale / tot_ref[1, r : r + 1]
                es.append(refs[i][k, :rows] * scale)
                hards.append(refs[i][k, rows : rows + 1] * scale)
                chosen = jnp.broadcast_to(refs[i][k, rows + 1 : rows + 2], (lanes, rows))
                first = (r - g * group) * rows
                local_ref[g, first : first + rows] = chosen.T.astype(jnp.int32)
            x = jnp.concatenate(xs, axis=1)
            chance = jnp.concatenate(es, axis=1)
            total = total + dot(chance, x, ((1,), (1,)), precision=lax.Precision.HIGHEST)
            high, low = split2(x * (jnp.concatenate(hards, axis=1) / logit_divisor))
            scaled_ref[g, :features] = high
            scaled_ref[g, features:] = low
        dd_ref[...] = (total - q_ref[...]) / logit_divisor

    width = pool_ref.shape[1]
    first = pl.program_id(0) * width
    acc = jnp.zeros((2 * features, width), f32)
    for g in range(n // group):
        local = local_ref[g]
        column = first + lax.broadcasted_iota(jnp.int32, local.shape, 1)
        marks = jnp.concatenate(
            [
                jnp.where(local == column + t * lanes, 1.0, 0.0).astype(bf16)
                for t in range(width // lanes)
            ],
            axis=1,
        )
        acc = acc + dot(scaled_ref[g], marks)
    pool_ref[...] = acc[:features] + acc[features:]


def per_device(question_matrix, document_matrix, pool, hard_owner, hard_local):
    n, depth = lax.axis_size("blk"), lax.axis_size("dim")
    rows, features = question_matrix.shape
    columns = pool.shape[1]
    me = lax.axis_index("blk")
    smem = pl.BlockSpec(memory_space=pltpu.SMEM)
    vmem = pl.BlockSpec(memory_space=pltpu.VMEM)
    block = shape(features + SLACK, rows)
    line = Line()

    def full(*dims):
        return pl.BlockSpec(dims, lambda i: (0,) * len(dims))

    def send(x, mask):
        return lax.ppermute(x, "blk", [(i, i ^ mask) for i in range(n)])

    far = n // 4
    x, x_arrays, x_place = {}, [], {}

    def keep(array, r):
        x[r] = array
        x_place[r] = (len(x_arrays), None)
        x_arrays.append(array)

    def relay(r):
        x_arrays[x_place[r][0]] = x[r] = line(relay_body, block, "relay", [x[r]], 0.05)

    def forward(k):
        relay(4 * k)
        if k % 2 == 0 and k + 1 < far:
            keep(send(x[4 * k], 4), 4 * k + 4)
        keep(send(x[4 * k], 2), 4 * k + 2)

    def share(*blocks):
        for r in blocks:
            keep(send(x[r], 1), r + 1)

    weights, sums, e_place = [], {}, {}
    waiting, stage = [], {}

    def score(blocks):
        k = len(blocks)
        used = sorted({x_place[r][0] for r in blocks})
        part, found = line(
            functools.partial(
                score_body, [(used.index(x_place[r][0]), x_place[r][1]) for r in blocks]
            ),
            (shape(k, rows + SLACK, rows), shape(k, features, rows)),
            "score",
            [me.reshape(1), document_matrix, pool] + [x_arrays[i] for i in used],
            0.9 * k,
            [smem] + [vmem] * (2 + len(used)),
        )
        got = [
            lax.ppermute(part, "dim", [(i, (i + s) % depth) for i in range(depth)])
            for s in range(1, depth)
        ]
        waiting.append((blocks, part, found, got))

    def softmax():
        blocks, part, found, got = waiting.pop(0)
        k = len(blocks)
        e, *out = line(
            functools.partial(softmax_body, len(got)),
            [shape(k, rows + SLACK, rows)] + [block] * k,
            "softmax",
            [dt, found, part, *got],
            0.25 * k,
        )
        for i, r in enumerate(blocks):
            e_place[r] = (len(weights), i)
        weights.append(e)
        for r, array in zip(blocks, out):
            sums[r] = send(array, 1) if r % 2 else array

    over_x, home = {}, []

    def add(*terms):
        return line(merge_body, block, "merge", list(terms), 0.05)

    def beside(k):
        over_x[k] = send(add(sums[4 * k + 2], sums[4 * k + 3]), 2)

    def inward(k):
        whole = add(sums[4 * k], sums[4 * k + 1], over_x[k])
        home.append(send(whole, 4 * k) if k else whole)

    packed = line(
        functools.partial(pack_body, columns),
        block,
        "pack",
        [question_matrix, hard_owner.T, hard_local.T],
        1.8,
        [pl.BlockSpec(memory_space=pltpu.HBM)] * 3,
        limit=62,
        scratch_shapes=[
            pltpu.VMEM(question_matrix.shape, f32),
            pltpu.VMEM(hard_owner.shape[::-1], jnp.int32),
            pltpu.VMEM(hard_local.shape[::-1], jnp.int32),
            pltpu.SemaphoreType.DMA((3,)),
        ],
    )
    keep(packed, 0)
    for k in [2, 1] + [k for k in range(4, far) if k % 2 == 0]:
        keep(send(packed, 4 * k), 4 * k)
    keep(send(packed, 2), 2)
    keep(send(packed, 1), 1)
    dt = line(flip_body, shape(features, rows), "flip", [document_matrix], 0.1)
    score([0, 1])
    relay(2)
    forward(2)
    forward(1)
    share(2, 4, 8)
    softmax()
    score([2, 4, 8])
    relay(10)
    if far > 3:
        forward(3)
    share(10, 6)
    score([3, 5, 9])
    softmax()
    relay(6)
    score([10, 6, 11, 7])
    softmax()
    for k in range(3, far):
        if k + 1 < far:
            forward(k + 1)
        share(4 * k, 4 * k + 2)
        score([4 * k, 4 * k + 2, 4 * k + 1, 4 * k + 3])
        if k == 3:
            beside(0)
        softmax()
        if k == 3:
            beside(2)
            beside(1)
        else:
            beside(k - 1)
    inward(0)
    softmax()

    totals = line(
        functools.partial(stats_body, [e_place[r] for r in range(n)]),
        shape(2, n, rows),
        "stats",
        weights,
        0.05,
        [
            pl.BlockSpec((e.shape[0], SLACK, rows), lambda i: (0, rows // SLACK, 0))
            for e in weights
        ],
        grid=(1,),
        out_specs=full(2, n, rows),
    )
    mask = 1
    while mask < n:
        there = send(totals, mask)
        totals = line(
            functools.partial(stats_merge_body, [mask]),
            shape(2, n, rows),
            "stats_merge",
            [totals, there],
            0.05,
        )
        if mask == 2 and far > 3:
            inward(2)
        if mask == 1:
            beside(far - 1)
        if mask == 4:
            inward(1)
            for k in range(3, far - 1):
                inward(k)
        mask *= 2
    inward(far - 1)

    group = 4
    width = 512
    e_at = 2 + len(x_arrays)
    document_derivative, grad_pool = line(
        functools.partial(
            gradient_body,
            [(x_place[r][0] + 2, x_place[r][1]) for r in range(n)],
            [(e_at + e_place[r][0], e_place[r][1]) for r in range(n)],
            group,
        ),
        (shape(rows, features), shape(features, columns)),
        "gradient",
        [question_matrix, totals, *x_arrays, *weights],
        11.0,
        limit=48,
        grid=(columns // width,),
        out_specs=(full(rows, features), pl.BlockSpec((features, width), lambda i: (0, i))),
        scratch_shapes=[
            pltpu.VMEM((n // group, 2 * features, group * rows), bf16),
            pltpu.VMEM((n // group, group * rows, 128), jnp.int32),
        ],
    )

    line.last = totals
    arrays = home
    question_derivative, loss = line(
        last_body,
        (shape(rows, features), shape(rows)),
        "finish",
        [document_matrix, weights[0], *arrays],
        0.8,
        [full(rows, features)]
        + [pl.BlockSpec((1, SLACK, rows), lambda i: (0, rows // SLACK, 0))]
        + [full(*a.shape) for a in arrays],
        grid=(1,),
        out_specs=(full(rows, features), full(rows)),
    )
    return loss, question_derivative, document_derivative, grad_pool


def solution(mesh):
    placed = (P("blk", "dim"), P("blk", "dim"), P("dim", "blk"), P("blk", None), P("blk", None))
    return jax.shard_map(
        per_device,
        mesh=mesh,
        in_specs=placed,
        out_specs=(P("blk"), P("blk", "dim"), P("blk", "dim"), P("dim", "blk")),
        check_vma=False,
    )
```

```python
import functools

import jax
import jax.numpy as jnp
from jax import lax
from jax.experimental import pallas as pl
from jax.experimental.pallas import tpu as pltpu
from jax.sharding import PartitionSpec as P

logit_divisor = 0.05
LOWEST = -3.0e38
COST = 3.7e6
SLACK = 8

f32 = jnp.float32
bf16 = jnp.bfloat16


def split2(x):
    high = x.astype(bf16)
    return high, (x - high.astype(f32)).astype(bf16)


def dot(a, b, contract=((1,), (0,)), precision=None):
    return lax.dot_general(
        a, b, (contract, ((), ())), precision=precision, preferred_element_type=f32
    )


class Line:
    def __init__(self):
        self.last = None

    def __call__(self, body, out_shape, name, arrays, us, in_specs=None, limit=16, **kw):
        count = len(arrays)
        if in_specs is None:
            in_specs = [pl.BlockSpec(memory_space=pltpu.VMEM)] * count
        if self.last is not None:
            in_specs = list(in_specs) + [pl.BlockSpec(memory_space=pl.ANY)]
            arrays = list(arrays) + [self.last]

        def kernel(*refs):
            body(*refs[:count], *refs[len(arrays) :])

        out = pl.pallas_call(
            kernel,
            out_shape=out_shape,
            name=name,
            in_specs=in_specs,
            cost_estimate=pl.CostEstimate(
                flops=0, bytes_accessed=int(us * COST), transcendentals=0
            ),
            compiler_params=pltpu.CompilerParams(vmem_limit_bytes=limit << 20),
            **kw,
        )(*arrays)
        self.last = out[-1] if isinstance(out, (list, tuple)) else out
        return out


def shape(*dims, dtype=f32):
    return jax.ShapeDtypeStruct(dims, dtype)


def pack_body(columns, q_hbm, owner_hbm, local_hbm, x_ref, q_ref, owner_ref, local_ref, sems):
    pairs = ((q_hbm, q_ref), (owner_hbm, owner_ref), (local_hbm, local_ref))
    copies = [pltpu.make_async_copy(a, b, sems.at[i]) for i, (a, b) in enumerate(pairs)]
    for copy in copies:
        copy.start()
    for copy in copies:
        copy.wait()
    features = q_ref.shape[1]
    x_ref[:features, :] = q_ref[...].T
    x_ref[features:, :] = (owner_ref[...] * columns + local_ref[...]).astype(f32)


def relay_body(*refs):
    for k, ref in enumerate(refs[:-1]):
        refs[-1][k] = ref[...]


def flip_body(d_ref, dt_ref):
    dt_ref[...] = d_ref[...].T


def score_body(places, me_ref, d_ref, pool_ref, *refs):
    part_ref, rows_ref = refs[-2:]
    rows, features = d_ref.shape
    columns = pool_ref.shape[1]
    tile = 128
    blocks = [refs[a][...] if k is None else refs[a][k] for a, k in places]
    for k, block in enumerate(blocks):
        x = block[:features]
        named = block[features:].astype(jnp.int32) - me_ref[0] * columns
        here = (named >= 0) & (named < columns)
        local = jnp.sum(jnp.where(here, named, 0), axis=0, keepdims=True)
        owned = jnp.any(here, axis=0, keepdims=True)
        lane = jnp.broadcast_to(local % tile, (features, rows))
        found = jnp.zeros((features, rows), f32)
        for t in range(columns // tile):
            picked = jnp.take_along_axis(
                pool_ref[:, t * tile : (t + 1) * tile], lane, axis=1, mode="promise_in_bounds"
            )
            found = jnp.where(local // tile == t, picked, found)
        rows_ref[k] = found
        hard = jnp.sum(x * found, axis=0, keepdims=True)
        chosen = jnp.where(owned, local, -1).astype(f32)
        part_ref[k, rows:] = jnp.concatenate(
            [hard, chosen, jnp.zeros((SLACK - 2, rows), f32)], axis=0
        )
    x = [block[:features] for block in blocks]
    x = x[0] if len(x) == 1 else jnp.concatenate(x, axis=1)
    scores = dot(d_ref[...], x, precision=lax.Precision.HIGHEST)
    for k in range(len(blocks)):
        part_ref[k, :rows] = scores[:, k * rows : (k + 1) * rows]


def softmax_body(evens, others, dt_ref, rows_ref, part_ref, *refs):
    got, (e_ref, *sum_refs) = refs[:others], refs[others:]
    features, rows = dt_ref.shape
    count = part_ref.shape[0]
    own = lax.broadcasted_iota(jnp.int32, (rows, rows), 0) == lax.broadcasted_iota(
        jnp.int32, (rows, rows), 1
    )
    tails, es = [], []
    for k in range(count):
        whole = part_ref[k]
        chosen = whole[rows + 1 : rows + 2]
        for r in got:
            whole = whole + r[k]
        scores = whole[:rows] / logit_divisor
        hard = jnp.where(chosen >= 0, whole[rows : rows + 1] / logit_divisor, LOWEST)
        peak = jnp.maximum(jnp.max(scores, axis=0, keepdims=True), hard)
        e = jnp.exp(scores - peak)
        hard_e = jnp.where(chosen >= 0, jnp.exp(hard - peak), 0.0)
        total = jnp.sum(e, axis=0, keepdims=True) + hard_e
        positive = jnp.sum(jnp.where(own, scores, 0.0), axis=0, keepdims=True)
        e_ref[k, :rows] = e
        e_ref[k, rows:] = jnp.concatenate(
            [hard_e, chosen, peak, total, positive, jnp.zeros((SLACK - 5, rows), f32)], axis=0
        )
        es.append(e)
        tails.append((hard_e, peak, total))
    e = es[0] if count == 1 else jnp.concatenate(es, axis=1)
    sums = dot(dt_ref[...], e, precision=lax.Precision.HIGHEST)
    for k, (hard_e, peak, total) in enumerate(tails):
        at = sum_refs[k] if k < evens else sum_refs[-1].at[k - evens]
        at[:features] = sums[:, k * rows : (k + 1) * rows] + rows_ref[k] * hard_e
        at[features:] = jnp.concatenate([peak, total, jnp.zeros((SLACK - 2, rows), f32)], axis=0)


def merge(terms):
    size = terms[0].shape[0] - SLACK
    peaks = [t[size : size + 1] for t in terms]
    peak = functools.reduce(jnp.maximum, peaks)
    scales = [jnp.exp(p - peak) for p in peaks]
    sums = functools.reduce(jnp.add, [t[:size] * s for t, s in zip(terms, scales)])
    total = functools.reduce(
        jnp.add, [t[size + 1 : size + 2] * s for t, s in zip(terms, scales)]
    )
    return sums, peak, total


def merge_body(places, *refs):
    out_ref = refs[-1]
    sums, peak, total = merge([r[...] if k is None else r[k] for r, k in zip(refs, places)])
    size = sums.shape[0]
    out_ref[:size] = sums
    out_ref[size:] = jnp.concatenate(
        [peak, total, jnp.zeros((SLACK - 2, peak.shape[1]), f32)], axis=0
    )


def last_body(d_ref, e_ref, *refs):
    dq_ref, loss_ref = refs[-2:]
    sums, peak, total = merge([ref[...] for ref in refs[:-2]])
    dq_ref[...] = ((sums / total).T - d_ref[...]) / logit_divisor
    log_total = peak + jnp.log(total)
    loss_ref[...] = (log_total - e_ref[0, 4:5]).reshape(loss_ref.shape)


def stats_body(places, *refs):
    out_ref = refs[-1]
    for r, (i, k) in enumerate(places):
        out_ref[0, r : r + 1] = refs[i][k, 2:3]
        out_ref[1, r : r + 1] = refs[i][k, 3:4]


def stats_merge_body(masks, own_ref, *refs):
    out_ref = refs[-1]
    n = own_ref.shape[1]
    peaks, totals = [own_ref[0]], [own_ref[1]]
    for ref, mask in zip(refs, masks):
        for values, into in ((ref[0], peaks), (ref[1], totals)):
            into.append(
                jnp.concatenate([values[r ^ mask : (r ^ mask) + 1] for r in range(n)], axis=0)
            )
    peak = functools.reduce(jnp.maximum, peaks)
    out_ref[0] = peak
    out_ref[1] = functools.reduce(
        jnp.add, [t * jnp.exp(p - peak) for p, t in zip(peaks, totals)]
    )


def gradient_body(x_places, e_places, group, *refs):
    n = len(x_places)
    tot_ref = refs[0]
    dd_ref, pool_ref, scaled_ref, local_ref = refs[-4:]
    rows, features = dd_ref.shape
    lanes = local_ref.shape[-1]

    @pl.when(pl.program_id(0) == 0)
    def _():
        own = lax.broadcasted_iota(jnp.int32, (rows, rows), 0) == lax.broadcasted_iota(
            jnp.int32, (rows, rows), 1
        )
        total = jnp.zeros((features, rows), f32)
        for g in range(n // group):
            xs, es, hards = [], [], []
            for r in range(g * group, (g + 1) * group):
                i, k = x_places[r]
                xs.append(refs[i][:features] if k is None else refs[i][k, :features])
                i, k = e_places[r]
                scale = jnp.exp(refs[i][k, rows + 2 : rows + 3] - tot_ref[0, r : r + 1])
                scale = scale / tot_ref[1, r : r + 1]
                e = refs[i][k, :rows] * scale
                es.append(e if r else jnp.where(own, e - 1.0, e))
                hards.append(refs[i][k, rows : rows + 1] * scale)
                chosen = jnp.broadcast_to(refs[i][k, rows + 1 : rows + 2], (lanes, rows))
                first = (r - g * group) * rows
                local_ref[g, first : first + rows] = chosen.T.astype(jnp.int32)
            x = jnp.concatenate(xs, axis=1)
            chance = jnp.concatenate(es, axis=1)
            high, low = split2(x)
            c_high, c_low = split2(chance)
            both = dot(jnp.concatenate([high, low], axis=0), c_high, ((1,), (1,)))
            total = total + both[:features] + both[features:]
            total = total + dot(high, c_low, ((1,), (1,)))
            high, low = split2(x * (jnp.concatenate(hards, axis=1) / logit_divisor))
            scaled_ref[g, :features] = high
            scaled_ref[g, features:] = low
        dd_ref[...] = total.T / logit_divisor

    width = pool_ref.shape[1]
    first = pl.program_id(0) * width
    acc = jnp.zeros((2 * features, width), f32)
    for g in range(n // group):
        local = local_ref[g]
        column = first + lax.broadcasted_iota(jnp.int32, local.shape, 1)
        marks = jnp.concatenate(
            [
                jnp.where(local == column + t * lanes, 1.0, 0.0).astype(bf16)
                for t in range(width // lanes)
            ],
            axis=1,
        )
        acc = acc + dot(scaled_ref[g], marks)
    pool_ref[...] = acc[:features] + acc[features:]


def per_device(question_matrix, document_matrix, pool, hard_owner, hard_local):
    n, depth = lax.axis_size("blk"), lax.axis_size("dim")
    rows, features = question_matrix.shape
    columns = pool.shape[1]
    me = lax.axis_index("blk")
    smem = pl.BlockSpec(memory_space=pltpu.SMEM)
    vmem = pl.BlockSpec(memory_space=pltpu.VMEM)
    block = shape(features + SLACK, rows)
    line = Line()

    def full(*dims):
        return pl.BlockSpec(dims, lambda i: (0,) * len(dims))

    def send(x, mask):
        return lax.ppermute(x, "blk", [(i, i ^ mask) for i in range(n)])

    far = n // 4
    x, x_arrays, x_place = {}, [], {}

    def keep(array, *blocks):
        for k, r in enumerate(blocks):
            x[r] = array
            x_place[r] = (len(x_arrays), k if array.ndim == 3 else None)
        x_arrays.append(array)

    def pass_on(array):
        return line(lambda a, out: out.__setitem__(..., a[...]), block, "relay", [array], 0.05)

    def relay(r):
        x_arrays[x_place[r][0]] = x[r] = pass_on(x[r])

    def forward(k):
        relay(4 * k)
        if k % 2 == 0 and k + 1 < far:
            keep(send(x[4 * k], 4), 4 * k + 4)
        keep(send(x[4 * k], 2), 4 * k + 2)

    def share(*blocks):
        for r in blocks:
            keep(send(x[r], 1), r + 1)

    def share_all(*blocks):
        out = shape(len(blocks), features + SLACK, rows)
        held = line(relay_body, out, "relay", [x[r] for r in blocks], 0.05)
        keep(send(held, 1), *[r + 1 for r in blocks])

    weights, sums, e_place = [], {}, {}
    waiting, stage = [], {}

    def score(blocks):
        k = len(blocks)
        used = sorted({x_place[r][0] for r in blocks})
        part, found = line(
            functools.partial(
                score_body, [(used.index(x_place[r][0]), x_place[r][1]) for r in blocks]
            ),
            (shape(k, rows + SLACK, rows), shape(k, features, rows)),
            "score",
            [me.reshape(1), document_matrix, pool] + [x_arrays[i] for i in used],
            0.9 * k,
            [smem] + [vmem] * (2 + len(used)),
        )
        got = [
            lax.ppermute(part, "dim", [(i, (i + s) % depth) for i in range(depth)])
            for s in range(1, depth)
        ]
        waiting.append((blocks, part, found, got))

    def softmax():
        blocks, part, found, got = waiting.pop(0)
        k = len(blocks)
        odds = [r for r in blocks if r % 2]
        evens = k - len(odds)
        e, *out = line(
            functools.partial(softmax_body, evens, len(got)),
            [shape(k, rows + SLACK, rows)]
            + [block] * evens
            + [shape(len(odds), features + SLACK, rows)] * (len(odds) > 0),
            "softmax",
            [dt, found, part, *got],
            0.25 * k,
        )
        for i, r in enumerate(blocks):
            e_place[r] = (len(weights), i)
        weights.append(e)
        for r, array in zip(blocks, out[:evens]):
            sums[r] = (array, None)
        if odds:
            shared = send(out[-1], 1)
            for i, r in enumerate(odds):
                sums[r] = (shared, i)

    over_x, home = {}, []

    def add(*terms):
        arrays = [array for array, k in terms]
        places = [k for array, k in terms]
        return line(functools.partial(merge_body, places), block, "merge", arrays, 0.05)

    def pair(*blocks):
        for r in blocks:
            sums[r] = (add(sums[r], sums[r + 1]), None)

    def beside(k):
        over_x[k] = send(sums[4 * k + 2][0], 2)

    def inward(k):
        whole = add(sums[4 * k], (over_x[k], None))
        home.append(send(whole, 4 * k) if k else whole)

    packed = line(
        functools.partial(pack_body, columns),
        block,
        "pack",
        [question_matrix, hard_owner.T, hard_local.T],
        1.8,
        [pl.BlockSpec(memory_space=pltpu.HBM)] * 3,
        limit=62,
        scratch_shapes=[
            pltpu.VMEM(question_matrix.shape, f32),
            pltpu.VMEM(hard_owner.shape[::-1], jnp.int32),
            pltpu.VMEM(hard_local.shape[::-1], jnp.int32),
            pltpu.SemaphoreType.DMA((3,)),
        ],
    )
    keep(packed, 0)
    for k in [2, 1] + [k for k in range(4, far) if k % 2 == 0]:
        keep(send(packed, 4 * k), 4 * k)
    keep(send(packed, 2), 2)
    keep(send(packed, 1), 1)
    dt = line(flip_body, shape(features, rows), "flip", [document_matrix], 0.1)
    score([0, 1])
    forward(2)
    forward(1)
    relay(2)
    share_all(2, 4, 8)
    softmax()
    score([2, 4, 8])
    relay(10)
    forward(3)
    score([3, 5, 9])
    relay(6)
    share(10, 6)
    softmax()
    score([10, 6, 11, 7])
    relay(14)
    share(12, 14)
    softmax()
    for k in range(3, far):
        if k + 1 < far:
            forward(k + 1)
        score([4 * k, 4 * k + 2, 4 * k + 1, 4 * k + 3])
        if k + 1 < far:
            relay(4 * k + 6)
            share(4 * k + 4, 4 * k + 6)
        if k == 3:
            pair(0, 2, 4, 8)
        softmax()
        if k == 3:
            pair(10)
            beside(2)
            pair(6)
            beside(1)
        else:
            pair(4 * k - 2, 4 * k - 4)
            beside(k - 1)
    softmax()

    totals = line(
        functools.partial(stats_body, [e_place[r] for r in range(n)]),
        shape(2, n, rows),
        "stats",
        weights,
        0.05,
        [
            pl.BlockSpec((e.shape[0], SLACK, rows), lambda i: (0, rows // SLACK, 0))
            for e in weights
        ],
        grid=(1,),
        out_specs=full(2, n, rows),
    )
    mask = 1
    while mask < n:
        there = send(totals, mask)
        if mask == 1:
            inward(2)
        totals = line(
            functools.partial(stats_merge_body, [mask]),
            shape(2, n, rows),
            "stats_merge",
            [totals, there],
            0.05,
        )
        if mask == 2:
            inward(1)
            pair(4 * far - 2)
            beside(far - 1)
            beside(0)
            pair(4 * far - 4)
        if mask == 4:
            for k in range(3, far):
                inward(k)
        mask *= 2
    sums[0] = (add(sums[0], (home.pop(0), None)), None)

    group = 4
    width = 512
    e_at = 1 + len(x_arrays)
    document_derivative, grad_pool = line(
        functools.partial(
            gradient_body,
            [(x_place[r][0] + 1, x_place[r][1]) for r in range(n)],
            [(e_at + e_place[r][0], e_place[r][1]) for r in range(n)],
            group,
        ),
        (shape(rows, features), shape(features, columns)),
        "gradient",
        [totals, *x_arrays, *weights],
        11.0,
        limit=48,
        grid=(columns // width,),
        out_specs=(full(rows, features), pl.BlockSpec((features, width), lambda i: (0, i))),
        scratch_shapes=[
            pltpu.VMEM((n // group, 2 * features, group * rows), bf16),
            pltpu.VMEM((n // group, group * rows, 128), jnp.int32),
        ],
    )

    line.last = totals
    inward(0)
    arrays = home
    question_derivative, loss = line(
        last_body,
        (shape(rows, features), shape(rows)),
        "finish",
        [document_matrix, weights[0], *arrays],
        0.8,
        [full(rows, features)]
        + [pl.BlockSpec((1, SLACK, rows), lambda i: (0, rows // SLACK, 0))]
        + [full(*a.shape) for a in arrays],
        grid=(1,),
        out_specs=(full(rows, features), full(rows)),
    )
    return loss, question_derivative, document_derivative, grad_pool


def solution(mesh):
    placed = (P("blk", "dim"), P("blk", "dim"), P("dim", "blk"), P("blk", None), P("blk", None))
    return jax.shard_map(
        per_device,
        mesh=mesh,
        in_specs=placed,
        out_specs=(P("blk"), P("blk", "dim"), P("blk", "dim"), P("dim", "blk")),
        check_vma=False,
    )
```

```python
import functools

import jax
import jax.numpy as jnp
from jax import lax
from jax.experimental import pallas as pl
from jax.experimental.pallas import tpu as pltpu
from jax.sharding import PartitionSpec as P

logit_divisor = 0.05
LOWEST = -3.0e38
COST = 3.7e6
SLACK = 8

f32 = jnp.float32
bf16 = jnp.bfloat16


def split2(x):
    high = x.astype(bf16)
    return high, (x - high.astype(f32)).astype(bf16)


def dot(a, b, contract=((1,), (0,)), precision=None):
    return lax.dot_general(
        a, b, (contract, ((), ())), precision=precision, preferred_element_type=f32
    )


class Line:
    def __init__(self):
        self.last = None

    def __call__(self, body, out_shape, name, arrays, us, in_specs=None, limit=16, **kw):
        count = len(arrays)
        if in_specs is None:
            in_specs = [pl.BlockSpec(memory_space=pltpu.VMEM)] * count
        if self.last is not None:
            in_specs = list(in_specs) + [pl.BlockSpec(memory_space=pl.ANY)]
            arrays = list(arrays) + [self.last]

        def kernel(*refs):
            body(*refs[:count], *refs[len(arrays) :])

        out = pl.pallas_call(
            kernel,
            out_shape=out_shape,
            name=name,
            in_specs=in_specs,
            cost_estimate=pl.CostEstimate(
                flops=0, bytes_accessed=int(us * COST), transcendentals=0
            ),
            compiler_params=pltpu.CompilerParams(vmem_limit_bytes=limit << 20),
            **kw,
        )(*arrays)
        self.last = out[-1] if isinstance(out, (list, tuple)) else out
        return out


def shape(*dims, dtype=f32):
    return jax.ShapeDtypeStruct(dims, dtype)


def pack_body(columns, q_hbm, owner_hbm, local_hbm, x_ref, q_ref, owner_ref, local_ref, sems):
    pairs = ((q_hbm, q_ref), (owner_hbm, owner_ref), (local_hbm, local_ref))
    copies = [pltpu.make_async_copy(a, b, sems.at[i]) for i, (a, b) in enumerate(pairs)]
    for copy in copies:
        copy.start()
    for copy in copies:
        copy.wait()
    features = q_ref.shape[1]
    x_ref[:features, :] = q_ref[...].T
    x_ref[features:, :] = (owner_ref[...] * columns + local_ref[...]).astype(f32)


def relay_body(*refs):
    for k, ref in enumerate(refs[:-1]):
        refs[-1][k] = ref[...]


def flip_body(d_ref, dt_ref):
    dt_ref[...] = d_ref[...].T


def score_body(places, me_ref, d_ref, pool_ref, *refs):
    part_ref, rows_ref = refs[-2:]
    rows, features = d_ref.shape
    columns = pool_ref.shape[1]
    tile = 128
    blocks = [refs[a][...] if k is None else refs[a][k] for a, k in places]
    for k, block in enumerate(blocks):
        x = block[:features]
        named = block[features:].astype(jnp.int32) - me_ref[0] * columns
        here = (named >= 0) & (named < columns)
        local = jnp.sum(jnp.where(here, named, 0), axis=0, keepdims=True)
        owned = jnp.any(here, axis=0, keepdims=True)
        lane = jnp.broadcast_to(local % tile, (features, rows))
        found = jnp.zeros((features, rows), f32)
        for t in range(columns // tile):
            picked = jnp.take_along_axis(
                pool_ref[:, t * tile : (t + 1) * tile], lane, axis=1, mode="promise_in_bounds"
            )
            found = jnp.where(local // tile == t, picked, found)
        rows_ref[k] = found
        hard = jnp.sum(x * found, axis=0, keepdims=True)
        chosen = jnp.where(owned, local, -1).astype(f32)
        part_ref[k, rows:] = jnp.concatenate(
            [hard, chosen, jnp.zeros((SLACK - 2, rows), f32)], axis=0
        )
    x = [block[:features] for block in blocks]
    x = x[0] if len(x) == 1 else jnp.concatenate(x, axis=1)
    scores = dot(d_ref[...], x, precision=lax.Precision.HIGHEST)
    for k in range(len(blocks)):
        part_ref[k, :rows] = scores[:, k * rows : (k + 1) * rows]


def softmax_body(evens, others, dt_ref, rows_ref, part_ref, *refs):
    got, (e_ref, *sum_refs) = refs[:others], refs[others:]
    features, rows = dt_ref.shape
    count = part_ref.shape[0]
    own = lax.broadcasted_iota(jnp.int32, (rows, rows), 0) == lax.broadcasted_iota(
        jnp.int32, (rows, rows), 1
    )
    tails, es = [], []
    for k in range(count):
        whole = part_ref[k]
        chosen = whole[rows + 1 : rows + 2]
        for r in got:
            whole = whole + r[k]
        scores = whole[:rows] / logit_divisor
        hard = jnp.where(chosen >= 0, whole[rows : rows + 1] / logit_divisor, LOWEST)
        peak = jnp.maximum(jnp.max(scores, axis=0, keepdims=True), hard)
        e = jnp.exp(scores - peak)
        hard_e = jnp.where(chosen >= 0, jnp.exp(hard - peak), 0.0)
        total = jnp.sum(e, axis=0, keepdims=True) + hard_e
        positive = jnp.sum(jnp.where(own, scores, 0.0), axis=0, keepdims=True)
        e_ref[k, :rows] = e
        e_ref[k, rows:] = jnp.concatenate(
            [hard_e, chosen, peak, total, positive, jnp.zeros((SLACK - 5, rows), f32)], axis=0
        )
        es.append(e)
        tails.append((hard_e, peak, total))
    e = es[0] if count == 1 else jnp.concatenate(es, axis=1)
    sums = dot(dt_ref[...], e, precision=lax.Precision.HIGHEST)
    for k, (hard_e, peak, total) in enumerate(tails):
        at = sum_refs[k] if k < evens else sum_refs[-1].at[k - evens]
        at[:features] = sums[:, k * rows : (k + 1) * rows] + rows_ref[k] * hard_e
        at[features:] = jnp.concatenate([peak, total, jnp.zeros((SLACK - 2, rows), f32)], axis=0)


def merge(terms):
    size = terms[0].shape[0] - SLACK
    peaks = [t[size : size + 1] for t in terms]
    peak = functools.reduce(jnp.maximum, peaks)
    scales = [jnp.exp(p - peak) for p in peaks]
    sums = functools.reduce(jnp.add, [t[:size] * s for t, s in zip(terms, scales)])
    total = functools.reduce(
        jnp.add, [t[size + 1 : size + 2] * s for t, s in zip(terms, scales)]
    )
    return sums, peak, total


def merge_body(places, *refs):
    out_ref = refs[-1]
    sums, peak, total = merge([r[...] if k is None else r[k] for r, k in zip(refs, places)])
    size = sums.shape[0]
    out_ref[:size] = sums
    out_ref[size:] = jnp.concatenate(
        [peak, total, jnp.zeros((SLACK - 2, peak.shape[1]), f32)], axis=0
    )


def last_body(d_ref, e_ref, *refs):
    dq_ref, loss_ref = refs[-2:]
    sums, peak, total = merge([ref[...] for ref in refs[:-2]])
    dq_ref[...] = ((sums / total).T - d_ref[...]) / logit_divisor
    log_total = peak + jnp.log(total)
    loss_ref[...] = (log_total - e_ref[0, 4:5]).reshape(loss_ref.shape)


def stats_body(places, *refs):
    out_ref = refs[-1]
    for r, (i, k) in enumerate(places):
        out_ref[0, r : r + 1] = refs[i][k, 2:3]
        out_ref[1, r : r + 1] = refs[i][k, 3:4]


def stats_merge_body(masks, own_ref, *refs):
    out_ref = refs[-1]
    n = own_ref.shape[1]
    peaks, totals = [own_ref[0]], [own_ref[1]]
    for ref, mask in zip(refs, masks):
        for values, into in ((ref[0], peaks), (ref[1], totals)):
            into.append(
                jnp.concatenate([values[r ^ mask : (r ^ mask) + 1] for r in range(n)], axis=0)
            )
    peak = functools.reduce(jnp.maximum, peaks)
    out_ref[0] = peak
    out_ref[1] = functools.reduce(
        jnp.add, [t * jnp.exp(p - peak) for p, t in zip(peaks, totals)]
    )


def gradient_body(x_places, e_places, group, *refs):
    n = len(x_places)
    tot_ref = refs[0]
    dd_ref, pool_ref, scaled_ref, local_ref = refs[-4:]
    rows, features = dd_ref.shape
    lanes = local_ref.shape[-1]

    @pl.when(pl.program_id(0) == 0)
    def _():
        own = lax.broadcasted_iota(jnp.int32, (rows, rows), 0) == lax.broadcasted_iota(
            jnp.int32, (rows, rows), 1
        )
        total = jnp.zeros((features, rows), f32)
        for g in range(n // group):
            xs, es, hards = [], [], []
            for r in range(g * group, (g + 1) * group):
                i, k = x_places[r]
                xs.append(refs[i][:features] if k is None else refs[i][k, :features])
                i, k = e_places[r]
                scale = jnp.exp(refs[i][k, rows + 2 : rows + 3] - tot_ref[0, r : r + 1])
                scale = scale / tot_ref[1, r : r + 1]
                e = refs[i][k, :rows] * scale
                es.append(e if r else jnp.where(own, e - 1.0, e))
                hards.append(refs[i][k, rows : rows + 1] * scale)
                chosen = jnp.broadcast_to(refs[i][k, rows + 1 : rows + 2], (lanes, rows))
                first = (r - g * group) * rows
                local_ref[g, first : first + rows] = chosen.T.astype(jnp.int32)
            x = jnp.concatenate(xs, axis=1)
            chance = jnp.concatenate(es, axis=1)
            high, low = split2(x)
            c_high, c_low = split2(chance)
            both = dot(jnp.concatenate([high, low], axis=0), c_high, ((1,), (1,)))
            total = total + both[:features] + both[features:]
            total = total + dot(high, c_low, ((1,), (1,)))
            high, low = split2(x * (jnp.concatenate(hards, axis=1) / logit_divisor))
            scaled_ref[g, :features] = high
            scaled_ref[g, features:] = low
        dd_ref[...] = total.T / logit_divisor

    width = pool_ref.shape[1]
    first = pl.program_id(0) * width
    acc = jnp.zeros((2 * features, width), f32)
    for g in range(n // group):
        local = local_ref[g]
        column = first + lax.broadcasted_iota(jnp.int32, local.shape, 1)
        marks = jnp.concatenate(
            [
                jnp.where(local == column + t * lanes, 1.0, 0.0).astype(bf16)
                for t in range(width // lanes)
            ],
            axis=1,
        )
        acc = acc + dot(scaled_ref[g], marks)
    pool_ref[...] = acc[:features] + acc[features:]


def per_device(question_matrix, document_matrix, pool, hard_owner, hard_local):
    n, depth = lax.axis_size("blk"), lax.axis_size("dim")
    rows, features = question_matrix.shape
    columns = pool.shape[1]
    me = lax.axis_index("blk")
    smem = pl.BlockSpec(memory_space=pltpu.SMEM)
    vmem = pl.BlockSpec(memory_space=pltpu.VMEM)
    block = shape(features + SLACK, rows)
    line = Line()

    def full(*dims):
        return pl.BlockSpec(dims, lambda i: (0,) * len(dims))

    def send(x, mask):
        return lax.ppermute(x, "blk", [(i, i ^ mask) for i in range(n)])

    far = n // 4
    x, x_arrays, x_place = {}, [], {}

    def keep(array, *blocks):
        for k, r in enumerate(blocks):
            x[r] = array
            x_place[r] = (len(x_arrays), k if array.ndim == 3 else None)
        x_arrays.append(array)

    def pass_on(array):
        return line(lambda a, out: out.__setitem__(..., a[...]), block, "relay", [array], 0.05)

    def relay(r):
        x_arrays[x_place[r][0]] = x[r] = pass_on(x[r])

    def forward(k):
        relay(4 * k)
        if k % 2 == 0 and k + 1 < far:
            keep(send(x[4 * k], 4), 4 * k + 4)
        keep(send(x[4 * k], 2), 4 * k + 2)

    def share(*blocks):
        for r in blocks:
            keep(send(x[r], 1), r + 1)

    def share_all(*blocks):
        out = shape(len(blocks), features + SLACK, rows)
        held = line(relay_body, out, "relay", [x[r] for r in blocks], 0.05)
        keep(send(held, 1), *[r + 1 for r in blocks])

    weights, sums, e_place = [], {}, {}
    waiting, stage = [], {}

    def score(blocks):
        k = len(blocks)
        used = sorted({x_place[r][0] for r in blocks})
        part, found = line(
            functools.partial(
                score_body, [(used.index(x_place[r][0]), x_place[r][1]) for r in blocks]
            ),
            (shape(k, rows + SLACK, rows), shape(k, features, rows)),
            "score",
            [me.reshape(1), document_matrix, pool] + [x_arrays[i] for i in used],
            0.9 * k,
            [smem] + [vmem] * (2 + len(used)),
        )
        got = [
            lax.ppermute(part, "dim", [(i, (i + s) % depth) for i in range(depth)])
            for s in range(1, depth)
        ]
        waiting.append((blocks, part, found, got))

    def softmax():
        blocks, part, found, got = waiting.pop(0)
        k = len(blocks)
        odds = [r for r in blocks if r % 2]
        evens = k - len(odds)
        stacked = len(odds) > 2
        e, *out = line(
            functools.partial(softmax_body, evens if stacked else k, len(got)),
            [shape(k, rows + SLACK, rows)]
            + [block] * (evens if stacked else k)
            + [shape(len(odds), features + SLACK, rows)] * stacked,
            "softmax",
            [dt, found, part, *got],
            0.25 * k,
        )
        for i, r in enumerate(blocks):
            e_place[r] = (len(weights), i)
        weights.append(e)
        for r, array in zip(blocks, out[:evens]):
            sums[r] = (array, None)
        shared = send(out[-1], 1) if stacked else None
        for i, r in enumerate(odds):
            sums[r] = (shared, i) if stacked else (send(out[evens + i], 1), None)

    over_x, home = {}, []

    def add(*terms):
        arrays = [array for array, k in terms]
        places = [k for array, k in terms]
        return line(functools.partial(merge_body, places), block, "merge", arrays, 0.05)

    def pair(*blocks):
        for r in blocks:
            sums[r] = (add(sums[r], sums[r + 1]), None)

    def beside(k):
        over_x[k] = send(sums[4 * k + 2][0], 2)

    def inward(k):
        whole = add(sums[4 * k], (over_x[k], None))
        home.append(send(whole, 4 * k) if k else whole)

    packed = line(
        functools.partial(pack_body, columns),
        block,
        "pack",
        [question_matrix, hard_owner.T, hard_local.T],
        1.8,
        [pl.BlockSpec(memory_space=pltpu.HBM)] * 3,
        limit=62,
        scratch_shapes=[
            pltpu.VMEM(question_matrix.shape, f32),
            pltpu.VMEM(hard_owner.shape[::-1], jnp.int32),
            pltpu.VMEM(hard_local.shape[::-1], jnp.int32),
            pltpu.SemaphoreType.DMA((3,)),
        ],
    )
    keep(packed, 0)
    for k in [2, 1] + [k for k in range(4, far) if k % 2 == 0]:
        keep(send(packed, 4 * k), 4 * k)
    keep(send(packed, 2), 2)
    keep(send(packed, 1), 1)
    dt = line(flip_body, shape(features, rows), "flip", [document_matrix], 0.1)
    score([0, 1])
    forward(2)
    forward(1)
    relay(2)
    share_all(2, 4, 8)
    score([2, 4, 8])
    softmax()
    relay(10)
    forward(3)
    score([3, 5, 9])
    relay(6)
    share(10, 6)
    softmax()
    score([10, 6, 11, 7])
    relay(14)
    share(12, 14)
    softmax()
    for k in range(3, far):
        if k + 1 < far:
            forward(k + 1)
        score([4 * k, 4 * k + 2, 4 * k + 1, 4 * k + 3])
        if k + 1 < far:
            relay(4 * k + 6)
            share(4 * k + 4, 4 * k + 6)
        if k == 3:
            pair(0, 2, 4, 8)
        softmax()
        if k == 3:
            pair(10)
            beside(2)
            pair(6)
            beside(1)
        else:
            pair(4 * k - 2, 4 * k - 4)
            beside(k - 1)
    softmax()
    over_x[2] = pass_on(over_x[2])

    totals = line(
        functools.partial(stats_body, [e_place[r] for r in range(n)]),
        shape(2, n, rows),
        "stats",
        weights,
        0.05,
        [
            pl.BlockSpec((e.shape[0], SLACK, rows), lambda i: (0, rows // SLACK, 0))
            for e in weights
        ],
        grid=(1,),
        out_specs=full(2, n, rows),
    )
    masks = [1] + [4 << i for i in reversed(range(far.bit_length() - 1))] + [2]
    for mask in masks:
        there = send(totals, mask)
        if mask == 2:
            pair(4 * far - 4)
            inward(2)
            inward(1)
        totals = line(
            functools.partial(stats_merge_body, [mask]),
            shape(2, n, rows),
            "stats_merge",
            [totals, there],
            0.05,
        )
        if mask == 2 * far:
            over_x[1] = pass_on(over_x[1])
        if mask == 1:
            pair(4 * far - 2)
            beside(far - 1)
    sums[2] = (pass_on(sums[2][0]), None)
    beside(0)
    for k in range(3, far):
        inward(k)

    group = 4
    width = 512
    e_at = 1 + len(x_arrays)
    document_derivative, grad_pool = line(
        functools.partial(
            gradient_body,
            [(x_place[r][0] + 1, x_place[r][1]) for r in range(n)],
            [(e_at + e_place[r][0], e_place[r][1]) for r in range(n)],
            group,
        ),
        (shape(rows, features), shape(features, columns)),
        "gradient",
        [totals, *x_arrays, *weights],
        11.0,
        limit=48,
        grid=(columns // width,),
        out_specs=(full(rows, features), pl.BlockSpec((features, width), lambda i: (0, i))),
        scratch_shapes=[
            pltpu.VMEM((n // group, 2 * features, group * rows), bf16),
            pltpu.VMEM((n // group, group * rows, 128), jnp.int32),
        ],
    )

    line.last = totals
    inward(0)
    arrays = home
    question_derivative, loss = line(
        last_body,
        (shape(rows, features), shape(rows)),
        "finish",
        [document_matrix, weights[0], *arrays],
        0.8,
        [full(rows, features)]
        + [pl.BlockSpec((1, SLACK, rows), lambda i: (0, rows // SLACK, 0))]
        + [full(*a.shape) for a in arrays],
        grid=(1,),
        out_specs=(full(rows, features), full(rows)),
    )
    return loss, question_derivative, document_derivative, grad_pool


def solution(mesh):
    placed = (P("blk", "dim"), P("blk", "dim"), P("dim", "blk"), P("blk", None), P("blk", None))
    return jax.shard_map(
        per_device,
        mesh=mesh,
        in_specs=placed,
        out_specs=(P("blk"), P("blk", "dim"), P("blk", "dim"), P("dim", "blk")),
        check_vma=False,
    )
```

```python
import functools

import jax
import jax.numpy as jnp
from jax import lax
from jax.experimental import pallas as pl
from jax.experimental.pallas import tpu as pltpu
from jax.sharding import PartitionSpec as P

logit_divisor = 0.05
LOWEST = -3.0e38
COST = 3.7e6
SLACK = 8

f32 = jnp.float32
bf16 = jnp.bfloat16


def split2(x):
    high = x.astype(bf16)
    return high, (x - high.astype(f32)).astype(bf16)


def dot(a, b, contract=((1,), (0,)), precision=None):
    return lax.dot_general(
        a, b, (contract, ((), ())), precision=precision, preferred_element_type=f32
    )


class Line:
    def __init__(self):
        self.last = None

    def __call__(self, body, out_shape, name, arrays, us, in_specs=None, limit=16, **kw):
        count = len(arrays)
        if in_specs is None:
            in_specs = [pl.BlockSpec(memory_space=pltpu.VMEM)] * count
        if self.last is not None:
            in_specs = list(in_specs) + [pl.BlockSpec(memory_space=pl.ANY)]
            arrays = list(arrays) + [self.last]

        def kernel(*refs):
            body(*refs[:count], *refs[len(arrays) :])

        out = pl.pallas_call(
            kernel,
            out_shape=out_shape,
            name=name,
            in_specs=in_specs,
            cost_estimate=pl.CostEstimate(
                flops=0, bytes_accessed=int(us * COST), transcendentals=0
            ),
            compiler_params=pltpu.CompilerParams(vmem_limit_bytes=limit << 20),
            **kw,
        )(*arrays)
        self.last = min(jax.tree.leaves(out), key=lambda array: array.size)
        return out


def shape(*dims, dtype=f32):
    return jax.ShapeDtypeStruct(dims, dtype)


def pack_body(columns, q_hbm, owner_hbm, local_hbm, x_ref, q_ref, owner_ref, local_ref, sems):
    pairs = ((q_hbm, q_ref), (owner_hbm, owner_ref), (local_hbm, local_ref))
    copies = [pltpu.make_async_copy(a, b, sems.at[i]) for i, (a, b) in enumerate(pairs)]
    for copy in copies:
        copy.start()
    for copy in copies:
        copy.wait()
    features = q_ref.shape[1]
    x_ref[:features, :] = q_ref[...].T
    x_ref[features:, :] = (owner_ref[...] * columns + local_ref[...]).astype(f32)


def settle_body(out_ref):
    out_ref[...] = jnp.zeros_like(out_ref)


def relay_body(*refs):
    for k, ref in enumerate(refs[:-1]):
        refs[-1][k] = ref[...]


def flip_body(d_ref, dt_ref):
    dt_ref[...] = d_ref[...].T


def score_body(places, me_ref, d_ref, pool_ref, *refs):
    part_ref, rows_ref, token_ref = refs[-3:]
    token_ref[...] = jnp.zeros_like(token_ref)
    rows, features = d_ref.shape
    columns = pool_ref.shape[1]
    tile = 128
    blocks = [refs[a][...] if k is None else refs[a][k] for a, k in places]
    for k, block in enumerate(blocks):
        x = block[:features]
        named = block[features:].astype(jnp.int32) - me_ref[0] * columns
        here = (named >= 0) & (named < columns)
        local = jnp.sum(jnp.where(here, named, 0), axis=0, keepdims=True)
        owned = jnp.any(here, axis=0, keepdims=True)
        lane = jnp.broadcast_to(local % tile, (features, rows))
        found = jnp.zeros((features, rows), f32)
        for t in range(columns // tile):
            picked = jnp.take_along_axis(
                pool_ref[:, t * tile : (t + 1) * tile], lane, axis=1, mode="promise_in_bounds"
            )
            found = jnp.where(local // tile == t, picked, found)
        rows_ref[k] = found
        hard = jnp.sum(x * found, axis=0, keepdims=True)
        chosen = jnp.where(owned, local, -1).astype(f32)
        part_ref[k, rows:] = jnp.concatenate(
            [hard, chosen, jnp.zeros((SLACK - 2, rows), f32)], axis=0
        )
    x = [block[:features] for block in blocks]
    x = x[0] if len(x) == 1 else jnp.concatenate(x, axis=1)
    scores = dot(d_ref[...], x, precision=lax.Precision.HIGHEST)
    for k in range(len(blocks)):
        part_ref[k, :rows] = scores[:, k * rows : (k + 1) * rows]


def softmax_body(evens, others, dt_ref, rows_ref, part_ref, *refs):
    got, (e_ref, *sum_refs) = refs[:others], refs[others:]
    features, rows = dt_ref.shape
    count = part_ref.shape[0]
    own = lax.broadcasted_iota(jnp.int32, (rows, rows), 0) == lax.broadcasted_iota(
        jnp.int32, (rows, rows), 1
    )
    tails, es = [], []
    for k in range(count):
        whole = part_ref[k]
        chosen = whole[rows + 1 : rows + 2]
        for r in got:
            whole = whole + r[k]
        scores = whole[:rows] / logit_divisor
        hard = jnp.where(chosen >= 0, whole[rows : rows + 1] / logit_divisor, LOWEST)
        peak = jnp.maximum(jnp.max(scores, axis=0, keepdims=True), hard)
        e = jnp.exp(scores - peak)
        hard_e = jnp.where(chosen >= 0, jnp.exp(hard - peak), 0.0)
        total = jnp.sum(e, axis=0, keepdims=True) + hard_e
        positive = jnp.sum(jnp.where(own, scores, 0.0), axis=0, keepdims=True)
        e_ref[k, :rows] = e
        e_ref[k, rows:] = jnp.concatenate(
            [hard_e, chosen, peak, total, positive, jnp.zeros((SLACK - 5, rows), f32)], axis=0
        )
        es.append(e)
        tails.append((hard_e, peak, total))
    e = es[0] if count == 1 else jnp.concatenate(es, axis=1)
    sums = dot(dt_ref[...], e, precision=lax.Precision.HIGHEST)
    for k, (hard_e, peak, total) in enumerate(tails):
        at = sum_refs[k] if k < evens else sum_refs[-1].at[k - evens]
        at[:features] = sums[:, k * rows : (k + 1) * rows] + rows_ref[k] * hard_e
        at[features:] = jnp.concatenate([peak, total, jnp.zeros((SLACK - 2, rows), f32)], axis=0)


def merge(terms):
    size = terms[0].shape[0] - SLACK
    peaks = [t[size : size + 1] for t in terms]
    peak = functools.reduce(jnp.maximum, peaks)
    scales = [jnp.exp(p - peak) for p in peaks]
    sums = functools.reduce(jnp.add, [t[:size] * s for t, s in zip(terms, scales)])
    total = functools.reduce(
        jnp.add, [t[size + 1 : size + 2] * s for t, s in zip(terms, scales)]
    )
    return sums, peak, total


def merge_body(places, *refs):
    out_ref = refs[-1]
    sums, peak, total = merge([r[...] if k is None else r[k] for r, k in zip(refs, places)])
    size = sums.shape[0]
    out_ref[:size] = sums
    out_ref[size:] = jnp.concatenate(
        [peak, total, jnp.zeros((SLACK - 2, peak.shape[1]), f32)], axis=0
    )


def merge_all_body(places, *refs):
    out_ref = refs[-1]
    size = out_ref.shape[1] - SLACK
    for slot, terms in enumerate(places):
        terms = [refs[i][...] if k is None else refs[i][k] for i, k in terms]
        if len(terms) == 1:
            out_ref[slot] = terms[0]
        else:
            sums, peak, total = merge(terms)
            out_ref[slot, :size] = sums
            out_ref[slot, size:] = jnp.concatenate(
                [peak, total, jnp.zeros((SLACK - 2, peak.shape[1]), f32)], axis=0
            )


def last_body(d_ref, e_ref, *refs):
    dq_ref, loss_ref = refs[-2:]
    sums, peak, total = merge([ref[...] for ref in refs[:-2]])
    dq_ref[...] = ((sums / total).T - d_ref[...]) / logit_divisor
    log_total = peak + jnp.log(total)
    loss_ref[...] = (log_total - e_ref[0, 4:5]).reshape(loss_ref.shape)


def stats_body(places, *refs):
    out_ref = refs[-1]
    for r, (i, k) in enumerate(places):
        out_ref[0, r : r + 1] = refs[i][k, 2:3]
        out_ref[1, r : r + 1] = refs[i][k, 3:4]


def stats_merge_body(masks, own_ref, *refs):
    out_ref = refs[-1]
    n = own_ref.shape[1]
    peaks, totals = [own_ref[0]], [own_ref[1]]
    for ref, mask in zip(refs, masks):
        for values, into in ((ref[0], peaks), (ref[1], totals)):
            into.append(
                jnp.concatenate([values[r ^ mask : (r ^ mask) + 1] for r in range(n)], axis=0)
            )
    peak = functools.reduce(jnp.maximum, peaks)
    out_ref[0] = peak
    out_ref[1] = functools.reduce(
        jnp.add, [t * jnp.exp(p - peak) for p, t in zip(peaks, totals)]
    )


def gradient_body(x_places, e_places, group, *refs):
    n = len(x_places)
    tot_ref = refs[0]
    dd_ref, pool_ref, scaled_ref, local_ref = refs[-4:]
    rows, features = dd_ref.shape
    lanes = local_ref.shape[-1]

    @pl.when(pl.program_id(0) == 0)
    def _():
        own = lax.broadcasted_iota(jnp.int32, (rows, rows), 0) == lax.broadcasted_iota(
            jnp.int32, (rows, rows), 1
        )
        total = jnp.zeros((features, rows), f32)
        for g in range(n // group):
            xs, es, hards = [], [], []
            for r in range(g * group, (g + 1) * group):
                i, k = x_places[r]
                xs.append(refs[i][:features] if k is None else refs[i][k, :features])
                i, k = e_places[r]
                scale = jnp.exp(refs[i][k, rows + 2 : rows + 3] - tot_ref[0, r : r + 1])
                scale = scale / tot_ref[1, r : r + 1]
                e = refs[i][k, :rows] * scale
                es.append(e if r else jnp.where(own, e - 1.0, e))
                hards.append(refs[i][k, rows : rows + 1] * scale)
                chosen = jnp.broadcast_to(refs[i][k, rows + 1 : rows + 2], (lanes, rows))
                first = (r - g * group) * rows
                local_ref[g, first : first + rows] = chosen.T.astype(jnp.int32)
            x = jnp.concatenate(xs, axis=1)
            chance = jnp.concatenate(es, axis=1)
            high, low = split2(x)
            c_high, c_low = split2(chance)
            both = dot(jnp.concatenate([high, low], axis=0), c_high, ((1,), (1,)))
            total = total + both[:features] + both[features:]
            total = total + dot(high, c_low, ((1,), (1,)))
            high, low = split2(x * (jnp.concatenate(hards, axis=1) / logit_divisor))
            scaled_ref[g, :features] = high
            scaled_ref[g, features:] = low
        dd_ref[...] = total.T / logit_divisor

    width = pool_ref.shape[1]
    first = pl.program_id(0) * width
    acc = jnp.zeros((2 * features, width), f32)
    for g in range(n // group):
        local = local_ref[g]
        column = first + lax.broadcasted_iota(jnp.int32, local.shape, 1)
        marks = jnp.concatenate(
            [
                jnp.where(local == column + t * lanes, 1.0, 0.0).astype(bf16)
                for t in range(width // lanes)
            ],
            axis=1,
        )
        acc = acc + dot(scaled_ref[g], marks)
    pool_ref[...] = acc[:features] + acc[features:]


def per_device(question_matrix, document_matrix, pool, hard_owner, hard_local):
    n, depth = lax.axis_size("blk"), lax.axis_size("dim")
    rows, features = question_matrix.shape
    columns = pool.shape[1]
    me = lax.axis_index("blk")
    smem = pl.BlockSpec(memory_space=pltpu.SMEM)
    vmem = pl.BlockSpec(memory_space=pltpu.VMEM)
    block = shape(features + SLACK, rows)
    line = Line()

    def full(*dims):
        return pl.BlockSpec(dims, lambda i: (0,) * len(dims))

    def send(x, mask):
        return lax.ppermute(x, "blk", [(i, i ^ mask) for i in range(n)])

    far = n // 4
    x, x_arrays, x_place = {}, [], {}

    def keep(array, *blocks):
        for k, r in enumerate(blocks):
            x[r] = array
            x_place[r] = (len(x_arrays), k if array.ndim == 3 else None)
        x_arrays.append(array)

    def pass_on(array):
        return line(lambda a, out: out.__setitem__(..., a[...]), block, "relay", [array], 0.05)

    def relay(r):
        x_arrays[x_place[r][0]] = x[r] = pass_on(x[r])

    def forward(k):
        relay(4 * k)
        if k % 2 == 0 and k + 1 < far:
            keep(send(x[4 * k], 4), 4 * k + 4)
        keep(send(x[4 * k], 2), 4 * k + 2)

    def share(*blocks):
        for r in blocks:
            keep(send(x[r], 1), r + 1)

    def share_all(*blocks):
        out = shape(len(blocks), features + SLACK, rows)
        held = line(relay_body, out, "relay", [x[r] for r in blocks], 0.05)
        keep(send(held, 1), *[r + 1 for r in blocks])

    weights, sums, e_place = [], {}, {}
    waiting, stage = [], {}

    def score(blocks, limit=16):
        k = len(blocks)
        used = sorted({x_place[r][0] for r in blocks})
        part, found, token = line(
            functools.partial(
                score_body, [(used.index(x_place[r][0]), x_place[r][1]) for r in blocks]
            ),
            (shape(k, rows + SLACK, rows), shape(k, features, rows), shape(SLACK, rows)),
            "score",
            [me.reshape(1), document_matrix, pool] + [x_arrays[i] for i in used],
            0.9 * k,
            [smem] + [vmem] * (2 + len(used)),
            limit=limit,
        )
        got = [
            lax.ppermute(part, "dim", [(i, (i + s) % depth) for i in range(depth)])
            for s in range(1, depth)
        ]
        waiting.append((blocks, part, found, got))

    def softmax():
        blocks, part, found, got = waiting.pop(0)
        k = len(blocks)
        odds = [r for r in blocks if r % 2]
        evens = k - len(odds)
        stacked = len(odds) > 2
        e, *out = line(
            functools.partial(softmax_body, evens if stacked else k, len(got)),
            [shape(k, rows + SLACK, rows)]
            + [block] * (evens if stacked else k)
            + [shape(len(odds), features + SLACK, rows)] * stacked,
            "softmax",
            [dt, found, part, *got],
            0.25 * k,
        )
        for i, r in enumerate(blocks):
            e_place[r] = (len(weights), i)
        weights.append(e)
        for r, array in zip(blocks, out[:evens]):
            sums[r] = (array, None)
        shared = send(out[-1], 1) if stacked else None
        for i, r in enumerate(odds):
            sums[r] = (shared, i) if stacked else (send(out[evens + i], 1), None)

    over_x, home = {}, []

    def add(*terms):
        arrays = [array for array, k in terms]
        places = [k for array, k in terms]
        return line(functools.partial(merge_body, places), block, "merge", arrays, 0.05)

    def pair(*blocks):
        for r in blocks:
            sums[r] = (add(sums[r], sums[r + 1]), None)

    def beside(k):
        over_x[k] = (send(sums[4 * k + 2][0], 2), None)

    def beside_all(*blocks):
        arrays, places = [], []
        for terms in blocks:
            places.append([(len(arrays) + i, sums[r][1]) for i, r in enumerate(terms)])
            arrays += [sums[r][0] for r in terms]
        out = shape(len(blocks), features + SLACK, rows)
        held = line(functools.partial(merge_all_body, places), out, "merge", arrays, 0.1)
        shared = send(held, 2)
        for i, terms in enumerate(blocks):
            over_x[terms[0] // 4] = (shared, i)

    def inward(k):
        whole = add(sums[4 * k], over_x[k])
        home.append(send(whole, 4 * k) if k else whole)

    packed = line(
        functools.partial(pack_body, columns),
        block,
        "pack",
        [question_matrix, hard_owner.T, hard_local.T],
        1.8,
        [pl.BlockSpec(memory_space=pltpu.HBM)] * 3,
        limit=62,
        scratch_shapes=[
            pltpu.VMEM(question_matrix.shape, f32),
            pltpu.VMEM(hard_owner.shape[::-1], jnp.int32),
            pltpu.VMEM(hard_local.shape[::-1], jnp.int32),
            pltpu.SemaphoreType.DMA((3,)),
        ],
    )
    keep(packed, 0)
    for k in [2, 1] + [k for k in range(4, far) if k % 2 == 0]:
        keep(send(packed, 4 * k), 4 * k)
    keep(send(packed, 2), 2)
    keep(send(packed, 1), 1)
    dt = line(flip_body, shape(features, rows), "flip", [document_matrix], 0.1, limit=62)
    score([0, 1], limit=60)
    line(settle_body, shape(SLACK, rows), "settle", [], 0.05)
    forward(2)
    forward(1)
    relay(2)
    share_all(2, 4, 8)
    score([2, 4, 8])
    softmax()
    relay(10)
    forward(3)
    score([3, 5, 9])
    relay(6)
    share(10, 6)
    softmax()
    score([10, 6, 11, 7])
    relay(14)
    share(12, 14)
    softmax()
    for k in range(3, far):
        if k + 1 < far:
            forward(k + 1)
        score([4 * k, 4 * k + 2, 4 * k + 1, 4 * k + 3])
        if k + 1 < far:
            relay(4 * k + 6)
            share(4 * k + 4, 4 * k + 6)
        if k == 3:
            pair(0, 2, 4, 8)
        softmax()
        if k == 3:
            pair(10)
            beside(2)
            pair(6)
            beside(1)
        else:
            pair(4 * k - 2, 4 * k - 4)
            beside(k - 1)
    softmax()
    over_x[2] = (pass_on(over_x[2][0]), None)

    totals = line(
        functools.partial(stats_body, [e_place[r] for r in range(n)]),
        shape(2, n, rows),
        "stats",
        weights,
        0.05,
        [
            pl.BlockSpec((e.shape[0], SLACK, rows), lambda i: (0, rows // SLACK, 0))
            for e in weights
        ],
        grid=(1,),
        out_specs=full(2, n, rows),
    )
    masks = [1] + [4 << i for i in reversed(range(far.bit_length() - 1))] + [2]
    for mask in masks:
        there = send(totals, mask)
        if mask == 2:
            pair(4 * far - 4)
            inward(2)
            inward(1)
        totals = line(
            functools.partial(stats_merge_body, [mask]),
            shape(2, n, rows),
            "stats_merge",
            [totals, there],
            0.05,
        )
        if mask == 2 * far:
            over_x[1] = (pass_on(over_x[1][0]), None)
        if mask == 1:
            pair(4 * far - 2)
            beside(far - 1)
    sums[2] = (pass_on(sums[2][0]), None)
    beside(0)
    for k in range(3, far):
        inward(k)

    group = 4
    width = 512
    e_at = 1 + len(x_arrays)
    document_derivative, grad_pool = line(
        functools.partial(
            gradient_body,
            [(x_place[r][0] + 1, x_place[r][1]) for r in range(n)],
            [(e_at + e_place[r][0], e_place[r][1]) for r in range(n)],
            group,
        ),
        (shape(rows, features), shape(features, columns)),
        "gradient",
        [totals, *x_arrays, *weights],
        11.0,
        limit=48,
        grid=(columns // width,),
        out_specs=(full(rows, features), pl.BlockSpec((features, width), lambda i: (0, i))),
        scratch_shapes=[
            pltpu.VMEM((n // group, 2 * features, group * rows), bf16),
            pltpu.VMEM((n // group, group * rows, 128), jnp.int32),
        ],
    )

    line.last = totals
    inward(0)
    arrays = home
    question_derivative, loss = line(
        last_body,
        (shape(rows, features), shape(rows)),
        "finish",
        [document_matrix, weights[0], *arrays],
        0.8,
        [full(rows, features)]
        + [pl.BlockSpec((1, SLACK, rows), lambda i: (0, rows // SLACK, 0))]
        + [full(*a.shape) for a in arrays],
        grid=(1,),
        out_specs=(full(rows, features), full(rows)),
    )
    return loss, question_derivative, document_derivative, grad_pool


def solution(mesh):
    placed = (P("blk", "dim"), P("blk", "dim"), P("dim", "blk"), P("blk", None), P("blk", None))
    return jax.shard_map(
        per_device,
        mesh=mesh,
        in_specs=placed,
        out_specs=(P("blk"), P("blk", "dim"), P("blk", "dim"), P("dim", "blk")),
        check_vma=False,
    )
```

```python
import functools

import jax
import jax.numpy as jnp
from jax import lax
from jax.experimental import pallas as pl
from jax.experimental.pallas import tpu as pltpu
from jax.sharding import PartitionSpec as P

logit_divisor = 0.05
LOWEST = -3.0e38
COST = 3.7e6
SLACK = 8

f32 = jnp.float32
bf16 = jnp.bfloat16


def split2(x):
    high = x.astype(bf16)
    return high, (x - high.astype(f32)).astype(bf16)


def dot(a, b, contract=((1,), (0,)), precision=None):
    return lax.dot_general(
        a, b, (contract, ((), ())), precision=precision, preferred_element_type=f32
    )


class Line:
    def __init__(self):
        self.last = None

    def __call__(self, body, out_shape, name, arrays, us, in_specs=None, limit=16, **kw):
        count = len(arrays)
        if in_specs is None:
            in_specs = [pl.BlockSpec(memory_space=pltpu.VMEM)] * count
        if self.last is not None:
            in_specs = list(in_specs) + [pl.BlockSpec(memory_space=pl.ANY)]
            arrays = list(arrays) + [self.last]

        def kernel(*refs):
            body(*refs[:count], *refs[len(arrays) :])

        out = pl.pallas_call(
            kernel,
            out_shape=out_shape,
            name=name,
            in_specs=in_specs,
            cost_estimate=pl.CostEstimate(
                flops=0, bytes_accessed=int(us * COST), transcendentals=0
            ),
            compiler_params=pltpu.CompilerParams(vmem_limit_bytes=limit << 20),
            **kw,
        )(*arrays)
        self.last = out[-1] if isinstance(out, (list, tuple)) else out
        return out


def shape(*dims, dtype=f32):
    return jax.ShapeDtypeStruct(dims, dtype)


def pack_body(columns, q_hbm, owner_hbm, local_hbm, x_ref, q_ref, owner_ref, local_ref, sems):
    pairs = ((q_hbm, q_ref), (owner_hbm, owner_ref), (local_hbm, local_ref))
    copies = [pltpu.make_async_copy(a, b, sems.at[i]) for i, (a, b) in enumerate(pairs)]
    for copy in copies:
        copy.start()
    for copy in copies:
        copy.wait()
    features = q_ref.shape[1]
    x_ref[:features, :] = q_ref[...].T
    x_ref[features:, :] = (owner_ref[...] * columns + local_ref[...]).astype(f32)


def relay_body(*refs):
    for k, ref in enumerate(refs[:-1]):
        refs[-1][k] = ref[...]


def flip_body(d_ref, dt_ref):
    dt_ref[...] = d_ref[...].T


def score_body(places, me_ref, d_ref, pool_ref, *refs):
    part_ref, rows_ref = refs[-2:]
    rows, features = d_ref.shape
    columns = pool_ref.shape[1]
    tile = 128
    blocks = [refs[a][...] if k is None else refs[a][k] for a, k in places]
    for k, block in enumerate(blocks):
        x = block[:features]
        named = block[features:].astype(jnp.int32) - me_ref[0] * columns
        here = (named >= 0) & (named < columns)
        local = jnp.sum(jnp.where(here, named, 0), axis=0, keepdims=True)
        owned = jnp.any(here, axis=0, keepdims=True)
        lane = jnp.broadcast_to(local % tile, (features, rows))
        found = jnp.zeros((features, rows), f32)
        for t in range(columns // tile):
            picked = jnp.take_along_axis(
                pool_ref[:, t * tile : (t + 1) * tile], lane, axis=1, mode="promise_in_bounds"
            )
            found = jnp.where(local // tile == t, picked, found)
        rows_ref[k] = found
        hard = jnp.sum(x * found, axis=0, keepdims=True)
        chosen = jnp.where(owned, local, -1).astype(f32)
        part_ref[k, rows:] = jnp.concatenate(
            [hard, chosen, jnp.zeros((SLACK - 2, rows), f32)], axis=0
        )
    x = [block[:features] for block in blocks]
    x = x[0] if len(x) == 1 else jnp.concatenate(x, axis=1)
    scores = dot(d_ref[...], x, precision=lax.Precision.HIGHEST)
    for k in range(len(blocks)):
        part_ref[k, :rows] = scores[:, k * rows : (k + 1) * rows]


def softmax_body(evens, others, dt_ref, rows_ref, part_ref, *refs):
    got, (e_ref, *sum_refs) = refs[:others], refs[others:]
    features, rows = dt_ref.shape
    count = part_ref.shape[0]
    own = lax.broadcasted_iota(jnp.int32, (rows, rows), 0) == lax.broadcasted_iota(
        jnp.int32, (rows, rows), 1
    )
    tails, es = [], []
    for k in range(count):
        whole = part_ref[k]
        chosen = whole[rows + 1 : rows + 2]
        for r in got:
            whole = whole + r[k]
        scores = whole[:rows] / logit_divisor
        hard = jnp.where(chosen >= 0, whole[rows : rows + 1] / logit_divisor, LOWEST)
        peak = jnp.maximum(jnp.max(scores, axis=0, keepdims=True), hard)
        e = jnp.exp(scores - peak)
        hard_e = jnp.where(chosen >= 0, jnp.exp(hard - peak), 0.0)
        total = jnp.sum(e, axis=0, keepdims=True) + hard_e
        positive = jnp.sum(jnp.where(own, scores, 0.0), axis=0, keepdims=True)
        e_ref[k, :rows] = e
        e_ref[k, rows:] = jnp.concatenate(
            [hard_e, chosen, peak, total, positive, jnp.zeros((SLACK - 5, rows), f32)], axis=0
        )
        es.append(e)
        tails.append((hard_e, peak, total))
    e = es[0] if count == 1 else jnp.concatenate(es, axis=1)
    sums = dot(dt_ref[...], e, precision=lax.Precision.HIGHEST)
    for k, (hard_e, peak, total) in enumerate(tails):
        at = sum_refs[k] if k < evens else sum_refs[-1].at[k - evens]
        at[:features] = sums[:, k * rows : (k + 1) * rows] + rows_ref[k] * hard_e
        at[features:] = jnp.concatenate([peak, total, jnp.zeros((SLACK - 2, rows), f32)], axis=0)


def merge(terms):
    size = terms[0].shape[0] - SLACK
    peaks = [t[size : size + 1] for t in terms]
    peak = functools.reduce(jnp.maximum, peaks)
    scales = [jnp.exp(p - peak) for p in peaks]
    sums = functools.reduce(jnp.add, [t[:size] * s for t, s in zip(terms, scales)])
    total = functools.reduce(
        jnp.add, [t[size + 1 : size + 2] * s for t, s in zip(terms, scales)]
    )
    return sums, peak, total


def merge_body(places, *refs):
    out_ref = refs[-1]
    sums, peak, total = merge([r[...] if k is None else r[k] for r, k in zip(refs, places)])
    size = sums.shape[0]
    out_ref[:size] = sums
    out_ref[size:] = jnp.concatenate(
        [peak, total, jnp.zeros((SLACK - 2, peak.shape[1]), f32)], axis=0
    )


def merge_all_body(places, *refs):
    out_ref = refs[-1]
    size = out_ref.shape[1] - SLACK
    for slot, terms in enumerate(places):
        terms = [refs[i][...] if k is None else refs[i][k] for i, k in terms]
        if len(terms) == 1:
            out_ref[slot] = terms[0]
        else:
            sums, peak, total = merge(terms)
            out_ref[slot, :size] = sums
            out_ref[slot, size:] = jnp.concatenate(
                [peak, total, jnp.zeros((SLACK - 2, peak.shape[1]), f32)], axis=0
            )


def last_body(d_ref, e_ref, *refs):
    dq_ref, loss_ref = refs[-2:]
    sums, peak, total = merge([ref[...] for ref in refs[:-2]])
    dq_ref[...] = ((sums / total).T - d_ref[...]) / logit_divisor
    log_total = peak + jnp.log(total)
    loss_ref[...] = (log_total - e_ref[0, 4:5]).reshape(loss_ref.shape)


def stats_body(places, *refs):
    out_ref = refs[-1]
    for r, (i, k) in enumerate(places):
        out_ref[0, r : r + 1] = refs[i][k, 2:3]
        out_ref[1, r : r + 1] = refs[i][k, 3:4]


def stats_merge_body(masks, own_ref, *refs):
    out_ref = refs[-1]
    n = own_ref.shape[1]
    peaks, totals = [own_ref[0]], [own_ref[1]]
    for ref, mask in zip(refs, masks):
        for values, into in ((ref[0], peaks), (ref[1], totals)):
            into.append(
                jnp.concatenate([values[r ^ mask : (r ^ mask) + 1] for r in range(n)], axis=0)
            )
    peak = functools.reduce(jnp.maximum, peaks)
    out_ref[0] = peak
    out_ref[1] = functools.reduce(
        jnp.add, [t * jnp.exp(p - peak) for p, t in zip(peaks, totals)]
    )


def gradient_body(x_places, e_places, group, *refs):
    n = len(x_places)
    tot_ref = refs[0]
    dd_ref, pool_ref, scaled_ref, local_ref = refs[-4:]
    rows, features = dd_ref.shape
    lanes = local_ref.shape[-1]

    @pl.when(pl.program_id(0) == 0)
    def _():
        own = lax.broadcasted_iota(jnp.int32, (rows, rows), 0) == lax.broadcasted_iota(
            jnp.int32, (rows, rows), 1
        )
        total = jnp.zeros((features, rows), f32)
        for g in range(n // group):
            xs, es, hards = [], [], []
            for r in range(g * group, (g + 1) * group):
                i, k = x_places[r]
                xs.append(refs[i][:features] if k is None else refs[i][k, :features])
                i, k = e_places[r]
                scale = jnp.exp(refs[i][k, rows + 2 : rows + 3] - tot_ref[0, r : r + 1])
                scale = scale / tot_ref[1, r : r + 1]
                e = refs[i][k, :rows] * scale
                es.append(e if r else jnp.where(own, e - 1.0, e))
                hards.append(refs[i][k, rows : rows + 1] * scale)
                chosen = jnp.broadcast_to(refs[i][k, rows + 1 : rows + 2], (lanes, rows))
                first = (r - g * group) * rows
                local_ref[g, first : first + rows] = chosen.T.astype(jnp.int32)
            x = jnp.concatenate(xs, axis=1)
            chance = jnp.concatenate(es, axis=1)
            high, low = split2(x)
            c_high, c_low = split2(chance)
            both = dot(jnp.concatenate([high, low], axis=0), c_high, ((1,), (1,)))
            total = total + both[:features] + both[features:]
            total = total + dot(high, c_low, ((1,), (1,)))
            high, low = split2(x * (jnp.concatenate(hards, axis=1) / logit_divisor))
            scaled_ref[g, :features] = high
            scaled_ref[g, features:] = low
        dd_ref[...] = total.T / logit_divisor

    width = pool_ref.shape[1]
    first = pl.program_id(0) * width
    acc = jnp.zeros((2 * features, width), f32)
    for g in range(n // group):
        local = local_ref[g]
        column = first + lax.broadcasted_iota(jnp.int32, local.shape, 1)
        marks = jnp.concatenate(
            [
                jnp.where(local == column + t * lanes, 1.0, 0.0).astype(bf16)
                for t in range(width // lanes)
            ],
            axis=1,
        )
        acc = acc + dot(scaled_ref[g], marks)
    pool_ref[...] = acc[:features] + acc[features:]


def per_device(question_matrix, document_matrix, pool, hard_owner, hard_local):
    n, depth = lax.axis_size("blk"), lax.axis_size("dim")
    rows, features = question_matrix.shape
    columns = pool.shape[1]
    me = lax.axis_index("blk")
    smem = pl.BlockSpec(memory_space=pltpu.SMEM)
    vmem = pl.BlockSpec(memory_space=pltpu.VMEM)
    block = shape(features + SLACK, rows)
    line = Line()

    def full(*dims):
        return pl.BlockSpec(dims, lambda i: (0,) * len(dims))

    def send(x, mask):
        return lax.ppermute(x, "blk", [(i, i ^ mask) for i in range(n)])

    far = n // 4
    x, x_arrays, x_place = {}, [], {}

    def keep(array, *blocks):
        for k, r in enumerate(blocks):
            x[r] = array
            x_place[r] = (len(x_arrays), k if array.ndim == 3 else None)
        x_arrays.append(array)

    def pass_on(array):
        return line(lambda a, out: out.__setitem__(..., a[...]), block, "relay", [array], 0.05)

    def relay(r):
        x_arrays[x_place[r][0]] = x[r] = pass_on(x[r])

    def forward(k):
        relay(4 * k)
        if k % 2 == 0 and k + 1 < far:
            keep(send(x[4 * k], 4), 4 * k + 4)
        keep(send(x[4 * k], 2), 4 * k + 2)

    def share(*blocks):
        for r in blocks:
            keep(send(x[r], 1), r + 1)

    def share_all(*blocks):
        out = shape(len(blocks), features + SLACK, rows)
        held = line(relay_body, out, "relay", [x[r] for r in blocks], 0.05)
        keep(send(held, 1), *[r + 1 for r in blocks])

    weights, sums, e_place = [], {}, {}
    waiting, stage = [], {}

    def score(blocks):
        k = len(blocks)
        used = sorted({x_place[r][0] for r in blocks})
        part, found = line(
            functools.partial(
                score_body, [(used.index(x_place[r][0]), x_place[r][1]) for r in blocks]
            ),
            (shape(k, rows + SLACK, rows), shape(k, features, rows)),
            "score",
            [me.reshape(1), document_matrix, pool] + [x_arrays[i] for i in used],
            0.9 * k,
            [smem] + [vmem] * (2 + len(used)),
        )
        got = [
            lax.ppermute(part, "dim", [(i, (i + s) % depth) for i in range(depth)])
            for s in range(1, depth)
        ]
        waiting.append((blocks, part, found, got))

    def softmax():
        blocks, part, found, got = waiting.pop(0)
        k = len(blocks)
        odds = [r for r in blocks if r % 2]
        evens = k - len(odds)
        stacked = len(odds) > 2
        e, *out = line(
            functools.partial(softmax_body, evens if stacked else k, len(got)),
            [shape(k, rows + SLACK, rows)]
            + [block] * (evens if stacked else k)
            + [shape(len(odds), features + SLACK, rows)] * stacked,
            "softmax",
            [dt, found, part, *got],
            0.25 * k,
        )
        for i, r in enumerate(blocks):
            e_place[r] = (len(weights), i)
        weights.append(e)
        for r, array in zip(blocks, out[:evens]):
            sums[r] = (array, None)
        shared = send(out[-1], 1) if stacked else None
        for i, r in enumerate(odds):
            sums[r] = (shared, i) if stacked else (send(out[evens + i], 1), None)

    over_x, home = {}, []

    def add(*terms):
        arrays = [array for array, k in terms]
        places = [k for array, k in terms]
        return line(functools.partial(merge_body, places), block, "merge", arrays, 0.05)

    def pair(*blocks):
        for r in blocks:
            sums[r] = (add(sums[r], sums[r + 1]), None)

    def beside(k):
        over_x[k] = (send(sums[4 * k + 2][0], 2), None)

    def beside_all(*blocks):
        arrays, places = [], []
        for terms in blocks:
            places.append([(len(arrays) + i, sums[r][1]) for i, r in enumerate(terms)])
            arrays += [sums[r][0] for r in terms]
        out = shape(len(blocks), features + SLACK, rows)
        held = line(functools.partial(merge_all_body, places), out, "merge", arrays, 0.1)
        shared = send(held, 2)
        for i, terms in enumerate(blocks):
            over_x[terms[0] // 4] = (shared, i)

    def inward(k):
        whole = add(sums[4 * k], over_x[k])
        home.append(send(whole, 4 * k) if k else whole)

    packed = line(
        functools.partial(pack_body, columns),
        block,
        "pack",
        [question_matrix, hard_owner.T, hard_local.T],
        1.8,
        [pl.BlockSpec(memory_space=pltpu.HBM)] * 3,
        limit=62,
        scratch_shapes=[
            pltpu.VMEM(question_matrix.shape, f32),
            pltpu.VMEM(hard_owner.shape[::-1], jnp.int32),
            pltpu.VMEM(hard_local.shape[::-1], jnp.int32),
            pltpu.SemaphoreType.DMA((3,)),
        ],
    )
    keep(packed, 0)
    for k in [2, 1] + [k for k in range(4, far) if k % 2 == 0]:
        keep(send(packed, 4 * k), 4 * k)
    keep(send(packed, 2), 2)
    keep(send(packed, 1), 1)
    dt = line(flip_body, shape(features, rows), "flip", [document_matrix], 0.1)
    score([0, 1])
    forward(2)
    forward(1)
    relay(2)
    share_all(2, 4, 8)
    score([2, 4, 8])
    softmax()
    relay(10)
    forward(3)
    score([3, 5, 9])
    relay(6)
    share(10, 6)
    softmax()
    relay(14)
    score([10, 6, 11, 7])
    share(12, 14)
    softmax()
    for k in range(3, far):
        if k + 1 < far:
            forward(k + 1)
        score([4 * k, 4 * k + 2, 4 * k + 1, 4 * k + 3])
        if k + 1 < far:
            relay(4 * k + 6)
            share(4 * k + 4, 4 * k + 6)
        if k == 3:
            pair(0, 2, 4, 8)
            beside(0)
        softmax()
        if k == 3:
            beside_all((10, 11), (6, 7))
        else:
            pair(4 * k - 2, 4 * k - 4)
            beside(k - 1)
    softmax()

    totals = line(
        functools.partial(stats_body, [e_place[r] for r in range(n)]),
        shape(2, n, rows),
        "stats",
        weights,
        0.05,
        [
            pl.BlockSpec((e.shape[0], SLACK, rows), lambda i: (0, rows // SLACK, 0))
            for e in weights
        ],
        grid=(1,),
        out_specs=full(2, n, rows),
    )
    masks = [1] + [4 << i for i in reversed(range(far.bit_length() - 1))] + [2]
    for mask in masks:
        there = send(totals, mask)
        if mask == 2:
            pair(4 * far - 4)
            inward(2)
            inward(1)
        totals = line(
            functools.partial(stats_merge_body, [mask]),
            shape(2, n, rows),
            "stats_merge",
            [totals, there],
            0.05,
        )
        if mask == 1:
            pair(4 * far - 2)
            beside(far - 1)
    for k in range(3, far):
        inward(k)

    group = 4
    width = 512
    e_at = 1 + len(x_arrays)
    document_derivative, grad_pool = line(
        functools.partial(
            gradient_body,
            [(x_place[r][0] + 1, x_place[r][1]) for r in range(n)],
            [(e_at + e_place[r][0], e_place[r][1]) for r in range(n)],
            group,
        ),
        (shape(rows, features), shape(features, columns)),
        "gradient",
        [totals, *x_arrays, *weights],
        11.0,
        limit=48,
        grid=(columns // width,),
        out_specs=(full(rows, features), pl.BlockSpec((features, width), lambda i: (0, i))),
        scratch_shapes=[
            pltpu.VMEM((n // group, 2 * features, group * rows), bf16),
            pltpu.VMEM((n // group, group * rows, 128), jnp.int32),
        ],
    )

    line.last = totals
    inward(0)
    arrays = home
    question_derivative, loss = line(
        last_body,
        (shape(rows, features), shape(rows)),
        "finish",
        [document_matrix, weights[0], *arrays],
        0.8,
        [full(rows, features)]
        + [pl.BlockSpec((1, SLACK, rows), lambda i: (0, rows // SLACK, 0))]
        + [full(*a.shape) for a in arrays],
        grid=(1,),
        out_specs=(full(rows, features), full(rows)),
    )
    return loss, question_derivative, document_derivative, grad_pool


def solution(mesh):
    placed = (P("blk", "dim"), P("blk", "dim"), P("dim", "blk"), P("blk", None), P("blk", None))
    return jax.shard_map(
        per_device,
        mesh=mesh,
        in_specs=placed,
        out_specs=(P("blk"), P("blk", "dim"), P("blk", "dim"), P("dim", "blk")),
        check_vma=False,
    )
```

```python
import functools

import jax
import jax.numpy as jnp
from jax import lax
from jax.experimental import pallas as pl
from jax.experimental.pallas import tpu as pltpu
from jax.sharding import PartitionSpec as P

logit_divisor = 0.05
LOWEST = -3.0e38
COST = 3.7e6
SLACK = 8

f32 = jnp.float32
bf16 = jnp.bfloat16


def split2(x):
    high = x.astype(bf16)
    return high, (x - high.astype(f32)).astype(bf16)


def dot(a, b, contract=((1,), (0,)), precision=None):
    return lax.dot_general(
        a, b, (contract, ((), ())), precision=precision, preferred_element_type=f32
    )


class Line:
    def __init__(self):
        self.last = None

    def __call__(self, body, out_shape, name, arrays, us, in_specs=None, limit=16, **kw):
        count = len(arrays)
        if in_specs is None:
            in_specs = [pl.BlockSpec(memory_space=pltpu.VMEM)] * count
        if self.last is not None:
            in_specs = list(in_specs) + [pl.BlockSpec(memory_space=pl.ANY)]
            arrays = list(arrays) + [self.last]

        def kernel(*refs):
            body(*refs[:count], *refs[len(arrays) :])

        out = pl.pallas_call(
            kernel,
            out_shape=out_shape,
            name=name,
            in_specs=in_specs,
            cost_estimate=pl.CostEstimate(
                flops=0, bytes_accessed=int(us * COST), transcendentals=0
            ),
            compiler_params=pltpu.CompilerParams(vmem_limit_bytes=limit << 20),
            **kw,
        )(*arrays)
        self.last = out[-1] if isinstance(out, (list, tuple)) else out
        return out


def shape(*dims, dtype=f32):
    return jax.ShapeDtypeStruct(dims, dtype)


def pack_body(columns, q_hbm, owner_hbm, local_hbm, x_ref, q_ref, owner_ref, local_ref, sems):
    pairs = ((q_hbm, q_ref), (owner_hbm, owner_ref), (local_hbm, local_ref))
    copies = [pltpu.make_async_copy(a, b, sems.at[i]) for i, (a, b) in enumerate(pairs)]
    for copy in copies:
        copy.start()
    for copy in copies:
        copy.wait()
    features = q_ref.shape[1]
    x_ref[:features, :] = q_ref[...].T
    x_ref[features:, :] = (owner_ref[...] * columns + local_ref[...]).astype(f32)


def relay_body(*refs):
    for k, ref in enumerate(refs[:-1]):
        refs[-1][k] = ref[...]


def flip_body(d_ref, dt_ref):
    dt_ref[...] = d_ref[...].T


def score_body(places, early, me_ref, d_ref, pool_ref, *refs):
    part_ref, rows_ref = refs[-2:]
    if early:
        early_part_ref, early_rows_ref = refs[-4:-2]
        part_ref[len(places) :] = early_part_ref[...]
        rows_ref[len(places) :] = early_rows_ref[...]
    rows, features = d_ref.shape
    columns = pool_ref.shape[1]
    tile = 128
    blocks = [refs[a][...] if k is None else refs[a][k] for a, k in places]
    for k, block in enumerate(blocks):
        x = block[:features]
        named = block[features:].astype(jnp.int32) - me_ref[0] * columns
        here = (named >= 0) & (named < columns)
        local = jnp.sum(jnp.where(here, named, 0), axis=0, keepdims=True)
        owned = jnp.any(here, axis=0, keepdims=True)
        lane = jnp.broadcast_to(local % tile, (features, rows))
        found = jnp.zeros((features, rows), f32)
        for t in range(columns // tile):
            picked = jnp.take_along_axis(
                pool_ref[:, t * tile : (t + 1) * tile], lane, axis=1, mode="promise_in_bounds"
            )
            found = jnp.where(local // tile == t, picked, found)
        rows_ref[k] = found
        hard = jnp.sum(x * found, axis=0, keepdims=True)
        chosen = jnp.where(owned, local, -1).astype(f32)
        part_ref[k, rows:] = jnp.concatenate(
            [hard, chosen, jnp.zeros((SLACK - 2, rows), f32)], axis=0
        )
    x = [block[:features] for block in blocks]
    x = x[0] if len(x) == 1 else jnp.concatenate(x, axis=1)
    scores = dot(d_ref[...], x, precision=lax.Precision.HIGHEST)
    for k in range(len(blocks)):
        part_ref[k, :rows] = scores[:, k * rows : (k + 1) * rows]


def softmax_body(evens, others, dt_ref, rows_ref, part_ref, *refs):
    got, (e_ref, *sum_refs) = refs[:others], refs[others:]
    features, rows = dt_ref.shape
    count = part_ref.shape[0]
    own = lax.broadcasted_iota(jnp.int32, (rows, rows), 0) == lax.broadcasted_iota(
        jnp.int32, (rows, rows), 1
    )
    tails, es = [], []
    for k in range(count):
        whole = part_ref[k]
        chosen = whole[rows + 1 : rows + 2]
        for r in got:
            whole = whole + r[k]
        scores = whole[:rows] / logit_divisor
        hard = jnp.where(chosen >= 0, whole[rows : rows + 1] / logit_divisor, LOWEST)
        peak = jnp.maximum(jnp.max(scores, axis=0, keepdims=True), hard)
        e = jnp.exp(scores - peak)
        hard_e = jnp.where(chosen >= 0, jnp.exp(hard - peak), 0.0)
        total = jnp.sum(e, axis=0, keepdims=True) + hard_e
        positive = jnp.sum(jnp.where(own, scores, 0.0), axis=0, keepdims=True)
        e_ref[k, :rows] = e
        e_ref[k, rows:] = jnp.concatenate(
            [hard_e, chosen, peak, total, positive, jnp.zeros((SLACK - 5, rows), f32)], axis=0
        )
        es.append(e)
        tails.append((hard_e, peak, total))
    e = es[0] if count == 1 else jnp.concatenate(es, axis=1)
    sums = dot(dt_ref[...], e, precision=lax.Precision.HIGHEST)
    for k, (hard_e, peak, total) in enumerate(tails):
        at = sum_refs[k] if k < evens else sum_refs[-1].at[k - evens]
        at[:features] = sums[:, k * rows : (k + 1) * rows] + rows_ref[k] * hard_e
        at[features:] = jnp.concatenate([peak, total, jnp.zeros((SLACK - 2, rows), f32)], axis=0)


def merge(terms):
    size = terms[0].shape[0] - SLACK
    peaks = [t[size : size + 1] for t in terms]
    peak = functools.reduce(jnp.maximum, peaks)
    scales = [jnp.exp(p - peak) for p in peaks]
    sums = functools.reduce(jnp.add, [t[:size] * s for t, s in zip(terms, scales)])
    total = functools.reduce(
        jnp.add, [t[size + 1 : size + 2] * s for t, s in zip(terms, scales)]
    )
    return sums, peak, total


def merge_body(places, *refs):
    out_ref = refs[-1]
    sums, peak, total = merge([r[...] if k is None else r[k] for r, k in zip(refs, places)])
    size = sums.shape[0]
    out_ref[:size] = sums
    out_ref[size:] = jnp.concatenate(
        [peak, total, jnp.zeros((SLACK - 2, peak.shape[1]), f32)], axis=0
    )


def merge_all_body(places, *refs):
    out_ref = refs[-1]
    size = out_ref.shape[1] - SLACK
    for slot, terms in enumerate(places):
        terms = [refs[i][...] if k is None else refs[i][k] for i, k in terms]
        if len(terms) == 1:
            out_ref[slot] = terms[0]
        else:
            sums, peak, total = merge(terms)
            out_ref[slot, :size] = sums
            out_ref[slot, size:] = jnp.concatenate(
                [peak, total, jnp.zeros((SLACK - 2, peak.shape[1]), f32)], axis=0
            )


def last_body(d_ref, e_ref, *refs):
    dq_ref, loss_ref = refs[-2:]
    sums, peak, total = merge([ref[...] for ref in refs[:-2]])
    dq_ref[...] = ((sums / total).T - d_ref[...]) / logit_divisor
    log_total = peak + jnp.log(total)
    loss_ref[...] = (log_total - e_ref[0, 4:5]).reshape(loss_ref.shape)


def stats_body(places, *refs):
    out_ref = refs[-1]
    for r, (i, k) in enumerate(places):
        out_ref[0, r : r + 1] = refs[i][k, 2:3]
        out_ref[1, r : r + 1] = refs[i][k, 3:4]


def stats_merge_body(masks, own_ref, *refs):
    out_ref = refs[-1]
    n = own_ref.shape[1]
    peaks, totals = [own_ref[0]], [own_ref[1]]
    for ref, mask in zip(refs, masks):
        for values, into in ((ref[0], peaks), (ref[1], totals)):
            into.append(
                jnp.concatenate([values[r ^ mask : (r ^ mask) + 1] for r in range(n)], axis=0)
            )
    peak = functools.reduce(jnp.maximum, peaks)
    out_ref[0] = peak
    out_ref[1] = functools.reduce(
        jnp.add, [t * jnp.exp(p - peak) for p, t in zip(peaks, totals)]
    )


def gradient_body(x_places, e_places, group, *refs):
    n = len(x_places)
    tot_ref = refs[0]
    dd_ref, pool_ref, scaled_ref, local_ref = refs[-4:]
    rows, features = dd_ref.shape
    lanes = local_ref.shape[-1]

    @pl.when(pl.program_id(0) == 0)
    def _():
        own = lax.broadcasted_iota(jnp.int32, (rows, rows), 0) == lax.broadcasted_iota(
            jnp.int32, (rows, rows), 1
        )
        total = jnp.zeros((features, rows), f32)
        for g in range(n // group):
            xs, es, hards = [], [], []
            for r in range(g * group, (g + 1) * group):
                i, k = x_places[r]
                xs.append(refs[i][:features] if k is None else refs[i][k, :features])
                i, k = e_places[r]
                scale = jnp.exp(refs[i][k, rows + 2 : rows + 3] - tot_ref[0, r : r + 1])
                scale = scale / tot_ref[1, r : r + 1]
                e = refs[i][k, :rows] * scale
                es.append(e if r else jnp.where(own, e - 1.0, e))
                hards.append(refs[i][k, rows : rows + 1] * scale)
                chosen = jnp.broadcast_to(refs[i][k, rows + 1 : rows + 2], (lanes, rows))
                first = (r - g * group) * rows
                local_ref[g, first : first + rows] = chosen.T.astype(jnp.int32)
            x = jnp.concatenate(xs, axis=1)
            chance = jnp.concatenate(es, axis=1)
            high, low = split2(x)
            c_high, c_low = split2(chance)
            both = dot(jnp.concatenate([high, low], axis=0), c_high, ((1,), (1,)))
            total = total + both[:features] + both[features:]
            total = total + dot(high, c_low, ((1,), (1,)))
            high, low = split2(x * (jnp.concatenate(hards, axis=1) / logit_divisor))
            scaled_ref[g, :features] = high
            scaled_ref[g, features:] = low
        dd_ref[...] = total.T / logit_divisor

    width = pool_ref.shape[1]
    first = pl.program_id(0) * width
    acc = jnp.zeros((2 * features, width), f32)
    for g in range(n // group):
        local = local_ref[g]
        column = first + lax.broadcasted_iota(jnp.int32, local.shape, 1)
        marks = jnp.concatenate(
            [
                jnp.where(local == column + t * lanes, 1.0, 0.0).astype(bf16)
                for t in range(width // lanes)
            ],
            axis=1,
        )
        acc = acc + dot(scaled_ref[g], marks)
    pool_ref[...] = acc[:features] + acc[features:]


def per_device(question_matrix, document_matrix, pool, hard_owner, hard_local):
    n, depth = lax.axis_size("blk"), lax.axis_size("dim")
    rows, features = question_matrix.shape
    columns = pool.shape[1]
    me = lax.axis_index("blk")
    smem = pl.BlockSpec(memory_space=pltpu.SMEM)
    vmem = pl.BlockSpec(memory_space=pltpu.VMEM)
    block = shape(features + SLACK, rows)
    line = Line()

    def full(*dims):
        return pl.BlockSpec(dims, lambda i: (0,) * len(dims))

    def send(x, mask):
        return lax.ppermute(x, "blk", [(i, i ^ mask) for i in range(n)])

    far = n // 4
    x, x_arrays, x_place = {}, [], {}

    def keep(array, *blocks):
        for k, r in enumerate(blocks):
            x[r] = array
            x_place[r] = (len(x_arrays), k if array.ndim == 3 else None)
        x_arrays.append(array)

    def pass_on(array):
        return line(lambda a, out: out.__setitem__(..., a[...]), block, "relay", [array], 0.05)

    def relay(r):
        x_arrays[x_place[r][0]] = x[r] = pass_on(x[r])

    def forward(k):
        relay(4 * k)
        if k % 2 == 0 and k + 1 < far:
            keep(send(x[4 * k], 4), 4 * k + 4)
        keep(send(x[4 * k], 2), 4 * k + 2)

    def share(*blocks):
        for r in blocks:
            keep(send(x[r], 1), r + 1)

    def share_all(*blocks):
        out = shape(len(blocks), features + SLACK, rows)
        held = line(relay_body, out, "relay", [x[r] for r in blocks], 0.05)
        keep(send(held, 1), *[r + 1 for r in blocks])

    weights, sums, e_place = [], {}, {}
    waiting, stage = [], {}

    held = []

    def score(blocks, hold=False):
        early = held.pop() if held else ([], ())
        k = len(blocks) + len(early[0])
        used = sorted({x_place[r][0] for r in blocks})
        part, found = line(
            functools.partial(
                score_body,
                [(used.index(x_place[r][0]), x_place[r][1]) for r in blocks],
                len(early[0]),
            ),
            (shape(k, rows + SLACK, rows), shape(k, features, rows)),
            "score",
            [me.reshape(1), document_matrix, pool] + [x_arrays[i] for i in used] + [*early[1]],
            0.9 * len(blocks),
            [smem] + [vmem] * (2 + len(used) + len(early[1])),
        )
        blocks = blocks + early[0]
        if hold:
            held.append((blocks, (part, found)))
            return
        got = [
            lax.ppermute(part, "dim", [(i, (i + s) % depth) for i in range(depth)])
            for s in range(1, depth)
        ]
        waiting.append((blocks, part, found, got))

    def softmax():
        blocks, part, found, got = waiting.pop(0)
        k = len(blocks)
        odds = [r for r in blocks if r % 2]
        evens = k - len(odds)
        stacked = len(odds) > 2
        e, *out = line(
            functools.partial(softmax_body, evens if stacked else k, len(got)),
            [shape(k, rows + SLACK, rows)]
            + [block] * (evens if stacked else k)
            + [shape(len(odds), features + SLACK, rows)] * stacked,
            "softmax",
            [dt, found, part, *got],
            0.25 * k,
        )
        for i, r in enumerate(blocks):
            e_place[r] = (len(weights), i)
        weights.append(e)
        for r, array in zip(blocks, out[:evens]):
            sums[r] = (array, None)
        shared = send(out[-1], 1) if stacked else None
        for i, r in enumerate(odds):
            sums[r] = (shared, i) if stacked else (send(out[evens + i], 1), None)

    over_x, home = {}, []

    def add(*terms):
        arrays = [array for array, k in terms]
        places = [k for array, k in terms]
        return line(functools.partial(merge_body, places), block, "merge", arrays, 0.05)

    def pair(*blocks):
        for r in blocks:
            sums[r] = (add(sums[r], sums[r + 1]), None)

    def beside(k):
        over_x[k] = (send(sums[4 * k + 2][0], 2), None)

    def beside_all(*blocks):
        arrays, places = [], []
        for terms in blocks:
            places.append([(len(arrays) + i, sums[r][1]) for i, r in enumerate(terms)])
            arrays += [sums[r][0] for r in terms]
        out = shape(len(blocks), features + SLACK, rows)
        held = line(functools.partial(merge_all_body, places), out, "merge", arrays, 0.1)
        shared = send(held, 2)
        for i, terms in enumerate(blocks):
            over_x[terms[0] // 4] = (shared, i)

    def inward(k):
        whole = add(sums[4 * k], over_x[k])
        home.append(send(whole, 4 * k) if k else whole)

    packed = line(
        functools.partial(pack_body, columns),
        block,
        "pack",
        [question_matrix, hard_owner.T, hard_local.T],
        1.8,
        [pl.BlockSpec(memory_space=pltpu.HBM)] * 3,
        limit=62,
        scratch_shapes=[
            pltpu.VMEM(question_matrix.shape, f32),
            pltpu.VMEM(hard_owner.shape[::-1], jnp.int32),
            pltpu.VMEM(hard_local.shape[::-1], jnp.int32),
            pltpu.SemaphoreType.DMA((3,)),
        ],
    )
    keep(packed, 0)
    for k in [2, 1] + [k for k in range(4, far) if k % 2 == 0]:
        keep(send(packed, 4 * k), 4 * k)
    keep(send(packed, 2), 2)
    keep(send(packed, 1), 1)
    dt = line(flip_body, shape(features, rows), "flip", [document_matrix], 0.1)
    score([0, 1], hold=True)
    forward(2)
    forward(1)
    relay(2)
    share_all(2, 4, 8)
    score([2, 4, 8])
    relay(10)
    forward(3)
    score([3, 5, 9])
    relay(6)
    share(10, 6)
    softmax()
    score([10, 6, 11, 7])
    relay(14)
    share(12, 14)
    softmax()
    for k in range(3, far):
        if k + 1 < far:
            forward(k + 1)
        score([4 * k, 4 * k + 2, 4 * k + 1, 4 * k + 3])
        if k + 1 < far:
            relay(4 * k + 6)
            share(4 * k + 4, 4 * k + 6)
        if k == 3:
            pair(0, 2, 4, 8)
            beside(0)
        softmax()
        if k == 3:
            beside_all((10, 11), (6, 7))
        else:
            pair(4 * k - 2, 4 * k - 4)
            beside(k - 1)
    softmax()

    totals = line(
        functools.partial(stats_body, [e_place[r] for r in range(n)]),
        shape(2, n, rows),
        "stats",
        weights,
        0.05,
        [
            pl.BlockSpec((e.shape[0], SLACK, rows), lambda i: (0, rows // SLACK, 0))
            for e in weights
        ],
        grid=(1,),
        out_specs=full(2, n, rows),
    )
    masks = [1] + [4 << i for i in reversed(range(far.bit_length() - 1))] + [2]
    for mask in masks:
        there = send(totals, mask)
        if mask == 2:
            pair(4 * far - 4)
            inward(2)
            inward(1)
        totals = line(
            functools.partial(stats_merge_body, [mask]),
            shape(2, n, rows),
            "stats_merge",
            [totals, there],
            0.05,
        )
        if mask == 1:
            pair(4 * far - 2)
            beside(far - 1)
    for k in range(3, far):
        inward(k)

    group = 4
    width = 512
    e_at = 1 + len(x_arrays)
    document_derivative, grad_pool = line(
        functools.partial(
            gradient_body,
            [(x_place[r][0] + 1, x_place[r][1]) for r in range(n)],
            [(e_at + e_place[r][0], e_place[r][1]) for r in range(n)],
            group,
        ),
        (shape(rows, features), shape(features, columns)),
        "gradient",
        [totals, *x_arrays, *weights],
        11.0,
        limit=48,
        grid=(columns // width,),
        out_specs=(full(rows, features), pl.BlockSpec((features, width), lambda i: (0, i))),
        scratch_shapes=[
            pltpu.VMEM((n // group, 2 * features, group * rows), bf16),
            pltpu.VMEM((n // group, group * rows, 128), jnp.int32),
        ],
    )

    line.last = totals
    inward(0)
    arrays = home
    question_derivative, loss = line(
        last_body,
        (shape(rows, features), shape(rows)),
        "finish",
        [document_matrix, weights[e_place[0][0]], *arrays],
        0.8,
        [full(rows, features)]
        + [pl.BlockSpec((1, SLACK, rows), lambda i: (e_place[0][1], rows // SLACK, 0))]
        + [full(*a.shape) for a in arrays],
        grid=(1,),
        out_specs=(full(rows, features), full(rows)),
    )
    return loss, question_derivative, document_derivative, grad_pool


def solution(mesh):
    placed = (P("blk", "dim"), P("blk", "dim"), P("dim", "blk"), P("blk", None), P("blk", None))
    return jax.shard_map(
        per_device,
        mesh=mesh,
        in_specs=placed,
        out_specs=(P("blk"), P("blk", "dim"), P("blk", "dim"), P("dim", "blk")),
        check_vma=False,
    )
```

```python
import functools

import jax
import jax.numpy as jnp
from jax import lax
from jax.experimental import pallas as pl
from jax.experimental.pallas import tpu as pltpu
from jax.sharding import PartitionSpec as P

logit_divisor = 0.05
LOWEST = -3.0e38
COST = 3.7e6
SLACK = 8

f32 = jnp.float32
bf16 = jnp.bfloat16


def split2(x):
    high = x.astype(bf16)
    return high, (x - high.astype(f32)).astype(bf16)


def dot(a, b, contract=((1,), (0,)), precision=None):
    return lax.dot_general(
        a, b, (contract, ((), ())), precision=precision, preferred_element_type=f32
    )


class Line:
    def __init__(self):
        self.last = None

    def __call__(self, body, out_shape, name, arrays, us, in_specs=None, limit=16, **kw):
        count = len(arrays)
        if in_specs is None:
            in_specs = [pl.BlockSpec(memory_space=pltpu.VMEM)] * count
        if self.last is not None:
            in_specs = list(in_specs) + [pl.BlockSpec(memory_space=pl.ANY)]
            arrays = list(arrays) + [self.last]

        def kernel(*refs):
            body(*refs[:count], *refs[len(arrays) :])

        out = pl.pallas_call(
            kernel,
            out_shape=out_shape,
            name=name,
            in_specs=in_specs,
            cost_estimate=pl.CostEstimate(
                flops=0, bytes_accessed=int(us * COST), transcendentals=0
            ),
            compiler_params=pltpu.CompilerParams(vmem_limit_bytes=limit << 20),
            **kw,
        )(*arrays)
        self.last = out[-1] if isinstance(out, (list, tuple)) else out
        return out


def shape(*dims, dtype=f32):
    return jax.ShapeDtypeStruct(dims, dtype)


def pack_body(columns, q_hbm, owner_hbm, local_hbm, x_ref, q_ref, owner_ref, local_ref, sems):
    pairs = ((q_hbm, q_ref), (owner_hbm, owner_ref), (local_hbm, local_ref))
    copies = [pltpu.make_async_copy(a, b, sems.at[i]) for i, (a, b) in enumerate(pairs)]
    for copy in copies:
        copy.start()
    for copy in copies:
        copy.wait()
    features = q_ref.shape[1]
    x_ref[:features, :] = q_ref[...].T
    x_ref[features:, :] = (owner_ref[...] * columns + local_ref[...]).astype(f32)


def relay_body(*refs):
    for k, ref in enumerate(refs[:-1]):
        refs[-1][k] = ref[...]


def flip_body(d_ref, dt_ref):
    dt_ref[...] = d_ref[...].T


def score_body(places, early, me_ref, d_ref, pool_ref, *refs):
    part_ref, rows_ref = refs[-2:]
    if early:
        early_part_ref, early_rows_ref = refs[-4:-2]
        part_ref[len(places) :] = early_part_ref[...]
        rows_ref[len(places) :] = early_rows_ref[...]
    rows, features = d_ref.shape
    columns = pool_ref.shape[1]
    tile = 128
    blocks = [refs[a][...] if k is None else refs[a][k] for a, k in places]
    for k, block in enumerate(blocks):
        x = block[:features]
        named = block[features:].astype(jnp.int32) - me_ref[0] * columns
        here = (named >= 0) & (named < columns)
        local = jnp.sum(jnp.where(here, named, 0), axis=0, keepdims=True)
        owned = jnp.any(here, axis=0, keepdims=True)
        lane = jnp.broadcast_to(local % tile, (features, rows))
        found = jnp.zeros((features, rows), f32)
        for t in range(columns // tile):
            picked = jnp.take_along_axis(
                pool_ref[:, t * tile : (t + 1) * tile], lane, axis=1, mode="promise_in_bounds"
            )
            found = jnp.where(local // tile == t, picked, found)
        rows_ref[k] = found
        hard = jnp.sum(x * found, axis=0, keepdims=True)
        chosen = jnp.where(owned, local, -1).astype(f32)
        part_ref[k, rows:] = jnp.concatenate(
            [hard, chosen, jnp.zeros((SLACK - 2, rows), f32)], axis=0
        )
    x = [block[:features] for block in blocks]
    x = x[0] if len(x) == 1 else jnp.concatenate(x, axis=1)
    scores = dot(d_ref[...], x, precision=lax.Precision.HIGHEST)
    for k in range(len(blocks)):
        part_ref[k, :rows] = scores[:, k * rows : (k + 1) * rows]


def softmax_body(evens, others, dt_ref, rows_ref, part_ref, *refs):
    got, (e_ref, *sum_refs) = refs[:others], refs[others:]
    features, rows = dt_ref.shape
    count = part_ref.shape[0]
    own = lax.broadcasted_iota(jnp.int32, (rows, rows), 0) == lax.broadcasted_iota(
        jnp.int32, (rows, rows), 1
    )
    tails, es = [], []
    for k in range(count):
        whole = part_ref[k]
        chosen = whole[rows + 1 : rows + 2]
        for r in got:
            whole = whole + r[k]
        scores = whole[:rows] / logit_divisor
        hard = jnp.where(chosen >= 0, whole[rows : rows + 1] / logit_divisor, LOWEST)
        peak = jnp.maximum(jnp.max(scores, axis=0, keepdims=True), hard)
        e = jnp.exp(scores - peak)
        hard_e = jnp.where(chosen >= 0, jnp.exp(hard - peak), 0.0)
        total = jnp.sum(e, axis=0, keepdims=True) + hard_e
        positive = jnp.sum(jnp.where(own, scores, 0.0), axis=0, keepdims=True)
        e_ref[k, :rows] = e
        e_ref[k, rows:] = jnp.concatenate(
            [hard_e, chosen, peak, total, positive, jnp.zeros((SLACK - 5, rows), f32)], axis=0
        )
        es.append(e)
        tails.append((hard_e, peak, total))
    e = es[0] if count == 1 else jnp.concatenate(es, axis=1)
    sums = dot(dt_ref[...], e, precision=lax.Precision.HIGHEST)
    for k, (hard_e, peak, total) in enumerate(tails):
        at = sum_refs[k] if k < evens else sum_refs[-1].at[k - evens]
        at[:features] = sums[:, k * rows : (k + 1) * rows] + rows_ref[k] * hard_e
        at[features:] = jnp.concatenate([peak, total, jnp.zeros((SLACK - 2, rows), f32)], axis=0)


def merge(terms):
    size = terms[0].shape[0] - SLACK
    peaks = [t[size : size + 1] for t in terms]
    peak = functools.reduce(jnp.maximum, peaks)
    scales = [jnp.exp(p - peak) for p in peaks]
    sums = functools.reduce(jnp.add, [t[:size] * s for t, s in zip(terms, scales)])
    total = functools.reduce(
        jnp.add, [t[size + 1 : size + 2] * s for t, s in zip(terms, scales)]
    )
    return sums, peak, total


def merge_body(places, *refs):
    out_ref = refs[-1]
    sums, peak, total = merge([r[...] if k is None else r[k] for r, k in zip(refs, places)])
    size = sums.shape[0]
    out_ref[:size] = sums
    out_ref[size:] = jnp.concatenate(
        [peak, total, jnp.zeros((SLACK - 2, peak.shape[1]), f32)], axis=0
    )


def merge_all_body(places, *refs):
    out_ref = refs[-1]
    size = out_ref.shape[1] - SLACK
    for slot, terms in enumerate(places):
        terms = [refs[i][...] if k is None else refs[i][k] for i, k in terms]
        if len(terms) == 1:
            out_ref[slot] = terms[0]
        else:
            sums, peak, total = merge(terms)
            out_ref[slot, :size] = sums
            out_ref[slot, size:] = jnp.concatenate(
                [peak, total, jnp.zeros((SLACK - 2, peak.shape[1]), f32)], axis=0
            )


def last_body(d_ref, e_ref, *refs):
    dq_ref, loss_ref = refs[-2:]
    sums, peak, total = merge([ref[...] for ref in refs[:-2]])
    dq_ref[...] = ((sums / total).T - d_ref[...]) / logit_divisor
    log_total = peak + jnp.log(total)
    loss_ref[...] = (log_total - e_ref[0, 4:5]).reshape(loss_ref.shape)


def stats_body(places, *refs):
    out_ref = refs[-1]
    for r, (i, k) in enumerate(places):
        out_ref[0, r : r + 1] = refs[i][k, 2:3]
        out_ref[1, r : r + 1] = refs[i][k, 3:4]


def stats_merge_body(masks, own_ref, *refs):
    out_ref = refs[-1]
    n = own_ref.shape[1]
    peaks, totals = [own_ref[0]], [own_ref[1]]
    for ref, mask in zip(refs, masks):
        for values, into in ((ref[0], peaks), (ref[1], totals)):
            into.append(
                jnp.concatenate([values[r ^ mask : (r ^ mask) + 1] for r in range(n)], axis=0)
            )
    peak = functools.reduce(jnp.maximum, peaks)
    out_ref[0] = peak
    out_ref[1] = functools.reduce(
        jnp.add, [t * jnp.exp(p - peak) for p, t in zip(peaks, totals)]
    )


def gradient_body(x_places, e_places, group, *refs):
    n = len(x_places)
    tot_ref = refs[0]
    dd_ref, pool_ref, scaled_ref, local_ref = refs[-4:]
    rows, features = dd_ref.shape
    lanes = local_ref.shape[-1]

    @pl.when(pl.program_id(0) == 0)
    def _():
        own = lax.broadcasted_iota(jnp.int32, (rows, rows), 0) == lax.broadcasted_iota(
            jnp.int32, (rows, rows), 1
        )
        total = jnp.zeros((features, rows), f32)
        for g in range(n // group):
            xs, es, hards = [], [], []
            for r in range(g * group, (g + 1) * group):
                i, k = x_places[r]
                xs.append(refs[i][:features] if k is None else refs[i][k, :features])
                i, k = e_places[r]
                scale = jnp.exp(refs[i][k, rows + 2 : rows + 3] - tot_ref[0, r : r + 1])
                scale = scale / tot_ref[1, r : r + 1]
                e = refs[i][k, :rows] * scale
                es.append(e if r else jnp.where(own, e - 1.0, e))
                hards.append(refs[i][k, rows : rows + 1] * scale)
                chosen = jnp.broadcast_to(refs[i][k, rows + 1 : rows + 2], (lanes, rows))
                first = (r - g * group) * rows
                local_ref[g, first : first + rows] = chosen.T.astype(jnp.int32)
            x = jnp.concatenate(xs, axis=1)
            chance = jnp.concatenate(es, axis=1)
            high, low = split2(x)
            c_high, c_low = split2(chance)
            both = dot(jnp.concatenate([high, low], axis=0), c_high, ((1,), (1,)))
            total = total + both[:features] + both[features:]
            total = total + dot(high, c_low, ((1,), (1,)))
            high, low = split2(x * (jnp.concatenate(hards, axis=1) / logit_divisor))
            scaled_ref[g, :features] = high
            scaled_ref[g, features:] = low
        dd_ref[...] = total.T / logit_divisor

    width = pool_ref.shape[1]
    first = pl.program_id(0) * width
    acc = jnp.zeros((2 * features, width), f32)
    for g in range(n // group):
        local = local_ref[g]
        column = first + lax.broadcasted_iota(jnp.int32, local.shape, 1)
        marks = jnp.concatenate(
            [
                jnp.where(local == column + t * lanes, 1.0, 0.0).astype(bf16)
                for t in range(width // lanes)
            ],
            axis=1,
        )
        acc = acc + dot(scaled_ref[g], marks)
    pool_ref[...] = acc[:features] + acc[features:]


def per_device(question_matrix, document_matrix, pool, hard_owner, hard_local):
    n, depth = lax.axis_size("blk"), lax.axis_size("dim")
    rows, features = question_matrix.shape
    columns = pool.shape[1]
    me = lax.axis_index("blk")
    smem = pl.BlockSpec(memory_space=pltpu.SMEM)
    vmem = pl.BlockSpec(memory_space=pltpu.VMEM)
    block = shape(features + SLACK, rows)
    line = Line()

    def full(*dims):
        return pl.BlockSpec(dims, lambda i: (0,) * len(dims))

    def send(x, mask):
        return lax.ppermute(x, "blk", [(i, i ^ mask) for i in range(n)])

    far = n // 4
    x, x_arrays, x_place = {}, [], {}

    def keep(array, *blocks):
        for k, r in enumerate(blocks):
            x[r] = array
            x_place[r] = (len(x_arrays), k if array.ndim == 3 else None)
        x_arrays.append(array)

    def pass_on(array):
        return line(lambda a, out: out.__setitem__(..., a[...]), block, "relay", [array], 0.05)

    def relay(r):
        x_arrays[x_place[r][0]] = x[r] = pass_on(x[r])

    def forward(k):
        relay(4 * k)
        if k % 2 == 0 and k + 1 < far:
            keep(send(x[4 * k], 4), 4 * k + 4)
        keep(send(x[4 * k], 2), 4 * k + 2)

    def share(*blocks):
        for r in blocks:
            keep(send(x[r], 1), r + 1)

    def share_all(*blocks):
        out = shape(len(blocks), features + SLACK, rows)
        held = line(relay_body, out, "relay", [x[r] for r in blocks], 0.05)
        keep(send(held, 1), *[r + 1 for r in blocks])

    weights, sums, e_place = [], {}, {}
    waiting, stage = [], {}

    held = []

    def score(blocks, hold=False):
        early = held.pop() if held else ([], ())
        k = len(blocks) + len(early[0])
        used = sorted({x_place[r][0] for r in blocks})
        part, found = line(
            functools.partial(
                score_body,
                [(used.index(x_place[r][0]), x_place[r][1]) for r in blocks],
                len(early[0]),
            ),
            (shape(k, rows + SLACK, rows), shape(k, features, rows)),
            "score",
            [me.reshape(1), document_matrix, pool] + [x_arrays[i] for i in used] + [*early[1]],
            0.9 * len(blocks),
            [smem] + [vmem] * (2 + len(used) + len(early[1])),
        )
        blocks = [r for r in blocks + early[0] if r % 2 == 0] + [
            r for r in blocks + early[0] if r % 2
        ]
        if hold:
            held.append((blocks, (part, found)))
            return
        got = [
            lax.ppermute(part, "dim", [(i, (i + s) % depth) for i in range(depth)])
            for s in range(1, depth)
        ]
        waiting.append((blocks, part, found, got))

    def softmax():
        blocks, part, found, got = waiting.pop(0)
        k = len(blocks)
        odds = [r for r in blocks if r % 2]
        evens = k - len(odds)
        stacked = False
        e, *out = line(
            functools.partial(softmax_body, evens if stacked else k, len(got)),
            [shape(k, rows + SLACK, rows)]
            + [block] * (evens if stacked else k)
            + [shape(len(odds), features + SLACK, rows)] * stacked,
            "softmax",
            [dt, found, part, *got],
            0.25 * k,
        )
        for i, r in enumerate(blocks):
            e_place[r] = (len(weights), i)
        weights.append(e)
        for r, array in zip(blocks, out[:evens]):
            sums[r] = (array, None)
        shared = send(out[-1], 1) if stacked else None
        for i, r in enumerate(odds):
            sums[r] = (shared, i) if stacked else (send(out[evens + i], 1), None)

    over_x, home = {}, []

    def add(*terms):
        arrays = [array for array, k in terms]
        places = [k for array, k in terms]
        return line(functools.partial(merge_body, places), block, "merge", arrays, 0.05)

    def pair(*blocks):
        for r in blocks:
            sums[r] = (add(sums[r], sums[r + 1]), None)

    def beside(k):
        over_x[k] = (send(sums[4 * k + 2][0], 2), None)

    def beside_all(*blocks):
        arrays, places = [], []
        for terms in blocks:
            places.append([(len(arrays) + i, sums[r][1]) for i, r in enumerate(terms)])
            arrays += [sums[r][0] for r in terms]
        out = shape(len(blocks), features + SLACK, rows)
        held = line(functools.partial(merge_all_body, places), out, "merge", arrays, 0.1)
        shared = send(held, 2)
        for i, terms in enumerate(blocks):
            over_x[terms[0] // 4] = (shared, i)

    def inward(k):
        whole = add(sums[4 * k], over_x[k])
        home.append(send(whole, 4 * k) if k else whole)

    packed = line(
        functools.partial(pack_body, columns),
        block,
        "pack",
        [question_matrix, hard_owner.T, hard_local.T],
        1.8,
        [pl.BlockSpec(memory_space=pltpu.HBM)] * 3,
        limit=62,
        scratch_shapes=[
            pltpu.VMEM(question_matrix.shape, f32),
            pltpu.VMEM(hard_owner.shape[::-1], jnp.int32),
            pltpu.VMEM(hard_local.shape[::-1], jnp.int32),
            pltpu.SemaphoreType.DMA((3,)),
        ],
    )
    keep(packed, 0)
    for k in [2, 1] + [k for k in range(4, far) if k % 2 == 0]:
        keep(send(packed, 4 * k), 4 * k)
    keep(send(packed, 2), 2)
    keep(send(packed, 1), 1)
    line.last = None
    dt = line(flip_body, shape(features, rows), "flip", [document_matrix], 0.1)
    score([0, 1], hold=True)
    forward(2)
    forward(1)
    relay(2)
    share_all(2, 4, 8)
    score([2, 4, 8])
    relay(10)
    forward(3)
    score([3, 5, 9])
    relay(6)
    share(10, 6)
    score([10, 6, 11, 7])
    softmax()
    relay(14)
    share(12, 14)
    softmax()
    for k in range(3, far):
        if k + 1 < far:
            forward(k + 1)
        score([4 * k, 4 * k + 2, 4 * k + 1, 4 * k + 3])
        if k + 1 < far:
            relay(4 * k + 6)
            share(4 * k + 4, 4 * k + 6)
        if k == 3:
            pair(0, 2, 4, 8)
            beside(0)
        softmax()
        if k == 3:
            beside_all((10, 11), (6, 7))
        else:
            pair(4 * k - 2, 4 * k - 4)
            beside(k - 1)
    softmax()

    totals = line(
        functools.partial(stats_body, [e_place[r] for r in range(n)]),
        shape(2, n, rows),
        "stats",
        weights,
        0.05,
        [
            pl.BlockSpec((e.shape[0], SLACK, rows), lambda i: (0, rows // SLACK, 0))
            for e in weights
        ],
        grid=(1,),
        out_specs=full(2, n, rows),
    )
    masks = [1] + [4 << i for i in reversed(range(far.bit_length() - 1))] + [2]
    for mask in masks:
        there = send(totals, mask)
        if mask == 2:
            pair(4 * far - 4)
            inward(2)
            inward(1)
        totals = line(
            functools.partial(stats_merge_body, [mask]),
            shape(2, n, rows),
            "stats_merge",
            [totals, there],
            0.05,
        )
        if mask == 1:
            pair(4 * far - 2)
            beside(far - 1)
    for k in range(3, far):
        inward(k)

    group = 4
    width = 512
    e_at = 1 + len(x_arrays)
    document_derivative, grad_pool = line(
        functools.partial(
            gradient_body,
            [(x_place[r][0] + 1, x_place[r][1]) for r in range(n)],
            [(e_at + e_place[r][0], e_place[r][1]) for r in range(n)],
            group,
        ),
        (shape(rows, features), shape(features, columns)),
        "gradient",
        [totals, *x_arrays, *weights],
        11.0,
        limit=48,
        grid=(columns // width,),
        out_specs=(full(rows, features), pl.BlockSpec((features, width), lambda i: (0, i))),
        scratch_shapes=[
            pltpu.VMEM((n // group, 2 * features, group * rows), bf16),
            pltpu.VMEM((n // group, group * rows, 128), jnp.int32),
        ],
    )

    line.last = totals
    inward(0)
    arrays = home
    question_derivative, loss = line(
        last_body,
        (shape(rows, features), shape(rows)),
        "finish",
        [document_matrix, weights[e_place[0][0]], *arrays],
        0.8,
        [full(rows, features)]
        + [pl.BlockSpec((1, SLACK, rows), lambda i: (e_place[0][1], rows // SLACK, 0))]
        + [full(*a.shape) for a in arrays],
        grid=(1,),
        out_specs=(full(rows, features), full(rows)),
    )
    return loss, question_derivative, document_derivative, grad_pool


def solution(mesh):
    placed = (P("blk", "dim"), P("blk", "dim"), P("dim", "blk"), P("blk", None), P("blk", None))
    return jax.shard_map(
        per_device,
        mesh=mesh,
        in_specs=placed,
        out_specs=(P("blk"), P("blk", "dim"), P("blk", "dim"), P("dim", "blk")),
        check_vma=False,
    )
```

```python
import functools

import jax
import jax.numpy as jnp
from jax import lax
from jax.experimental import pallas as pl
from jax.experimental.pallas import tpu as pltpu
from jax.sharding import PartitionSpec as P

logit_divisor = 0.05
LOWEST = -3.0e38
COST = 3.7e6
SLACK = 8

f32 = jnp.float32
bf16 = jnp.bfloat16


def split2(x):
    high = x.astype(bf16)
    return high, (x - high.astype(f32)).astype(bf16)


def dot(a, b, contract=((1,), (0,)), precision=None):
    return lax.dot_general(
        a, b, (contract, ((), ())), precision=precision, preferred_element_type=f32
    )


class Line:
    def __init__(self):
        self.last = None

    def __call__(self, body, out_shape, name, arrays, us, in_specs=None, limit=16, **kw):
        count = len(arrays)
        if in_specs is None:
            in_specs = [pl.BlockSpec(memory_space=pltpu.VMEM)] * count
        if self.last is not None:
            in_specs = list(in_specs) + [pl.BlockSpec(memory_space=pl.ANY)]
            arrays = list(arrays) + [self.last]

        def kernel(*refs):
            body(*refs[:count], *refs[len(arrays) :])

        out = pl.pallas_call(
            kernel,
            out_shape=out_shape,
            name=name,
            in_specs=in_specs,
            cost_estimate=pl.CostEstimate(
                flops=0, bytes_accessed=int(us * COST), transcendentals=0
            ),
            compiler_params=pltpu.CompilerParams(vmem_limit_bytes=limit << 20),
            **kw,
        )(*arrays)
        self.last = out[-1] if isinstance(out, (list, tuple)) else out
        return out


def shape(*dims, dtype=f32):
    return jax.ShapeDtypeStruct(dims, dtype)


def pack_body(columns, q_hbm, owner_hbm, local_hbm, x_ref, q_ref, owner_ref, local_ref, sems):
    pairs = ((q_hbm, q_ref), (owner_hbm, owner_ref), (local_hbm, local_ref))
    copies = [pltpu.make_async_copy(a, b, sems.at[i]) for i, (a, b) in enumerate(pairs)]
    for copy in copies:
        copy.start()
    for copy in copies:
        copy.wait()
    features = q_ref.shape[1]
    x_ref[:features, :] = q_ref[...].T
    x_ref[features:, :] = (owner_ref[...] * columns + local_ref[...]).astype(f32)


def relay_body(*refs):
    for k, ref in enumerate(refs[:-1]):
        refs[-1][k] = ref[...]


def flip_body(d_ref, dt_ref):
    dt_ref[...] = d_ref[...].T


def score_body(places, early, me_ref, d_ref, pool_ref, *refs):
    part_ref, rows_ref = refs[-2:]
    if early:
        early_part_ref, early_rows_ref = refs[-4:-2]
        part_ref[len(places) :] = early_part_ref[...]
        rows_ref[len(places) :] = early_rows_ref[...]
    rows, features = d_ref.shape
    columns = pool_ref.shape[1]
    tile = 128
    blocks = [refs[a][...] if k is None else refs[a][k] for a, k in places]
    for k, block in enumerate(blocks):
        x = block[:features]
        named = block[features:].astype(jnp.int32) - me_ref[0] * columns
        here = (named >= 0) & (named < columns)
        local = jnp.sum(jnp.where(here, named, 0), axis=0, keepdims=True)
        owned = jnp.any(here, axis=0, keepdims=True)
        lane = jnp.broadcast_to(local % tile, (features, rows))
        found = jnp.zeros((features, rows), f32)
        for t in range(columns // tile):
            picked = jnp.take_along_axis(
                pool_ref[:, t * tile : (t + 1) * tile], lane, axis=1, mode="promise_in_bounds"
            )
            found = jnp.where(local // tile == t, picked, found)
        rows_ref[k] = found
        hard = jnp.sum(x * found, axis=0, keepdims=True)
        chosen = jnp.where(owned, local, -1).astype(f32)
        part_ref[k, rows:] = jnp.concatenate(
            [hard, chosen, jnp.zeros((SLACK - 2, rows), f32)], axis=0
        )
    x = [block[:features] for block in blocks]
    x = x[0] if len(x) == 1 else jnp.concatenate(x, axis=1)
    scores = dot(d_ref[...], x, precision=lax.Precision.HIGHEST)
    for k in range(len(blocks)):
        part_ref[k, :rows] = scores[:, k * rows : (k + 1) * rows]


def softmax_body(evens, others, dt_ref, rows_ref, part_ref, *refs):
    got, (e_ref, *sum_refs) = refs[:others], refs[others:]
    features, rows = dt_ref.shape
    count = part_ref.shape[0]
    own = lax.broadcasted_iota(jnp.int32, (rows, rows), 0) == lax.broadcasted_iota(
        jnp.int32, (rows, rows), 1
    )
    tails, es = [], []
    for k in range(count):
        whole = part_ref[k]
        chosen = whole[rows + 1 : rows + 2]
        for r in got:
            whole = whole + r[k]
        scores = whole[:rows] / logit_divisor
        hard = jnp.where(chosen >= 0, whole[rows : rows + 1] / logit_divisor, LOWEST)
        peak = jnp.maximum(jnp.max(scores, axis=0, keepdims=True), hard)
        e = jnp.exp(scores - peak)
        hard_e = jnp.where(chosen >= 0, jnp.exp(hard - peak), 0.0)
        total = jnp.sum(e, axis=0, keepdims=True) + hard_e
        positive = jnp.sum(jnp.where(own, scores, 0.0), axis=0, keepdims=True)
        e_ref[k, :rows] = e
        e_ref[k, rows:] = jnp.concatenate(
            [hard_e, chosen, peak, total, positive, jnp.zeros((SLACK - 5, rows), f32)], axis=0
        )
        es.append(e)
        tails.append((hard_e, peak, total))
    e = es[0] if count == 1 else jnp.concatenate(es, axis=1)
    sums = dot(dt_ref[...], e, precision=lax.Precision.HIGHEST)
    for k, (hard_e, peak, total) in enumerate(tails):
        at = sum_refs[k] if k < evens else sum_refs[-1].at[k - evens]
        at[:features] = sums[:, k * rows : (k + 1) * rows] + rows_ref[k] * hard_e
        at[features:] = jnp.concatenate([peak, total, jnp.zeros((SLACK - 2, rows), f32)], axis=0)


def merge(terms):
    size = terms[0].shape[0] - SLACK
    peaks = [t[size : size + 1] for t in terms]
    peak = functools.reduce(jnp.maximum, peaks)
    scales = [jnp.exp(p - peak) for p in peaks]
    sums = functools.reduce(jnp.add, [t[:size] * s for t, s in zip(terms, scales)])
    total = functools.reduce(
        jnp.add, [t[size + 1 : size + 2] * s for t, s in zip(terms, scales)]
    )
    return sums, peak, total


def merge_body(places, *refs):
    out_ref = refs[-1]
    sums, peak, total = merge([r[...] if k is None else r[k] for r, k in zip(refs, places)])
    size = sums.shape[0]
    out_ref[:size] = sums
    out_ref[size:] = jnp.concatenate(
        [peak, total, jnp.zeros((SLACK - 2, peak.shape[1]), f32)], axis=0
    )


def merge_all_body(places, *refs):
    out_ref = refs[-1]
    size = out_ref.shape[1] - SLACK
    for slot, terms in enumerate(places):
        terms = [refs[i][...] if k is None else refs[i][k] for i, k in terms]
        if len(terms) == 1:
            out_ref[slot] = terms[0]
        else:
            sums, peak, total = merge(terms)
            out_ref[slot, :size] = sums
            out_ref[slot, size:] = jnp.concatenate(
                [peak, total, jnp.zeros((SLACK - 2, peak.shape[1]), f32)], axis=0
            )


def last_body(d_ref, e_ref, *refs):
    dq_ref, loss_ref = refs[-2:]
    sums, peak, total = merge([ref[...] for ref in refs[:-2]])
    dq_ref[...] = ((sums / total).T - d_ref[...]) / logit_divisor
    log_total = peak + jnp.log(total)
    loss_ref[...] = (log_total - e_ref[0, 4:5]).reshape(loss_ref.shape)


def stats_body(places, *refs):
    out_ref = refs[-1]
    for r, (i, k) in enumerate(places):
        out_ref[0, r : r + 1] = refs[i][k, 2:3]
        out_ref[1, r : r + 1] = refs[i][k, 3:4]


def stats_merge_body(masks, own_ref, *refs):
    out_ref = refs[-1]
    n = own_ref.shape[1]
    peaks, totals = [own_ref[0]], [own_ref[1]]
    for ref, mask in zip(refs, masks):
        for values, into in ((ref[0], peaks), (ref[1], totals)):
            into.append(
                jnp.concatenate([values[r ^ mask : (r ^ mask) + 1] for r in range(n)], axis=0)
            )
    peak = functools.reduce(jnp.maximum, peaks)
    out_ref[0] = peak
    out_ref[1] = functools.reduce(
        jnp.add, [t * jnp.exp(p - peak) for p, t in zip(peaks, totals)]
    )


def gradient_body(x_places, e_places, group, *refs):
    n = len(x_places)
    tot_ref = refs[0]
    dd_ref, pool_ref, scaled_ref, local_ref = refs[-4:]
    rows, features = dd_ref.shape
    lanes = local_ref.shape[-1]

    @pl.when(pl.program_id(0) == 0)
    def _():
        own = lax.broadcasted_iota(jnp.int32, (rows, rows), 0) == lax.broadcasted_iota(
            jnp.int32, (rows, rows), 1
        )
        total = jnp.zeros((features, rows), f32)
        for g in range(n // group):
            xs, es, hards = [], [], []
            for r in range(g * group, (g + 1) * group):
                i, k = x_places[r]
                xs.append(refs[i][:features] if k is None else refs[i][k, :features])
                i, k = e_places[r]
                scale = jnp.exp(refs[i][k, rows + 2 : rows + 3] - tot_ref[0, r : r + 1])
                scale = scale / tot_ref[1, r : r + 1]
                e = refs[i][k, :rows] * scale
                es.append(e if r else jnp.where(own, e - 1.0, e))
                hards.append(refs[i][k, rows : rows + 1] * scale)
                chosen = jnp.broadcast_to(refs[i][k, rows + 1 : rows + 2], (lanes, rows))
                first = (r - g * group) * rows
                local_ref[g, first : first + rows] = chosen.T.astype(jnp.int32)
            x = jnp.concatenate(xs, axis=1)
            chance = jnp.concatenate(es, axis=1)
            high, low = split2(x)
            c_high, c_low = split2(chance)
            both = dot(jnp.concatenate([high, low], axis=0), c_high, ((1,), (1,)))
            total = total + both[:features] + both[features:]
            total = total + dot(high, c_low, ((1,), (1,)))
            high, low = split2(x * (jnp.concatenate(hards, axis=1) / logit_divisor))
            scaled_ref[g, :features] = high
            scaled_ref[g, features:] = low
        dd_ref[...] = total.T / logit_divisor

    width = pool_ref.shape[1]
    first = pl.program_id(0) * width
    acc = jnp.zeros((2 * features, width), f32)
    for g in range(n // group):
        local = local_ref[g]
        column = first + lax.broadcasted_iota(jnp.int32, local.shape, 1)
        marks = jnp.concatenate(
            [
                jnp.where(local == column + t * lanes, 1.0, 0.0).astype(bf16)
                for t in range(width // lanes)
            ],
            axis=1,
        )
        acc = acc + dot(scaled_ref[g], marks)
    pool_ref[...] = acc[:features] + acc[features:]


def per_device(question_matrix, document_matrix, pool, hard_owner, hard_local):
    n, depth = lax.axis_size("blk"), lax.axis_size("dim")
    rows, features = question_matrix.shape
    columns = pool.shape[1]
    me = lax.axis_index("blk")
    smem = pl.BlockSpec(memory_space=pltpu.SMEM)
    vmem = pl.BlockSpec(memory_space=pltpu.VMEM)
    block = shape(features + SLACK, rows)
    line = Line()

    def full(*dims):
        return pl.BlockSpec(dims, lambda i: (0,) * len(dims))

    def send(x, mask):
        return lax.ppermute(x, "blk", [(i, i ^ mask) for i in range(n)])

    far = n // 4
    x, x_arrays, x_place = {}, [], {}

    def keep(array, *blocks):
        for k, r in enumerate(blocks):
            x[r] = array
            x_place[r] = (len(x_arrays), k if array.ndim == 3 else None)
        x_arrays.append(array)

    def pass_on(array):
        return line(lambda a, out: out.__setitem__(..., a[...]), block, "relay", [array], 0.05)

    def relay(r):
        x_arrays[x_place[r][0]] = x[r] = pass_on(x[r])

    def forward(k):
        relay(4 * k)
        if k % 2 == 0 and k + 1 < far:
            keep(send(x[4 * k], 4), 4 * k + 4)
        keep(send(x[4 * k], 2), 4 * k + 2)

    def share(*blocks):
        for r in blocks:
            keep(send(x[r], 1), r + 1)

    def share_all(*blocks):
        out = shape(len(blocks), features + SLACK, rows)
        held = line(relay_body, out, "relay", [x[r] for r in blocks], 0.05)
        keep(send(held, 1), *[r + 1 for r in blocks])

    weights, sums, e_place = [], {}, {}
    waiting, stage = [], {}

    held = []

    def score(blocks, hold=False):
        early = held.pop() if held else ([], ())
        k = len(blocks) + len(early[0])
        used = sorted({x_place[r][0] for r in blocks})
        part, found = line(
            functools.partial(
                score_body,
                [(used.index(x_place[r][0]), x_place[r][1]) for r in blocks],
                len(early[0]),
            ),
            (shape(k, rows + SLACK, rows), shape(k, features, rows)),
            "score",
            [me.reshape(1), document_matrix, pool] + [x_arrays[i] for i in used] + [*early[1]],
            0.9 * len(blocks),
            [smem] + [vmem] * (2 + len(used) + len(early[1])),
        )
        blocks = [r for r in blocks + early[0] if r % 2 == 0] + [
            r for r in blocks + early[0] if r % 2
        ]
        if hold:
            held.append((blocks, (part, found)))
            return
        got = [
            lax.ppermute(part, "dim", [(i, (i + s) % depth) for i in range(depth)])
            for s in range(1, depth)
        ]
        waiting.append((blocks, part, found, got))

    def softmax():
        blocks, part, found, got = waiting.pop(0)
        k = len(blocks)
        odds = [r for r in blocks if r % 2]
        evens = k - len(odds)
        stacked = False
        e, *out = line(
            functools.partial(softmax_body, evens if stacked else k, len(got)),
            [shape(k, rows + SLACK, rows)]
            + [block] * (evens if stacked else k)
            + [shape(len(odds), features + SLACK, rows)] * stacked,
            "softmax",
            [dt, found, part, *got],
            0.25 * k,
        )
        for i, r in enumerate(blocks):
            e_place[r] = (len(weights), i)
        weights.append(e)
        for r, array in zip(blocks, out[:evens]):
            sums[r] = (array, None)
        shared = send(out[-1], 1) if stacked else None
        for i, r in enumerate(odds):
            sums[r] = (shared, i) if stacked else (send(out[evens + i], 1), None)

    over_x, home = {}, []

    def add(*terms):
        arrays = [array for array, k in terms]
        places = [k for array, k in terms]
        return line(functools.partial(merge_body, places), block, "merge", arrays, 0.05)

    def pair(*blocks):
        for r in blocks:
            sums[r] = (add(sums[r], sums[r + 1]), None)

    def beside(k):
        over_x[k] = (send(sums[4 * k + 2][0], 2), None)

    def beside_all(*blocks):
        arrays, places = [], []
        for terms in blocks:
            places.append([(len(arrays) + i, sums[r][1]) for i, r in enumerate(terms)])
            arrays += [sums[r][0] for r in terms]
        out = shape(len(blocks), features + SLACK, rows)
        held = line(functools.partial(merge_all_body, places), out, "merge", arrays, 0.1)
        shared = send(held, 2)
        for i, terms in enumerate(blocks):
            over_x[terms[0] // 4] = (shared, i)

    def inward(k):
        whole = add(sums[4 * k], over_x[k])
        home.append(send(whole, 4 * k) if k else whole)

    packed = line(
        functools.partial(pack_body, columns),
        block,
        "pack",
        [question_matrix, hard_owner.T, hard_local.T],
        1.8,
        [pl.BlockSpec(memory_space=pltpu.HBM)] * 3,
        limit=62,
        scratch_shapes=[
            pltpu.VMEM(question_matrix.shape, f32),
            pltpu.VMEM(hard_owner.shape[::-1], jnp.int32),
            pltpu.VMEM(hard_local.shape[::-1], jnp.int32),
            pltpu.SemaphoreType.DMA((3,)),
        ],
    )
    keep(packed, 0)
    for k in [2, 1] + [k for k in range(4, far) if k % 2 == 0]:
        keep(send(packed, 4 * k), 4 * k)
    keep(send(packed, 2), 2)
    keep(send(packed, 1), 1)
    line.last = None
    dt = line(flip_body, shape(features, rows), "flip", [document_matrix], 0.1)
    score([0, 1], hold=True)
    forward(2)
    forward(1)
    relay(2)
    share_all(2, 4, 8)
    score([2, 4, 8])
    relay(10)
    forward(3)
    score([3, 5, 9])
    relay(6)
    share(10, 6)
    score([10, 6, 11, 7])
    softmax()
    relay(14)
    share(12, 14)
    softmax()
    for k in range(3, far):
        if k + 1 < far:
            forward(k + 1)
        score([4 * k, 4 * k + 2, 4 * k + 1, 4 * k + 3])
        if k + 1 < far:
            relay(4 * k + 6)
            share(4 * k + 4, 4 * k + 6)
        if k == 3:
            pair(0, 2, 4, 8)
            beside(0)
        softmax()
        if k == 3:
            beside_all((10, 11), (6, 7))
        else:
            pair(4 * k - 2, 4 * k - 4)
            beside(k - 1)
    softmax()
    over_x[0] = (pass_on(over_x[0][0]), None)

    totals = line(
        functools.partial(stats_body, [e_place[r] for r in range(n)]),
        shape(2, n, rows),
        "stats",
        weights,
        0.05,
        [
            pl.BlockSpec((e.shape[0], SLACK, rows), lambda i: (0, rows // SLACK, 0))
            for e in weights
        ],
        grid=(1,),
        out_specs=full(2, n, rows),
    )
    masks = [1] + [4 << i for i in reversed(range(far.bit_length() - 1))] + [2]
    for mask in masks:
        there = send(totals, mask)
        if mask == 2:
            pair(4 * far - 4)
            inward(2)
            inward(1)
        totals = line(
            functools.partial(stats_merge_body, [mask]),
            shape(2, n, rows),
            "stats_merge",
            [totals, there],
            0.05,
        )
        if mask == 1:
            pair(4 * far - 2)
            beside(far - 1)
    for k in range(3, far):
        inward(k)

    group = 4
    width = 512
    e_at = 1 + len(x_arrays)
    document_derivative, grad_pool = line(
        functools.partial(
            gradient_body,
            [(x_place[r][0] + 1, x_place[r][1]) for r in range(n)],
            [(e_at + e_place[r][0], e_place[r][1]) for r in range(n)],
            group,
        ),
        (shape(rows, features), shape(features, columns)),
        "gradient",
        [totals, *x_arrays, *weights],
        11.0,
        limit=48,
        grid=(columns // width,),
        out_specs=(full(rows, features), pl.BlockSpec((features, width), lambda i: (0, i))),
        scratch_shapes=[
            pltpu.VMEM((n // group, 2 * features, group * rows), bf16),
            pltpu.VMEM((n // group, group * rows, 128), jnp.int32),
        ],
    )

    line.last = totals
    inward(0)
    arrays = home
    question_derivative, loss = line(
        last_body,
        (shape(rows, features), shape(rows)),
        "finish",
        [document_matrix, weights[e_place[0][0]], *arrays],
        0.8,
        [full(rows, features)]
        + [pl.BlockSpec((1, SLACK, rows), lambda i: (e_place[0][1], rows // SLACK, 0))]
        + [full(*a.shape) for a in arrays],
        grid=(1,),
        out_specs=(full(rows, features), full(rows)),
    )
    return loss, question_derivative, document_derivative, grad_pool


def solution(mesh):
    placed = (P("blk", "dim"), P("blk", "dim"), P("dim", "blk"), P("blk", None), P("blk", None))
    return jax.shard_map(
        per_device,
        mesh=mesh,
        in_specs=placed,
        out_specs=(P("blk"), P("blk", "dim"), P("blk", "dim"), P("dim", "blk")),
        check_vma=False,
    )
```

```python
import functools

import jax
import jax.numpy as jnp
from jax import lax
from jax.experimental import pallas as pl
from jax.experimental.pallas import tpu as pltpu
from jax.sharding import PartitionSpec as P

logit_divisor = 0.05
LOWEST = -3.0e38
COST = 3.7e6
SLACK = 8

f32 = jnp.float32
bf16 = jnp.bfloat16


def split2(x):
    high = x.astype(bf16)
    return high, (x - high.astype(f32)).astype(bf16)


def dot(a, b, contract=((1,), (0,)), precision=None):
    return lax.dot_general(
        a, b, (contract, ((), ())), precision=precision, preferred_element_type=f32
    )


class Line:
    def __init__(self):
        self.last = None

    def __call__(self, body, out_shape, name, arrays, us, in_specs=None, limit=16, **kw):
        count = len(arrays)
        if in_specs is None:
            in_specs = [pl.BlockSpec(memory_space=pltpu.VMEM)] * count
        if self.last is not None:
            in_specs = list(in_specs) + [pl.BlockSpec(memory_space=pl.ANY)]
            arrays = list(arrays) + [self.last]

        def kernel(*refs):
            body(*refs[:count], *refs[len(arrays) :])

        out = pl.pallas_call(
            kernel,
            out_shape=out_shape,
            name=name,
            in_specs=in_specs,
            cost_estimate=pl.CostEstimate(
                flops=0, bytes_accessed=int(us * COST), transcendentals=0
            ),
            compiler_params=pltpu.CompilerParams(vmem_limit_bytes=limit << 20),
            **kw,
        )(*arrays)
        self.last = out[-1] if isinstance(out, (list, tuple)) else out
        return out


def shape(*dims, dtype=f32):
    return jax.ShapeDtypeStruct(dims, dtype)


def pack_body(columns, q_hbm, owner_hbm, local_hbm, x_ref, q_ref, owner_ref, local_ref, sems):
    pairs = ((q_hbm, q_ref), (owner_hbm, owner_ref), (local_hbm, local_ref))
    copies = [pltpu.make_async_copy(a, b, sems.at[i]) for i, (a, b) in enumerate(pairs)]
    for copy in copies:
        copy.start()
    for copy in copies:
        copy.wait()
    features = q_ref.shape[1]
    x_ref[:features, :] = q_ref[...].T
    x_ref[features:, :] = (owner_ref[...] * columns + local_ref[...]).astype(f32)


def relay_body(*refs):
    for k, ref in enumerate(refs[:-1]):
        refs[-1][k] = ref[...]


def flip_body(d_ref, dt_ref):
    dt_ref[...] = d_ref[...].T


def score_body(places, early, me_ref, d_ref, pool_ref, *refs):
    part_ref, rows_ref = refs[-2:]
    if early:
        early_part_ref, early_rows_ref = refs[-4:-2]
        part_ref[len(places) :] = early_part_ref[...]
        rows_ref[len(places) :] = early_rows_ref[...]
    rows, features = d_ref.shape
    columns = pool_ref.shape[1]
    tile = 128
    blocks = [refs[a][...] if k is None else refs[a][k] for a, k in places]
    for k, block in enumerate(blocks):
        x = block[:features]
        named = block[features:].astype(jnp.int32) - me_ref[0] * columns
        here = (named >= 0) & (named < columns)
        local = jnp.sum(jnp.where(here, named, 0), axis=0, keepdims=True)
        owned = jnp.any(here, axis=0, keepdims=True)
        lane = jnp.broadcast_to(local % tile, (features, rows))
        found = jnp.zeros((features, rows), f32)
        for t in range(columns // tile):
            picked = jnp.take_along_axis(
                pool_ref[:, t * tile : (t + 1) * tile], lane, axis=1, mode="promise_in_bounds"
            )
            found = jnp.where(local // tile == t, picked, found)
        rows_ref[k] = found
        hard = jnp.sum(x * found, axis=0, keepdims=True)
        chosen = jnp.where(owned, local, -1).astype(f32)
        part_ref[k, rows:] = jnp.concatenate(
            [hard, chosen, jnp.zeros((SLACK - 2, rows), f32)], axis=0
        )
    x = [block[:features] for block in blocks]
    x = x[0] if len(x) == 1 else jnp.concatenate(x, axis=1)
    scores = dot(d_ref[...], x, precision=lax.Precision.HIGHEST)
    for k in range(len(blocks)):
        part_ref[k, :rows] = scores[:, k * rows : (k + 1) * rows]


def softmax_body(evens, others, dt_ref, rows_ref, part_ref, *refs):
    got, (e_ref, *sum_refs) = refs[:others], refs[others:]
    features, rows = dt_ref.shape
    count = part_ref.shape[0]
    own = lax.broadcasted_iota(jnp.int32, (rows, rows), 0) == lax.broadcasted_iota(
        jnp.int32, (rows, rows), 1
    )
    tails, es = [], []
    for k in range(count):
        whole = part_ref[k]
        chosen = whole[rows + 1 : rows + 2]
        for r in got:
            whole = whole + r[k]
        scores = whole[:rows] / logit_divisor
        hard = jnp.where(chosen >= 0, whole[rows : rows + 1] / logit_divisor, LOWEST)
        peak = jnp.maximum(jnp.max(scores, axis=0, keepdims=True), hard)
        e = jnp.exp(scores - peak)
        hard_e = jnp.where(chosen >= 0, jnp.exp(hard - peak), 0.0)
        total = jnp.sum(e, axis=0, keepdims=True) + hard_e
        positive = jnp.sum(jnp.where(own, scores, 0.0), axis=0, keepdims=True)
        e_ref[k, :rows] = e
        e_ref[k, rows:] = jnp.concatenate(
            [hard_e, chosen, peak, total, positive, jnp.zeros((SLACK - 5, rows), f32)], axis=0
        )
        es.append(e)
        tails.append((hard_e, peak, total))
    e = es[0] if count == 1 else jnp.concatenate(es, axis=1)
    sums = dot(dt_ref[...], e, precision=lax.Precision.HIGHEST)
    for k, (hard_e, peak, total) in enumerate(tails):
        at = sum_refs[k] if k < evens else sum_refs[-1].at[k - evens]
        at[:features] = sums[:, k * rows : (k + 1) * rows] + rows_ref[k] * hard_e
        at[features:] = jnp.concatenate([peak, total, jnp.zeros((SLACK - 2, rows), f32)], axis=0)


def merge(terms):
    size = terms[0].shape[0] - SLACK
    peaks = [t[size : size + 1] for t in terms]
    peak = functools.reduce(jnp.maximum, peaks)
    scales = [jnp.exp(p - peak) for p in peaks]
    sums = functools.reduce(jnp.add, [t[:size] * s for t, s in zip(terms, scales)])
    total = functools.reduce(
        jnp.add, [t[size + 1 : size + 2] * s for t, s in zip(terms, scales)]
    )
    return sums, peak, total


def merge_body(places, *refs):
    out_ref = refs[-1]
    sums, peak, total = merge([r[...] if k is None else r[k] for r, k in zip(refs, places)])
    size = sums.shape[0]
    out_ref[:size] = sums
    out_ref[size:] = jnp.concatenate(
        [peak, total, jnp.zeros((SLACK - 2, peak.shape[1]), f32)], axis=0
    )


def merge_all_body(places, *refs):
    out_ref = refs[-1]
    size = out_ref.shape[1] - SLACK
    for slot, terms in enumerate(places):
        terms = [refs[i][...] if k is None else refs[i][k] for i, k in terms]
        if len(terms) == 1:
            out_ref[slot] = terms[0]
        else:
            sums, peak, total = merge(terms)
            out_ref[slot, :size] = sums
            out_ref[slot, size:] = jnp.concatenate(
                [peak, total, jnp.zeros((SLACK - 2, peak.shape[1]), f32)], axis=0
            )


def last_body(d_ref, e_ref, *refs):
    dq_ref, loss_ref = refs[-2:]
    sums, peak, total = merge([ref[...] for ref in refs[:-2]])
    dq_ref[...] = ((sums / total).T - d_ref[...]) / logit_divisor
    log_total = peak + jnp.log(total)
    loss_ref[...] = (log_total - e_ref[0, 4:5]).reshape(loss_ref.shape)


def stats_body(places, *refs):
    out_ref = refs[-1]
    for r, (i, k) in enumerate(places):
        out_ref[0, r : r + 1] = refs[i][k, 2:3]
        out_ref[1, r : r + 1] = refs[i][k, 3:4]


def stats_merge_body(masks, own_ref, *refs):
    out_ref = refs[-1]
    n = own_ref.shape[1]
    peaks, totals = [own_ref[0]], [own_ref[1]]
    for ref, mask in zip(refs, masks):
        for values, into in ((ref[0], peaks), (ref[1], totals)):
            into.append(
                jnp.concatenate([values[r ^ mask : (r ^ mask) + 1] for r in range(n)], axis=0)
            )
    peak = functools.reduce(jnp.maximum, peaks)
    out_ref[0] = peak
    out_ref[1] = functools.reduce(
        jnp.add, [t * jnp.exp(p - peak) for p, t in zip(peaks, totals)]
    )


def gradient_body(x_places, e_places, group, *refs):
    n = len(x_places)
    tot_ref = refs[0]
    dd_ref, pool_ref, scaled_ref, local_ref = refs[-4:]
    rows, features = dd_ref.shape
    lanes = local_ref.shape[-1]

    @pl.when(pl.program_id(0) == 0)
    def _():
        own = lax.broadcasted_iota(jnp.int32, (rows, rows), 0) == lax.broadcasted_iota(
            jnp.int32, (rows, rows), 1
        )
        total = jnp.zeros((features, rows), f32)
        for g in range(n // group):
            xs, es, hards = [], [], []
            for r in range(g * group, (g + 1) * group):
                i, k = x_places[r]
                xs.append(refs[i][:features] if k is None else refs[i][k, :features])
                i, k = e_places[r]
                scale = jnp.exp(refs[i][k, rows + 2 : rows + 3] - tot_ref[0, r : r + 1])
                scale = scale / tot_ref[1, r : r + 1]
                e = refs[i][k, :rows] * scale
                es.append(e if r else jnp.where(own, e - 1.0, e))
                hards.append(refs[i][k, rows : rows + 1] * scale)
                chosen = jnp.broadcast_to(refs[i][k, rows + 1 : rows + 2], (lanes, rows))
                first = (r - g * group) * rows
                local_ref[g, first : first + rows] = chosen.T.astype(jnp.int32)
            x = jnp.concatenate(xs, axis=1)
            chance = jnp.concatenate(es, axis=1)
            high, low = split2(x)
            c_high, c_low = split2(chance)
            both = dot(jnp.concatenate([high, low], axis=0), c_high, ((1,), (1,)))
            total = total + both[:features] + both[features:]
            total = total + dot(high, c_low, ((1,), (1,)))
            high, low = split2(x * (jnp.concatenate(hards, axis=1) / logit_divisor))
            scaled_ref[g, :features] = high
            scaled_ref[g, features:] = low
        dd_ref[...] = total.T / logit_divisor

    width = pool_ref.shape[1]
    first = pl.program_id(0) * width
    acc = jnp.zeros((2 * features, width), f32)
    for g in range(n // group):
        local = local_ref[g]
        column = first + lax.broadcasted_iota(jnp.int32, local.shape, 1)
        marks = jnp.concatenate(
            [
                jnp.where(local == column + t * lanes, 1.0, 0.0).astype(bf16)
                for t in range(width // lanes)
            ],
            axis=1,
        )
        acc = acc + dot(scaled_ref[g], marks)
    pool_ref[...] = acc[:features] + acc[features:]


def per_device(question_matrix, document_matrix, pool, hard_owner, hard_local):
    n, depth = lax.axis_size("blk"), lax.axis_size("dim")
    rows, features = question_matrix.shape
    columns = pool.shape[1]
    me = lax.axis_index("blk")
    smem = pl.BlockSpec(memory_space=pltpu.SMEM)
    vmem = pl.BlockSpec(memory_space=pltpu.VMEM)
    block = shape(features + SLACK, rows)
    line = Line()

    def full(*dims):
        return pl.BlockSpec(dims, lambda i: (0,) * len(dims))

    def send(x, mask):
        return lax.ppermute(x, "blk", [(i, i ^ mask) for i in range(n)])

    far = n // 4
    x, x_arrays, x_place = {}, [], {}

    def keep(array, *blocks):
        for k, r in enumerate(blocks):
            x[r] = array
            x_place[r] = (len(x_arrays), k if array.ndim == 3 else None)
        x_arrays.append(array)

    def pass_on(array):
        return line(lambda a, out: out.__setitem__(..., a[...]), block, "relay", [array], 0.05)

    def relay(r):
        x_arrays[x_place[r][0]] = x[r] = pass_on(x[r])

    def forward(k):
        relay(4 * k)
        if k % 2 == 0 and k + 1 < far:
            keep(send(x[4 * k], 4), 4 * k + 4)
        keep(send(x[4 * k], 2), 4 * k + 2)

    def share(*blocks):
        for r in blocks:
            keep(send(x[r], 1), r + 1)

    def share_all(*blocks):
        out = shape(len(blocks), features + SLACK, rows)
        held = line(relay_body, out, "relay", [x[r] for r in blocks], 0.05)
        keep(send(held, 1), *[r + 1 for r in blocks])

    weights, sums, e_place = [], {}, {}
    waiting, stage = [], {}

    held = []

    def score(blocks, hold=False):
        early = held.pop() if held else ([], ())
        k = len(blocks) + len(early[0])
        used = sorted({x_place[r][0] for r in blocks})
        part, found = line(
            functools.partial(
                score_body,
                [(used.index(x_place[r][0]), x_place[r][1]) for r in blocks],
                len(early[0]),
            ),
            (shape(k, rows + SLACK, rows), shape(k, features, rows)),
            "score",
            [me.reshape(1), document_matrix, pool] + [x_arrays[i] for i in used] + [*early[1]],
            0.9 * len(blocks),
            [smem] + [vmem] * (2 + len(used) + len(early[1])),
        )
        blocks = [r for r in blocks + early[0] if r % 2 == 0] + [
            r for r in blocks + early[0] if r % 2
        ]
        if hold:
            held.append((blocks, (part, found)))
            return
        got = [
            lax.ppermute(part, "dim", [(i, (i + s) % depth) for i in range(depth)])
            for s in range(1, depth)
        ]
        waiting.append((blocks, part, found, got))

    def softmax():
        blocks, part, found, got = waiting.pop(0)
        k = len(blocks)
        odds = [r for r in blocks if r % 2]
        evens = k - len(odds)
        stacked = False
        e, *out = line(
            functools.partial(softmax_body, evens if stacked else k, len(got)),
            [shape(k, rows + SLACK, rows)]
            + [block] * (evens if stacked else k)
            + [shape(len(odds), features + SLACK, rows)] * stacked,
            "softmax",
            [dt, found, part, *got],
            0.25 * k,
        )
        for i, r in enumerate(blocks):
            e_place[r] = (len(weights), i)
        weights.append(e)
        for r, array in zip(blocks, out[:evens]):
            sums[r] = (array, None)
        shared = send(out[-1], 1) if stacked else None
        for i, r in enumerate(odds):
            sums[r] = (shared, i) if stacked else (send(out[evens + i], 1), None)

    over_x, home = {}, []

    def add(*terms):
        arrays = [array for array, k in terms]
        places = [k for array, k in terms]
        return line(functools.partial(merge_body, places), block, "merge", arrays, 0.05)

    def pair(*blocks):
        for r in blocks:
            sums[r] = (add(sums[r], sums[r + 1]), None)

    def beside(k):
        over_x[k] = (send(sums[4 * k + 2][0], 2), None)

    def beside_all(*blocks):
        arrays, places = [], []
        for terms in blocks:
            places.append([(len(arrays) + i, sums[r][1]) for i, r in enumerate(terms)])
            arrays += [sums[r][0] for r in terms]
        out = shape(len(blocks), features + SLACK, rows)
        held = line(functools.partial(merge_all_body, places), out, "merge", arrays, 0.1)
        shared = send(held, 2)
        for i, terms in enumerate(blocks):
            over_x[terms[0] // 4] = (shared, i)

    def inward(k):
        whole = add(sums[4 * k], over_x[k])
        home.append(send(whole, 4 * k) if k else whole)

    packed = line(
        functools.partial(pack_body, columns),
        block,
        "pack",
        [question_matrix, hard_owner.T, hard_local.T],
        1.8,
        [pl.BlockSpec(memory_space=pltpu.HBM)] * 3,
        limit=62,
        scratch_shapes=[
            pltpu.VMEM(question_matrix.shape, f32),
            pltpu.VMEM(hard_owner.shape[::-1], jnp.int32),
            pltpu.VMEM(hard_local.shape[::-1], jnp.int32),
            pltpu.SemaphoreType.DMA((3,)),
        ],
    )
    keep(packed, 0)
    for k in [2, 1] + [k for k in range(4, far) if k % 2 == 0]:
        keep(send(packed, 4 * k), 4 * k)
    keep(send(packed, 2), 2)
    keep(send(packed, 1), 1)
    line.last = None
    dt = line(flip_body, shape(features, rows), "flip", [document_matrix], 0.1)
    score([0, 1], hold=True)
    forward(2)
    forward(1)
    relay(2)
    share_all(2, 4, 8)
    score([2, 4, 8])
    relay(10)
    forward(3)
    score([3, 5, 9])
    relay(6)
    share(10, 6)
    score([10, 6, 11, 7])
    softmax()
    relay(14)
    share(12, 14)
    softmax()
    for k in range(3, far):
        if k + 1 < far:
            forward(k + 1)
        score([4 * k, 4 * k + 2, 4 * k + 1, 4 * k + 3])
        if k + 1 < far:
            relay(4 * k + 6)
            share(4 * k + 4, 4 * k + 6)
        if k == 3:
            pair(0, 2, 4, 8)
            beside(0)
        softmax()
        if k == 3:
            beside_all((10, 11), (6, 7))
        else:
            pair(4 * k - 2, 4 * k - 4)
            beside(k - 1)
    softmax()

    totals = line(
        functools.partial(stats_body, [e_place[r] for r in range(n)]),
        shape(2, n, rows),
        "stats",
        weights,
        0.05,
        [
            pl.BlockSpec((e.shape[0], SLACK, rows), lambda i: (0, rows // SLACK, 0))
            for e in weights
        ],
        grid=(1,),
        out_specs=full(2, n, rows),
    )
    masks = [1] + [4 << i for i in reversed(range(far.bit_length() - 1))] + [2]
    for mask in masks:
        there = send(totals, mask)
        if mask == 2:
            pair(4 * far - 4)
            inward(2)
            inward(1)
        totals = line(
            functools.partial(stats_merge_body, [mask]),
            shape(2, n, rows),
            "stats_merge",
            [totals, there],
            0.05,
        )
        if mask == 1:
            over_x[0] = (pass_on(over_x[0][0]), None)
            pair(4 * far - 2)
            beside(far - 1)
    for k in range(3, far):
        inward(k)

    group = 4
    width = 512
    e_at = 1 + len(x_arrays)
    document_derivative, grad_pool = line(
        functools.partial(
            gradient_body,
            [(x_place[r][0] + 1, x_place[r][1]) for r in range(n)],
            [(e_at + e_place[r][0], e_place[r][1]) for r in range(n)],
            group,
        ),
        (shape(rows, features), shape(features, columns)),
        "gradient",
        [totals, *x_arrays, *weights],
        11.0,
        limit=48,
        grid=(columns // width,),
        out_specs=(full(rows, features), pl.BlockSpec((features, width), lambda i: (0, i))),
        scratch_shapes=[
            pltpu.VMEM((n // group, 2 * features, group * rows), bf16),
            pltpu.VMEM((n // group, group * rows, 128), jnp.int32),
        ],
    )

    line.last = totals
    inward(0)
    arrays = home
    question_derivative, loss = line(
        last_body,
        (shape(rows, features), shape(rows)),
        "finish",
        [document_matrix, weights[e_place[0][0]], *arrays],
        0.8,
        [full(rows, features)]
        + [pl.BlockSpec((1, SLACK, rows), lambda i: (e_place[0][1], rows // SLACK, 0))]
        + [full(*a.shape) for a in arrays],
        grid=(1,),
        out_specs=(full(rows, features), full(rows)),
    )
    return loss, question_derivative, document_derivative, grad_pool


def solution(mesh):
    placed = (P("blk", "dim"), P("blk", "dim"), P("dim", "blk"), P("blk", None), P("blk", None))
    return jax.shard_map(
        per_device,
        mesh=mesh,
        in_specs=placed,
        out_specs=(P("blk"), P("blk", "dim"), P("blk", "dim"), P("dim", "blk")),
        check_vma=False,
    )
```

```python
import functools

import jax
import jax.numpy as jnp
from jax import lax
from jax.experimental import pallas as pl
from jax.experimental.pallas import tpu as pltpu
from jax.sharding import PartitionSpec as P

logit_divisor = 0.05
LOWEST = -3.0e38
COST = 3.7e6
SLACK = 8

f32 = jnp.float32
bf16 = jnp.bfloat16


def split2(x):
    high = x.astype(bf16)
    return high, (x - high.astype(f32)).astype(bf16)


def dot(a, b, contract=((1,), (0,)), precision=None):
    return lax.dot_general(
        a, b, (contract, ((), ())), precision=precision, preferred_element_type=f32
    )


class Line:
    def __init__(self):
        self.last = None

    def __call__(self, body, out_shape, name, arrays, us, in_specs=None, limit=16, **kw):
        count = len(arrays)
        if in_specs is None:
            in_specs = [pl.BlockSpec(memory_space=pltpu.VMEM)] * count
        if self.last is not None:
            in_specs = list(in_specs) + [pl.BlockSpec(memory_space=pl.ANY)]
            arrays = list(arrays) + [self.last]

        def kernel(*refs):
            body(*refs[:count], *refs[len(arrays) :])

        out = pl.pallas_call(
            kernel,
            out_shape=out_shape,
            name=name,
            in_specs=in_specs,
            cost_estimate=pl.CostEstimate(
                flops=0, bytes_accessed=int(us * COST), transcendentals=0
            ),
            compiler_params=pltpu.CompilerParams(vmem_limit_bytes=limit << 20),
            **kw,
        )(*arrays)
        self.last = out[-1] if isinstance(out, (list, tuple)) else out
        return out


def shape(*dims, dtype=f32):
    return jax.ShapeDtypeStruct(dims, dtype)


def pack_body(columns, q_hbm, owner_hbm, local_hbm, x_ref, q_ref, owner_ref, local_ref, sems):
    pairs = ((q_hbm, q_ref), (owner_hbm, owner_ref), (local_hbm, local_ref))
    copies = [pltpu.make_async_copy(a, b, sems.at[i]) for i, (a, b) in enumerate(pairs)]
    for copy in copies:
        copy.start()
    for copy in copies:
        copy.wait()
    features = q_ref.shape[1]
    x_ref[:features, :] = q_ref[...].T
    x_ref[features:, :] = (owner_ref[...] * columns + local_ref[...]).astype(f32)


def relay_body(*refs):
    for k, ref in enumerate(refs[:-1]):
        refs[-1][k] = ref[...]


def flip_body(d_ref, dt_ref):
    dt_ref[...] = d_ref[...].T


def score_body(places, early, me_ref, d_ref, pool_ref, *refs):
    part_ref, rows_ref = refs[-2:]
    if early:
        early_part_ref, early_rows_ref = refs[-4:-2]
        part_ref[len(places) :] = early_part_ref[...]
        rows_ref[len(places) :] = early_rows_ref[...]
    rows, features = d_ref.shape
    columns = pool_ref.shape[1]
    tile = 128
    blocks = [refs[a][...] if k is None else refs[a][k] for a, k in places]
    for k, block in enumerate(blocks):
        x = block[:features]
        named = block[features:].astype(jnp.int32) - me_ref[0] * columns
        here = (named >= 0) & (named < columns)
        local = jnp.sum(jnp.where(here, named, 0), axis=0, keepdims=True)
        owned = jnp.any(here, axis=0, keepdims=True)
        lane = jnp.broadcast_to(local % tile, (features, rows))
        found = jnp.zeros((features, rows), f32)
        for t in range(columns // tile):
            picked = jnp.take_along_axis(
                pool_ref[:, t * tile : (t + 1) * tile], lane, axis=1, mode="promise_in_bounds"
            )
            found = jnp.where(local // tile == t, picked, found)
        rows_ref[k] = found
        hard = jnp.sum(x * found, axis=0, keepdims=True)
        chosen = jnp.where(owned, local, -1).astype(f32)
        part_ref[k, rows:] = jnp.concatenate(
            [hard, chosen, jnp.zeros((SLACK - 2, rows), f32)], axis=0
        )
    x = [block[:features] for block in blocks]
    x = x[0] if len(x) == 1 else jnp.concatenate(x, axis=1)
    scores = dot(d_ref[...], x, precision=lax.Precision.HIGHEST)
    for k in range(len(blocks)):
        part_ref[k, :rows] = scores[:, k * rows : (k + 1) * rows]


def softmax_body(evens, others, dt_ref, rows_ref, part_ref, *refs):
    got, (e_ref, *sum_refs) = refs[:others], refs[others:]
    features, rows = dt_ref.shape
    count = part_ref.shape[0]
    own = lax.broadcasted_iota(jnp.int32, (rows, rows), 0) == lax.broadcasted_iota(
        jnp.int32, (rows, rows), 1
    )
    tails, es = [], []
    for k in range(count):
        whole = part_ref[k]
        chosen = whole[rows + 1 : rows + 2]
        for r in got:
            whole = whole + r[k]
        scores = whole[:rows] / logit_divisor
        hard = jnp.where(chosen >= 0, whole[rows : rows + 1] / logit_divisor, LOWEST)
        peak = jnp.maximum(jnp.max(scores, axis=0, keepdims=True), hard)
        e = jnp.exp(scores - peak)
        hard_e = jnp.where(chosen >= 0, jnp.exp(hard - peak), 0.0)
        total = jnp.sum(e, axis=0, keepdims=True) + hard_e
        positive = jnp.sum(jnp.where(own, scores, 0.0), axis=0, keepdims=True)
        e_ref[k, :rows] = e
        e_ref[k, rows:] = jnp.concatenate(
            [hard_e, chosen, peak, total, positive, jnp.zeros((SLACK - 5, rows), f32)], axis=0
        )
        es.append(e)
        tails.append((hard_e, peak, total))
    e = es[0] if count == 1 else jnp.concatenate(es, axis=1)
    sums = dot(dt_ref[...], e, precision=lax.Precision.HIGHEST)
    for k, (hard_e, peak, total) in enumerate(tails):
        at = sum_refs[k] if k < evens else sum_refs[-1].at[k - evens]
        at[:features] = sums[:, k * rows : (k + 1) * rows] + rows_ref[k] * hard_e
        at[features:] = jnp.concatenate([peak, total, jnp.zeros((SLACK - 2, rows), f32)], axis=0)


def merge(terms):
    size = terms[0].shape[0] - SLACK
    peaks = [t[size : size + 1] for t in terms]
    peak = functools.reduce(jnp.maximum, peaks)
    scales = [jnp.exp(p - peak) for p in peaks]
    sums = functools.reduce(jnp.add, [t[:size] * s for t, s in zip(terms, scales)])
    total = functools.reduce(
        jnp.add, [t[size + 1 : size + 2] * s for t, s in zip(terms, scales)]
    )
    return sums, peak, total


def merge_body(places, *refs):
    out_ref = refs[-1]
    sums, peak, total = merge([r[...] if k is None else r[k] for r, k in zip(refs, places)])
    size = sums.shape[0]
    out_ref[:size] = sums
    out_ref[size:] = jnp.concatenate(
        [peak, total, jnp.zeros((SLACK - 2, peak.shape[1]), f32)], axis=0
    )


def merge_all_body(places, *refs):
    out_ref = refs[-1]
    size = out_ref.shape[1] - SLACK
    for slot, terms in enumerate(places):
        terms = [refs[i][...] if k is None else refs[i][k] for i, k in terms]
        if len(terms) == 1:
            out_ref[slot] = terms[0]
        else:
            sums, peak, total = merge(terms)
            out_ref[slot, :size] = sums
            out_ref[slot, size:] = jnp.concatenate(
                [peak, total, jnp.zeros((SLACK - 2, peak.shape[1]), f32)], axis=0
            )


def last_body(d_ref, e_ref, *refs):
    dq_ref, loss_ref = refs[-2:]
    sums, peak, total = merge([ref[...] for ref in refs[:-2]])
    dq_ref[...] = ((sums / total).T - d_ref[...]) / logit_divisor
    log_total = peak + jnp.log(total)
    loss_ref[...] = (log_total - e_ref[0, 4:5]).reshape(loss_ref.shape)


def stats_body(places, *refs):
    out_ref = refs[-1]
    for r, (i, k) in enumerate(places):
        out_ref[0, r : r + 1] = refs[i][k, 2:3]
        out_ref[1, r : r + 1] = refs[i][k, 3:4]


def stats_merge_body(masks, own_ref, *refs):
    out_ref = refs[-1]
    n = own_ref.shape[1]
    peaks, totals = [own_ref[0]], [own_ref[1]]
    for ref, mask in zip(refs, masks):
        for values, into in ((ref[0], peaks), (ref[1], totals)):
            into.append(
                jnp.concatenate([values[r ^ mask : (r ^ mask) + 1] for r in range(n)], axis=0)
            )
    peak = functools.reduce(jnp.maximum, peaks)
    out_ref[0] = peak
    out_ref[1] = functools.reduce(
        jnp.add, [t * jnp.exp(p - peak) for p, t in zip(peaks, totals)]
    )


def gradient_body(x_places, e_places, group, *refs):
    n = len(x_places)
    tot_ref = refs[0]
    dd_ref, pool_ref, scaled_ref, local_ref = refs[-4:]
    rows, features = dd_ref.shape
    lanes = local_ref.shape[-1]

    @pl.when(pl.program_id(0) == 0)
    def _():
        own = lax.broadcasted_iota(jnp.int32, (rows, rows), 0) == lax.broadcasted_iota(
            jnp.int32, (rows, rows), 1
        )
        total = jnp.zeros((features, rows), f32)
        for g in range(n // group):
            xs, es, hards = [], [], []
            for r in range(g * group, (g + 1) * group):
                i, k = x_places[r]
                xs.append(refs[i][:features] if k is None else refs[i][k, :features])
                i, k = e_places[r]
                scale = jnp.exp(refs[i][k, rows + 2 : rows + 3] - tot_ref[0, r : r + 1])
                scale = scale / tot_ref[1, r : r + 1]
                e = refs[i][k, :rows] * scale
                es.append(e if r else jnp.where(own, e - 1.0, e))
                hards.append(refs[i][k, rows : rows + 1] * scale)
                chosen = jnp.broadcast_to(refs[i][k, rows + 1 : rows + 2], (lanes, rows))
                first = (r - g * group) * rows
                local_ref[g, first : first + rows] = chosen.T.astype(jnp.int32)
            x = jnp.concatenate(xs, axis=1)
            chance = jnp.concatenate(es, axis=1)
            high, low = split2(x)
            c_high, c_low = split2(chance)
            both = dot(jnp.concatenate([high, low], axis=0), c_high, ((1,), (1,)))
            total = total + both[:features] + both[features:]
            total = total + dot(high, c_low, ((1,), (1,)))
            high, low = split2(x * (jnp.concatenate(hards, axis=1) / logit_divisor))
            scaled_ref[g, :features] = high
            scaled_ref[g, features:] = low
        dd_ref[...] = total.T / logit_divisor

    width = pool_ref.shape[1]
    first = pl.program_id(0) * width
    acc = jnp.zeros((2 * features, width), f32)
    for g in range(n // group):
        local = local_ref[g]
        column = first + lax.broadcasted_iota(jnp.int32, local.shape, 1)
        marks = jnp.concatenate(
            [
                jnp.where(local == column + t * lanes, 1.0, 0.0).astype(bf16)
                for t in range(width // lanes)
            ],
            axis=1,
        )
        acc = acc + dot(scaled_ref[g], marks)
    pool_ref[...] = acc[:features] + acc[features:]


def per_device(question_matrix, document_matrix, pool, hard_owner, hard_local):
    n, depth = lax.axis_size("blk"), lax.axis_size("dim")
    rows, features = question_matrix.shape
    columns = pool.shape[1]
    me = lax.axis_index("blk")
    smem = pl.BlockSpec(memory_space=pltpu.SMEM)
    vmem = pl.BlockSpec(memory_space=pltpu.VMEM)
    block = shape(features + SLACK, rows)
    line = Line()

    def full(*dims):
        return pl.BlockSpec(dims, lambda i: (0,) * len(dims))

    def send(x, mask):
        return lax.ppermute(x, "blk", [(i, i ^ mask) for i in range(n)])

    far = n // 4
    x, x_arrays, x_place = {}, [], {}

    def keep(array, *blocks):
        for k, r in enumerate(blocks):
            x[r] = array
            x_place[r] = (len(x_arrays), k if array.ndim == 3 else None)
        x_arrays.append(array)

    def pass_on(array):
        return line(lambda a, out: out.__setitem__(..., a[...]), block, "relay", [array], 0.05)

    def relay(r):
        x_arrays[x_place[r][0]] = x[r] = pass_on(x[r])

    def forward(k):
        relay(4 * k)
        if k % 2 == 0 and k + 1 < far:
            keep(send(x[4 * k], 4), 4 * k + 4)
        keep(send(x[4 * k], 2), 4 * k + 2)

    def share(*blocks):
        for r in blocks:
            keep(send(x[r], 1), r + 1)

    def share_all(*blocks):
        out = shape(len(blocks), features + SLACK, rows)
        held = line(relay_body, out, "relay", [x[r] for r in blocks], 0.05)
        keep(send(held, 1), *[r + 1 for r in blocks])

    weights, sums, e_place = [], {}, {}
    waiting, stage = [], {}

    held = []

    def score(blocks, hold=False):
        early = held.pop() if held else ([], ())
        k = len(blocks) + len(early[0])
        used = sorted({x_place[r][0] for r in blocks})
        part, found = line(
            functools.partial(
                score_body,
                [(used.index(x_place[r][0]), x_place[r][1]) for r in blocks],
                len(early[0]),
            ),
            (shape(k, rows + SLACK, rows), shape(k, features, rows)),
            "score",
            [me.reshape(1), document_matrix, pool] + [x_arrays[i] for i in used] + [*early[1]],
            0.9 * len(blocks),
            [smem] + [vmem] * (2 + len(used) + len(early[1])),
        )
        blocks = [r for r in blocks + early[0] if r % 2 == 0] + [
            r for r in blocks + early[0] if r % 2
        ]
        if hold:
            held.append((blocks, (part, found)))
            return
        got = [
            lax.ppermute(part, "dim", [(i, (i + s) % depth) for i in range(depth)])
            for s in range(1, depth)
        ]
        waiting.append((blocks, part, found, got))

    def softmax():
        blocks, part, found, got = waiting.pop(0)
        k = len(blocks)
        odds = [r for r in blocks if r % 2]
        evens = k - len(odds)
        stacked = False
        e, *out = line(
            functools.partial(softmax_body, evens if stacked else k, len(got)),
            [shape(k, rows + SLACK, rows)]
            + [block] * (evens if stacked else k)
            + [shape(len(odds), features + SLACK, rows)] * stacked,
            "softmax",
            [dt, found, part, *got],
            0.25 * k,
        )
        for i, r in enumerate(blocks):
            e_place[r] = (len(weights), i)
        weights.append(e)
        for r, array in zip(blocks, out[:evens]):
            sums[r] = (array, None)
        shared = send(out[-1], 1) if stacked else None
        for i, r in enumerate(odds):
            sums[r] = (shared, i) if stacked else (send(out[evens + i], 1), None)

    over_x, home = {}, []

    def add(*terms):
        arrays = [array for array, k in terms]
        places = [k for array, k in terms]
        return line(functools.partial(merge_body, places), block, "merge", arrays, 0.05)

    def pair(*blocks):
        for r in blocks:
            sums[r] = (add(sums[r], sums[r + 1]), None)

    def beside(k):
        over_x[k] = (send(sums[4 * k + 2][0], 2), None)

    def beside_all(*blocks):
        arrays, places = [], []
        for terms in blocks:
            places.append([(len(arrays) + i, sums[r][1]) for i, r in enumerate(terms)])
            arrays += [sums[r][0] for r in terms]
        out = shape(len(blocks), features + SLACK, rows)
        held = line(functools.partial(merge_all_body, places), out, "merge", arrays, 0.1)
        shared = send(held, 2)
        for i, terms in enumerate(blocks):
            over_x[terms[0] // 4] = (shared, i)

    def inward(k):
        whole = add(sums[4 * k], over_x[k])
        home.append(send(whole, 4 * k) if k else whole)

    packed = line(
        functools.partial(pack_body, columns),
        block,
        "pack",
        [question_matrix, hard_owner.T, hard_local.T],
        1.8,
        [pl.BlockSpec(memory_space=pltpu.HBM)] * 3,
        limit=62,
        scratch_shapes=[
            pltpu.VMEM(question_matrix.shape, f32),
            pltpu.VMEM(hard_owner.shape[::-1], jnp.int32),
            pltpu.VMEM(hard_local.shape[::-1], jnp.int32),
            pltpu.SemaphoreType.DMA((3,)),
        ],
    )
    keep(packed, 0)
    for k in [2, 1] + [k for k in range(4, far) if k % 2 == 0]:
        keep(send(packed, 4 * k), 4 * k)
    keep(send(packed, 2), 2)
    keep(send(packed, 1), 1)
    line.last = None
    dt = line(flip_body, shape(features, rows), "flip", [document_matrix], 0.1)
    score([0, 1], hold=True)
    forward(2)
    forward(1)
    relay(2)
    share_all(2, 4, 8)
    score([2, 4, 8])
    relay(10)
    forward(3)
    score([10, 3, 5, 9])
    relay(6)
    share(10, 6)
    score([6, 12, 11, 7])
    softmax()
    relay(14)
    share(12, 14)
    softmax()
    for k in range(3, far):
        if k + 1 < far:
            forward(k + 1)
        score([4 * k + 2 * i for i in range(k == 3, 2)] + [4 * k + 1, 4 * k + 3])
        if k + 1 < far:
            relay(4 * k + 6)
            share(4 * k + 4, 4 * k + 6)
        if k == 3:
            pair(0, 2, 4, 8)
            beside(0)
        softmax()
        if k == 3:
            beside_all((10, 11), (6, 7))
        else:
            pair(4 * k - 2, 4 * k - 4)
            beside(k - 1)
    softmax()

    totals = line(
        functools.partial(stats_body, [e_place[r] for r in range(n)]),
        shape(2, n, rows),
        "stats",
        weights,
        0.05,
        [
            pl.BlockSpec((e.shape[0], SLACK, rows), lambda i: (0, rows // SLACK, 0))
            for e in weights
        ],
        grid=(1,),
        out_specs=full(2, n, rows),
    )
    masks = [1] + [4 << i for i in reversed(range(far.bit_length() - 1))] + [2]
    for mask in masks:
        there = send(totals, mask)
        if mask == 2:
            pair(4 * far - 4)
            inward(2)
            inward(1)
        totals = line(
            functools.partial(stats_merge_body, [mask]),
            shape(2, n, rows),
            "stats_merge",
            [totals, there],
            0.05,
        )
        if mask == 1:
            over_x[0] = (pass_on(over_x[0][0]), None)
            pair(4 * far - 2)
            beside(far - 1)
    for k in range(3, far):
        inward(k)

    group = 4
    width = 512
    e_at = 1 + len(x_arrays)
    document_derivative, grad_pool = line(
        functools.partial(
            gradient_body,
            [(x_place[r][0] + 1, x_place[r][1]) for r in range(n)],
            [(e_at + e_place[r][0], e_place[r][1]) for r in range(n)],
            group,
        ),
        (shape(rows, features), shape(features, columns)),
        "gradient",
        [totals, *x_arrays, *weights],
        11.0,
        limit=48,
        grid=(columns // width,),
        out_specs=(full(rows, features), pl.BlockSpec((features, width), lambda i: (0, i))),
        scratch_shapes=[
            pltpu.VMEM((n // group, 2 * features, group * rows), bf16),
            pltpu.VMEM((n // group, group * rows, 128), jnp.int32),
        ],
    )

    line.last = totals
    inward(0)
    arrays = home
    question_derivative, loss = line(
        last_body,
        (shape(rows, features), shape(rows)),
        "finish",
        [document_matrix, weights[e_place[0][0]], *arrays],
        0.8,
        [full(rows, features)]
        + [pl.BlockSpec((1, SLACK, rows), lambda i: (e_place[0][1], rows // SLACK, 0))]
        + [full(*a.shape) for a in arrays],
        grid=(1,),
        out_specs=(full(rows, features), full(rows)),
    )
    return loss, question_derivative, document_derivative, grad_pool


def solution(mesh):
    placed = (P("blk", "dim"), P("blk", "dim"), P("dim", "blk"), P("blk", None), P("blk", None))
    return jax.shard_map(
        per_device,
        mesh=mesh,
        in_specs=placed,
        out_specs=(P("blk"), P("blk", "dim"), P("blk", "dim"), P("dim", "blk")),
        check_vma=False,
    )
```

```python
import functools

import jax
import jax.numpy as jnp
from jax import lax
from jax.experimental import pallas as pl
from jax.experimental.pallas import tpu as pltpu
from jax.sharding import PartitionSpec as P

logit_divisor = 0.05
LOWEST = -3.0e38
COST = 3.7e6
SLACK = 8

f32 = jnp.float32
bf16 = jnp.bfloat16


def split2(x):
    high = x.astype(bf16)
    return high, (x - high.astype(f32)).astype(bf16)


def dot(a, b, contract=((1,), (0,)), precision=None):
    return lax.dot_general(
        a, b, (contract, ((), ())), precision=precision, preferred_element_type=f32
    )


class Line:
    def __init__(self):
        self.last = None

    def __call__(self, body, out_shape, name, arrays, us, in_specs=None, limit=16, **kw):
        count = len(arrays)
        if in_specs is None:
            in_specs = [pl.BlockSpec(memory_space=pltpu.VMEM)] * count
        if self.last is not None:
            in_specs = list(in_specs) + [pl.BlockSpec(memory_space=pl.ANY)]
            arrays = list(arrays) + [self.last]

        def kernel(*refs):
            body(*refs[:count], *refs[len(arrays) :])

        out = pl.pallas_call(
            kernel,
            out_shape=out_shape,
            name=name,
            in_specs=in_specs,
            cost_estimate=pl.CostEstimate(
                flops=0, bytes_accessed=int(us * COST), transcendentals=0
            ),
            compiler_params=pltpu.CompilerParams(vmem_limit_bytes=limit << 20),
            **kw,
        )(*arrays)
        self.last = out[-1] if isinstance(out, (list, tuple)) else out
        return out


def shape(*dims, dtype=f32):
    return jax.ShapeDtypeStruct(dims, dtype)


def pack_body(columns, q_hbm, owner_hbm, local_hbm, x_ref, q_ref, owner_ref, local_ref, sems):
    pairs = ((q_hbm, q_ref), (owner_hbm, owner_ref), (local_hbm, local_ref))
    copies = [pltpu.make_async_copy(a, b, sems.at[i]) for i, (a, b) in enumerate(pairs)]
    for copy in copies:
        copy.start()
    for copy in copies:
        copy.wait()
    features = q_ref.shape[1]
    x_ref[:features, :] = q_ref[...].T
    x_ref[features:, :] = (owner_ref[...] * columns + local_ref[...]).astype(f32)


def relay_body(*refs):
    for k, ref in enumerate(refs[:-1]):
        refs[-1][k] = ref[...]


def flip_body(d_ref, dt_ref):
    dt_ref[...] = d_ref[...].T


def score_body(places, early, me_ref, d_ref, pool_ref, *refs):
    part_ref, rows_ref = refs[-2:]
    if early:
        early_part_ref, early_rows_ref = refs[-4:-2]
        part_ref[len(places) :] = early_part_ref[...]
        rows_ref[len(places) :] = early_rows_ref[...]
    rows, features = d_ref.shape
    columns = pool_ref.shape[1]
    tile = 128
    blocks = [refs[a][...] if k is None else refs[a][k] for a, k in places]
    for k, block in enumerate(blocks):
        x = block[:features]
        named = block[features:].astype(jnp.int32) - me_ref[0] * columns
        here = (named >= 0) & (named < columns)
        local = jnp.sum(jnp.where(here, named, 0), axis=0, keepdims=True)
        owned = jnp.any(here, axis=0, keepdims=True)
        lane = jnp.broadcast_to(local % tile, (features, rows))
        found = jnp.zeros((features, rows), f32)
        for t in range(columns // tile):
            picked = jnp.take_along_axis(
                pool_ref[:, t * tile : (t + 1) * tile], lane, axis=1, mode="promise_in_bounds"
            )
            found = jnp.where(local // tile == t, picked, found)
        rows_ref[k] = found
        hard = jnp.sum(x * found, axis=0, keepdims=True)
        chosen = jnp.where(owned, local, -1).astype(f32)
        part_ref[k, rows:] = jnp.concatenate(
            [hard, chosen, jnp.zeros((SLACK - 2, rows), f32)], axis=0
        )
    x = [block[:features] for block in blocks]
    x = x[0] if len(x) == 1 else jnp.concatenate(x, axis=1)
    scores = dot(d_ref[...], x, precision=lax.Precision.HIGHEST)
    for k in range(len(blocks)):
        part_ref[k, :rows] = scores[:, k * rows : (k + 1) * rows]


def softmax_body(evens, others, dt_ref, rows_ref, part_ref, *refs):
    got, (e_ref, *sum_refs) = refs[:others], refs[others:]
    features, rows = dt_ref.shape
    count = part_ref.shape[0]
    own = lax.broadcasted_iota(jnp.int32, (rows, rows), 0) == lax.broadcasted_iota(
        jnp.int32, (rows, rows), 1
    )
    tails, es = [], []
    for k in range(count):
        whole = part_ref[k]
        chosen = whole[rows + 1 : rows + 2]
        for r in got:
            whole = whole + r[k]
        scores = whole[:rows] / logit_divisor
        hard = jnp.where(chosen >= 0, whole[rows : rows + 1] / logit_divisor, LOWEST)
        peak = jnp.maximum(jnp.max(scores, axis=0, keepdims=True), hard)
        e = jnp.exp(scores - peak)
        hard_e = jnp.where(chosen >= 0, jnp.exp(hard - peak), 0.0)
        total = jnp.sum(e, axis=0, keepdims=True) + hard_e
        positive = jnp.sum(jnp.where(own, scores, 0.0), axis=0, keepdims=True)
        e_ref[k, :rows] = e
        e_ref[k, rows:] = jnp.concatenate(
            [hard_e, chosen, peak, total, positive, jnp.zeros((SLACK - 5, rows), f32)], axis=0
        )
        es.append(e)
        tails.append((hard_e, peak, total))
    e = es[0] if count == 1 else jnp.concatenate(es, axis=1)
    sums = dot(dt_ref[...], e, precision=lax.Precision.HIGHEST)
    for k, (hard_e, peak, total) in enumerate(tails):
        at = sum_refs[k] if k < evens else sum_refs[-1].at[k - evens]
        at[:features] = sums[:, k * rows : (k + 1) * rows] + rows_ref[k] * hard_e
        at[features:] = jnp.concatenate([peak, total, jnp.zeros((SLACK - 2, rows), f32)], axis=0)


def merge(terms):
    size = terms[0].shape[0] - SLACK
    peaks = [t[size : size + 1] for t in terms]
    peak = functools.reduce(jnp.maximum, peaks)
    scales = [jnp.exp(p - peak) for p in peaks]
    sums = functools.reduce(jnp.add, [t[:size] * s for t, s in zip(terms, scales)])
    total = functools.reduce(
        jnp.add, [t[size + 1 : size + 2] * s for t, s in zip(terms, scales)]
    )
    return sums, peak, total


def merge_body(places, *refs):
    out_ref = refs[-1]
    sums, peak, total = merge([r[...] if k is None else r[k] for r, k in zip(refs, places)])
    size = sums.shape[0]
    out_ref[:size] = sums
    out_ref[size:] = jnp.concatenate(
        [peak, total, jnp.zeros((SLACK - 2, peak.shape[1]), f32)], axis=0
    )


def merge_all_body(places, *refs):
    out_ref = refs[-1]
    size = out_ref.shape[1] - SLACK
    for slot, terms in enumerate(places):
        terms = [refs[i][...] if k is None else refs[i][k] for i, k in terms]
        if len(terms) == 1:
            out_ref[slot] = terms[0]
        else:
            sums, peak, total = merge(terms)
            out_ref[slot, :size] = sums
            out_ref[slot, size:] = jnp.concatenate(
                [peak, total, jnp.zeros((SLACK - 2, peak.shape[1]), f32)], axis=0
            )


def last_body(d_ref, e_ref, *refs):
    dq_ref, loss_ref = refs[-2:]
    sums, peak, total = merge([ref[...] for ref in refs[:-2]])
    dq_ref[...] = ((sums / total).T - d_ref[...]) / logit_divisor
    log_total = peak + jnp.log(total)
    loss_ref[...] = (log_total - e_ref[0, 4:5]).reshape(loss_ref.shape)


def stats_body(places, *refs):
    out_ref = refs[-1]
    for r, (i, k) in enumerate(places):
        out_ref[0, r : r + 1] = refs[i][k, 2:3]
        out_ref[1, r : r + 1] = refs[i][k, 3:4]


def stats_merge_body(masks, own_ref, *refs):
    out_ref = refs[-1]
    n = own_ref.shape[1]
    peaks, totals = [own_ref[0]], [own_ref[1]]
    for ref, mask in zip(refs, masks):
        for values, into in ((ref[0], peaks), (ref[1], totals)):
            into.append(
                jnp.concatenate([values[r ^ mask : (r ^ mask) + 1] for r in range(n)], axis=0)
            )
    peak = functools.reduce(jnp.maximum, peaks)
    out_ref[0] = peak
    out_ref[1] = functools.reduce(
        jnp.add, [t * jnp.exp(p - peak) for p, t in zip(peaks, totals)]
    )


def gradient_body(x_places, e_places, group, *refs):
    n = len(x_places)
    tot_ref = refs[0]
    dd_ref, pool_ref, scaled_ref, local_ref = refs[-4:]
    rows, features = dd_ref.shape
    lanes = local_ref.shape[-1]

    @pl.when(pl.program_id(0) == 0)
    def _():
        own = lax.broadcasted_iota(jnp.int32, (rows, rows), 0) == lax.broadcasted_iota(
            jnp.int32, (rows, rows), 1
        )
        total = jnp.zeros((features, rows), f32)
        for g in range(n // group):
            xs, es, hards = [], [], []
            for r in range(g * group, (g + 1) * group):
                i, k = x_places[r]
                xs.append(refs[i][:features] if k is None else refs[i][k, :features])
                i, k = e_places[r]
                scale = jnp.exp(refs[i][k, rows + 2 : rows + 3] - tot_ref[0, r : r + 1])
                scale = scale / tot_ref[1, r : r + 1]
                e = refs[i][k, :rows] * scale
                es.append(e if r else jnp.where(own, e - 1.0, e))
                hards.append(refs[i][k, rows : rows + 1] * scale)
                chosen = jnp.broadcast_to(refs[i][k, rows + 1 : rows + 2], (lanes, rows))
                first = (r - g * group) * rows
                local_ref[g, first : first + rows] = chosen.T.astype(jnp.int32)
            x = jnp.concatenate(xs, axis=1)
            chance = jnp.concatenate(es, axis=1)
            high, low = split2(x)
            c_high, c_low = split2(chance)
            both = dot(jnp.concatenate([high, low], axis=0), c_high, ((1,), (1,)))
            total = total + both[:features] + both[features:]
            total = total + dot(high, c_low, ((1,), (1,)))
            high, low = split2(x * (jnp.concatenate(hards, axis=1) / logit_divisor))
            scaled_ref[g, :features] = high
            scaled_ref[g, features:] = low
        dd_ref[...] = total.T / logit_divisor

    width = pool_ref.shape[1]
    first = pl.program_id(0) * width
    acc = jnp.zeros((2 * features, width), f32)
    for g in range(n // group):
        local = local_ref[g]
        column = first + lax.broadcasted_iota(jnp.int32, local.shape, 1)
        marks = jnp.concatenate(
            [
                jnp.where(local == column + t * lanes, 1.0, 0.0).astype(bf16)
                for t in range(width // lanes)
            ],
            axis=1,
        )
        acc = acc + dot(scaled_ref[g], marks)
    pool_ref[...] = acc[:features] + acc[features:]


def per_device(question_matrix, document_matrix, pool, hard_owner, hard_local):
    n, depth = lax.axis_size("blk"), lax.axis_size("dim")
    rows, features = question_matrix.shape
    columns = pool.shape[1]
    me = lax.axis_index("blk")
    smem = pl.BlockSpec(memory_space=pltpu.SMEM)
    vmem = pl.BlockSpec(memory_space=pltpu.VMEM)
    block = shape(features + SLACK, rows)
    line = Line()

    def full(*dims):
        return pl.BlockSpec(dims, lambda i: (0,) * len(dims))

    def send(x, mask):
        return lax.ppermute(x, "blk", [(i, i ^ mask) for i in range(n)])

    far = n // 4
    x, x_arrays, x_place = {}, [], {}

    def keep(array, *blocks):
        for k, r in enumerate(blocks):
            x[r] = array
            x_place[r] = (len(x_arrays), k if array.ndim == 3 else None)
        x_arrays.append(array)

    def pass_on(array):
        return line(lambda a, out: out.__setitem__(..., a[...]), block, "relay", [array], 0.05)

    def relay(r):
        x_arrays[x_place[r][0]] = x[r] = pass_on(x[r])

    def forward(k):
        relay(4 * k)
        if k % 2 == 0 and k + 1 < far:
            keep(send(x[4 * k], 4), 4 * k + 4)
        keep(send(x[4 * k], 2), 4 * k + 2)

    def share(*blocks):
        for r in blocks:
            keep(send(x[r], 1), r + 1)

    def share_all(*blocks):
        out = shape(len(blocks), features + SLACK, rows)
        held = line(relay_body, out, "relay", [x[r] for r in blocks], 0.05)
        keep(send(held, 1), *[r + 1 for r in blocks])

    weights, sums, e_place = [], {}, {}
    waiting, stage = [], {}

    held = []

    def score(blocks, hold=False):
        early = held.pop() if held else ([], ())
        k = len(blocks) + len(early[0])
        used = sorted({x_place[r][0] for r in blocks})
        part, found = line(
            functools.partial(
                score_body,
                [(used.index(x_place[r][0]), x_place[r][1]) for r in blocks],
                len(early[0]),
            ),
            (shape(k, rows + SLACK, rows), shape(k, features, rows)),
            "score",
            [me.reshape(1), document_matrix, pool] + [x_arrays[i] for i in used] + [*early[1]],
            0.9 * len(blocks),
            [smem] + [vmem] * (2 + len(used) + len(early[1])),
        )
        blocks = [r for r in blocks + early[0] if r % 2 == 0] + [
            r for r in blocks + early[0] if r % 2
        ]
        if hold:
            held.append((blocks, (part, found)))
            return
        got = [
            lax.ppermute(part, "dim", [(i, (i + s) % depth) for i in range(depth)])
            for s in range(1, depth)
        ]
        waiting.append((blocks, part, found, got))

    def softmax():
        blocks, part, found, got = waiting.pop(0)
        k = len(blocks)
        odds = [r for r in blocks if r % 2]
        evens = k - len(odds)
        stacked = False
        e, *out = line(
            functools.partial(softmax_body, evens if stacked else k, len(got)),
            [shape(k, rows + SLACK, rows)]
            + [block] * (evens if stacked else k)
            + [shape(len(odds), features + SLACK, rows)] * stacked,
            "softmax",
            [dt, found, part, *got],
            0.25 * k,
        )
        for i, r in enumerate(blocks):
            e_place[r] = (len(weights), i)
        weights.append(e)
        for r, array in zip(blocks, out[:evens]):
            sums[r] = (array, None)
        shared = send(out[-1], 1) if stacked else None
        for i, r in enumerate(odds):
            sums[r] = (shared, i) if stacked else (send(out[evens + i], 1), None)

    over_x, home = {}, []

    def add(*terms):
        arrays = [array for array, k in terms]
        places = [k for array, k in terms]
        return line(functools.partial(merge_body, places), block, "merge", arrays, 0.05)

    def pair(*blocks):
        for r in blocks:
            sums[r] = (add(sums[r], sums[r + 1]), None)

    def beside(k):
        over_x[k] = (send(sums[4 * k + 2][0], 2), None)

    def beside_all(*blocks):
        arrays, places = [], []
        for terms in blocks:
            places.append([(len(arrays) + i, sums[r][1]) for i, r in enumerate(terms)])
            arrays += [sums[r][0] for r in terms]
        out = shape(len(blocks), features + SLACK, rows)
        held = line(functools.partial(merge_all_body, places), out, "merge", arrays, 0.1)
        shared = send(held, 2)
        for i, terms in enumerate(blocks):
            over_x[terms[0] // 4] = (shared, i)

    def inward(k):
        whole = add(sums[4 * k], over_x[k])
        home.append(send(whole, 4 * k) if k else whole)

    packed = line(
        functools.partial(pack_body, columns),
        block,
        "pack",
        [question_matrix, hard_owner.T, hard_local.T],
        1.8,
        [pl.BlockSpec(memory_space=pltpu.HBM)] * 3,
        limit=62,
        scratch_shapes=[
            pltpu.VMEM(question_matrix.shape, f32),
            pltpu.VMEM(hard_owner.shape[::-1], jnp.int32),
            pltpu.VMEM(hard_local.shape[::-1], jnp.int32),
            pltpu.SemaphoreType.DMA((3,)),
        ],
    )
    keep(packed, 0)
    for k in [2, 1] + [k for k in range(4, far) if k % 2 == 0]:
        keep(send(packed, 4 * k), 4 * k)
    keep(send(packed, 2), 2)
    keep(send(packed, 1), 1)
    line.last = None
    dt = line(flip_body, shape(features, rows), "flip", [document_matrix], 0.1)
    score([0, 1], hold=True)
    forward(2)
    forward(1)
    relay(2)
    share_all(2, 4, 8)
    score([2, 4, 8])
    relay(10)
    forward(3)
    score([10, 3, 5, 9])
    relay(6)
    share(10, 6)
    score([6, 12, 11, 7])
    softmax()
    relay(14)
    share(12, 14)
    softmax()
    for k in range(3, far):
        if k + 1 < far:
            forward(k + 1)
        score([4 * k + 2 * i for i in range(k == 3, 2)] + [4 * k + 1, 4 * k + 3])
        if k + 1 < far:
            relay(4 * k + 6)
            share(4 * k + 4, 4 * k + 6)
        if k == 3:
            pair(0, 2, 4, 8)
            beside(0)
        softmax()
        if k == 3:
            over_x[0] = (pass_on(over_x[0][0]), None)
            beside_all((10, 11), (6, 7))
        else:
            pair(4 * k - 2, 4 * k - 4)
            beside(k - 1)
    softmax()

    totals = line(
        functools.partial(stats_body, [e_place[r] for r in range(n)]),
        shape(2, n, rows),
        "stats",
        weights,
        0.05,
        [
            pl.BlockSpec((e.shape[0], SLACK, rows), lambda i: (0, rows // SLACK, 0))
            for e in weights
        ],
        grid=(1,),
        out_specs=full(2, n, rows),
    )
    masks = [1] + [4 << i for i in reversed(range(far.bit_length() - 1))] + [2]
    for mask in masks:
        there = send(totals, mask)
        if mask == 2:
            pair(4 * far - 4)
            inward(2)
            inward(1)
        totals = line(
            functools.partial(stats_merge_body, [mask]),
            shape(2, n, rows),
            "stats_merge",
            [totals, there],
            0.05,
        )
        if mask == 1:
            pair(4 * far - 2)
            beside(far - 1)
    for k in range(3, far):
        inward(k)

    group = 4
    width = 512
    e_at = 1 + len(x_arrays)
    document_derivative, grad_pool = line(
        functools.partial(
            gradient_body,
            [(x_place[r][0] + 1, x_place[r][1]) for r in range(n)],
            [(e_at + e_place[r][0], e_place[r][1]) for r in range(n)],
            group,
        ),
        (shape(rows, features), shape(features, columns)),
        "gradient",
        [totals, *x_arrays, *weights],
        11.0,
        limit=48,
        grid=(columns // width,),
        out_specs=(full(rows, features), pl.BlockSpec((features, width), lambda i: (0, i))),
        scratch_shapes=[
            pltpu.VMEM((n // group, 2 * features, group * rows), bf16),
            pltpu.VMEM((n // group, group * rows, 128), jnp.int32),
        ],
    )

    line.last = totals
    inward(0)
    arrays = home
    question_derivative, loss = line(
        last_body,
        (shape(rows, features), shape(rows)),
        "finish",
        [document_matrix, weights[e_place[0][0]], *arrays],
        0.8,
        [full(rows, features)]
        + [pl.BlockSpec((1, SLACK, rows), lambda i: (e_place[0][1], rows // SLACK, 0))]
        + [full(*a.shape) for a in arrays],
        grid=(1,),
        out_specs=(full(rows, features), full(rows)),
    )
    return loss, question_derivative, document_derivative, grad_pool


def solution(mesh):
    placed = (P("blk", "dim"), P("blk", "dim"), P("dim", "blk"), P("blk", None), P("blk", None))
    return jax.shard_map(
        per_device,
        mesh=mesh,
        in_specs=placed,
        out_specs=(P("blk"), P("blk", "dim"), P("blk", "dim"), P("dim", "blk")),
        check_vma=False,
    )
```
